32 devices in a mesh: dp: 4 (over x, core), mp: 8 (over z, y).
Axes of the slice: x: 2, y: 2, z: 4, core: 2. Of those that a mesh axis runs over, the one named last changes fastest.
Arguments:
- tokens: bfloat16 [4704, 768], P(('dp', 'mp')), may hold values from -6 to 6
- crop_kind: int32 [96], P('dp'), may hold values from 0 to 1, as said below
- norm1_gain: float32 [768], replicated, may hold values from 0.1 to 1.9
- norm1_bias: float32 [768], replicated, may hold values from -1.75 to 1.75
- qkv_weight: bfloat16 [3, 768, 768], P(None, None, 'mp'), may hold values from -0.21875 to 0.21875
- qv_bias: float32 [2, 768], P(None, 'mp'), may hold values from -3 to 3
- rel_table: float32 [169, 24], P(None, 'mp'), may hold values from -6 to 6
- proj_weight: bfloat16 [768, 768], P('mp'), may hold values from -0.875 to 0.875
- proj_bias: float32 [768], replicated, may hold values from -1.75 to 1.75
- norm2_gain: float32 [768], replicated, may hold values from 0.1 to 1.9
- norm2_bias: float32 [768], replicated, may hold values from -1.75 to 1.75
- fc1_weight: bfloat16 [768, 3072], P(None, 'mp'), may hold values from -0.21875 to 0.21875
- fc1_bias: float32 [3072], P('mp'), may hold values from -3 to 3
- fc2_weight: bfloat16 [3072, 768], P('mp'), may hold values from -0.109375 to 0.109375
- fc2_bias: float32 [768], replicated, may hold values from -1.75 to 1.75
- out_grad: bfloat16 [4704, 768], P(('dp', 'mp')), may hold values from -6 to 6
Outputs:
- block_out: bfloat16 [4704, 768], P(('dp', 'mp'))
- tokens_grad: bfloat16 [4704, 768], P(('dp', 'mp'))
- norm1_gain_grad: float32 [768], replicated
- norm1_bias_grad: float32 [768], replicated
- qkv_weight_grad: float32 [3, 768, 768], P(None, None, 'mp')
- qv_bias_grad: float32 [2, 768], P(None, 'mp')
- rel_table_grad: float32 [169, 24], P(None, 'mp')
- proj_weight_grad: float32 [768, 768], P('mp')
- proj_bias_grad: float32 [768], replicated
- norm2_gain_grad: float32 [768], replicated
- norm2_bias_grad: float32 [768], replicated
- fc1_weight_grad: float32 [768, 3072], P(None, 'mp')
- fc1_bias_grad: float32 [3072], P('mp')
- fc2_weight_grad: float32 [3072, 768], P('mp')
- fc2_bias_grad: float32 [768], replicated
The draws below stay inside these ranges and needn't reach their ends.
Inputs may be any that keep to these rules, and one draw needn't show every extreme that they name: `crop_kind`: 0 marks a global crop, whose 49 slots all hold patches; 1 marks a local crop, whose first 9 slots hold patches. Both kinds occur.
All inputs are finite; a program needn't handle non-finite values.
Results may differ from the reference program's by a relative error of at most 0.024.
Values may be sent and summed in bfloat16 or wider, within the bound.
A program may use at most 64 MiB of HBM per device.

```python
import jax
import jax.numpy as jnp
from jax import lax

D = 768
HEADS = 24
HEAD = 32
FF = 3072
SIDE = 7
LOCAL_SIDE = 3
WIN = 49
TABLE = 169
WIN_GROUP = 24
WINDOWS = 96
TOKENS = 4704
N_DP = 4


def draw_crop_kind(key, part):
    group_ids = jnp.arange(WINDOWS) // WIN_GROUP
    share_key = jax.random.fold_in(key, 11)
    roll_key = jax.random.fold_in(key, 23)
    shares = jax.random.randint(share_key, (WINDOWS // WIN_GROUP,), 2, 10)
    rolls = jax.random.randint(roll_key, (WINDOWS,), 0, 10)
    kinds = jnp.where(rolls < shares[group_ids], 0, 1).astype(jnp.int32)
    return kinds.at[0].set(0).at[1].set(1)


def block_levels(stream_key, extent, cuts, low, largest):
    loudness, own = 1.0, jax.random.fold_in(stream_key, 6)
    for axis_at, blocks in cuts:
        draws = jnp.exp(jax.random.uniform(jax.random.fold_in(own, axis_at), (blocks,), jnp.float32, low / len(cuts), largest / len(cuts)))
        loudness = loudness * jnp.repeat(draws, extent[axis_at] // blocks).reshape([-1 if axis == axis_at else 1 for axis in range(len(extent))])
    return loudness


def gaussian(rng, dims, scale, limit, shards=(), dtype=jnp.bfloat16):
    values = jax.random.normal(rng, dims, jnp.float32) * scale
    if len(shards) > 0:
        values = block_levels(rng, dims, shards, -0.22, 0.18) * values
    return jnp.clip(values, min=-limit, max=limit).astype(dtype)


def setup_inputs(seed: int = 0) -> dict:
    key_of = jax.random.split(jax.random.key(seed), 17)
    tokens = gaussian(key_of[0], (TOKENS, D), 1.0, 6.0, ((0, 32),))
    crop_kind = draw_crop_kind(jax.random.fold_in(key_of[16], 71), 0)
    norm1_gain = jnp.clip(1.0 + 0.18 * jax.random.normal(key_of[2], (D,), jnp.float32), 0.1, 1.9)
    norm1_bias = gaussian(key_of[3], (D,), 0.3, 1.75, (), jnp.float32)
    qkv_weight = gaussian(key_of[4], (3, D, D), D ** -0.5, 0.21875, ((2, 8),))
    qv_bias = gaussian(key_of[5], (2, D), 0.5, 3.0, ((1, 8),), jnp.float32)
    rel_table = gaussian(key_of[6], (TABLE, HEADS), 1.0, 6.0, ((1, 8),), jnp.float32)
    proj_weight = gaussian(key_of[7], (D, D), (D // 16) ** -0.5, 0.875, ((0, 8),))
    proj_bias = gaussian(key_of[8], (D,), 0.3, 1.75, (), jnp.float32)
    norm2_gain = jnp.clip(1.0 + 0.18 * jax.random.normal(key_of[9], (D,), jnp.float32), 0.1, 1.9)
    norm2_bias = gaussian(key_of[10], (D,), 0.3, 1.75, (), jnp.float32)
    fc1_weight = gaussian(key_of[11], (D, FF), D ** -0.5, 0.21875, ((1, 8),))
    fc1_bias = gaussian(key_of[12], (FF,), 0.5, 3.0, ((0, 8),), jnp.float32)
    fc2_weight = gaussian(key_of[13], (FF, D), FF ** -0.5, 0.109375, ((0, 8),))
    fc2_bias = gaussian(key_of[14], (D,), 0.3, 1.75, (), jnp.float32)
    out_grad = gaussian(key_of[15], (TOKENS, D), 1.0, 6.0, ((0, 32),))
    return dict(tokens=tokens, crop_kind=crop_kind, norm1_gain=norm1_gain, norm1_bias=norm1_bias, qkv_weight=qkv_weight, qv_bias=qv_bias, rel_table=rel_table, proj_weight=proj_weight, proj_bias=proj_bias, norm2_gain=norm2_gain, norm2_bias=norm2_bias, fc1_weight=fc1_weight, fc1_bias=fc1_bias, fc2_weight=fc2_weight, fc2_bias=fc2_bias, out_grad=out_grad)


EPSILON = 1e-05
NEG_FILL = -1000000000.0
HIGHEST = lax.Precision.HIGHEST

@jax.custom_vjp
def low(v):
    return lax.optimization_barrier(v.astype(jnp.bfloat16)).astype(jnp.float32)

@jax.custom_vjp
def low_back(v):
    return v

def low_keep(v):
    return (low(v), None)

def low_pass(kept, grad):
    return (grad,)

def back_keep(v):
    return (v, None)

def back_low(kept, grad):
    return (low(grad),)
low.defvjp(low_keep, low_pass)
low_back.defvjp(back_keep, back_low)

def normalize(values, gain_vec, shift_vec):
    centre = values - lax.optimization_barrier(jnp.mean(values, axis=-1, keepdims=True))
    spread = lax.optimization_barrier(jnp.mean(centre * centre, axis=-1, keepdims=True))
    return centre * lax.rsqrt(spread + EPSILON) * gain_vec + shift_vec

def gelu_tanh(values):
    return jax.nn.gelu(values, approximate=True)

def relative_index(side_len):
    slot_ids = jnp.minimum(jnp.arange(WIN), side_len * side_len - 1).astype(jnp.int32)
    slot_row = slot_ids // side_len
    slot_col = slot_ids % side_len
    offset_row = slot_row[:, None] - slot_row[None, :] + SIDE - 1
    offset_col = slot_col[:, None] - slot_col[None, :] + SIDE - 1
    return (offset_row * (2 * SIDE - 1) + offset_col).astype(jnp.int32)

def window_live(kinds):
    return jnp.where(kinds == 0, WIN, LOCAL_SIDE * LOCAL_SIDE)

def hdot(left, right):
    return jnp.dot(left, right, precision=HIGHEST)

def forward(inputs, kinds, weights):
    gain_one, shift_one, qkv_weight, qv_bias, rel_table, proj_weight, proj_bias, gain_two, shift_two, fc1_weight, fc1_bias, fc2_weight, fc2_bias = weights
    windows = kinds.shape[0]
    live_count = window_live(kinds)
    key_usable = jnp.arange(WIN)[None, :] < live_count[:, None]
    row_live = key_usable.astype(jnp.float32).reshape(windows * WIN, 1)
    rows_one = low(normalize(inputs, gain_one, shift_one))
    query_pre = low_back(hdot(rows_one, qkv_weight[0]) + qv_bias[0])
    query_rows = low(query_pre * HEAD ** (-0.5))
    key_rows = low(low_back(hdot(rows_one, qkv_weight[1])))
    value_rows = low(low_back(hdot(rows_one, qkv_weight[2]) + qv_bias[1]))
    win_shape = (windows, WIN, HEADS, HEAD)
    score_raw = low_back(jnp.einsum('wqhd,wkhd->whqk', query_rows.reshape(win_shape), key_rows.reshape(win_shape), precision=HIGHEST))
    index_both = jnp.stack([relative_index(SIDE), relative_index(LOCAL_SIDE)])
    bias_both = jnp.transpose(rel_table[index_both], (0, 3, 1, 2))
    is_global = (kinds == 0)[:, None, None, None]
    bias_win = jnp.where(is_global, bias_both[0][None], bias_both[1][None])
    scores = jnp.where(key_usable[:, None, None, :], score_raw + bias_win, NEG_FILL)
    prob_full = jax.nn.softmax(scores, axis=-1)
    head_out = jnp.einsum('whqk,wkhd->wqhd', low(prob_full), value_rows.reshape(win_shape), precision=HIGHEST).reshape(windows * WIN, HEADS * HEAD)
    head_out = low(low_back(head_out))
    attn_branch = low_back(hdot(head_out, proj_weight))
    middle = inputs + (attn_branch + proj_bias) * row_live
    rows_two = low(normalize(middle, gain_two, shift_two))
    hidden_pre = low_back(hdot(rows_two, fc1_weight) + fc1_bias)
    hidden_act = low(gelu_tanh(hidden_pre))
    mlp_branch = low_back(hdot(hidden_act, fc2_weight))
    return middle + (mlp_branch + fc2_bias) * row_live

def reference(tokens, crop_kind, norm1_gain, norm1_bias, qkv_weight, qv_bias, rel_table, proj_weight, proj_bias, norm2_gain, norm2_bias, fc1_weight, fc1_bias, fc2_weight, fc2_bias, out_grad):
    group_rows = WIN_GROUP * WIN
    weights = (norm1_gain, norm1_bias, qkv_weight.astype(jnp.float32), qv_bias, rel_table, proj_weight.astype(jnp.float32), proj_bias, norm2_gain, norm2_bias, fc1_weight.astype(jnp.float32), fc1_bias, fc2_weight.astype(jnp.float32), fc2_bias)
    token_groups = tokens.astype(jnp.float32).reshape(N_DP, group_rows, D)
    kind_groups = crop_kind.reshape(N_DP, WIN_GROUP)
    grad_groups = out_grad.astype(jnp.float32).reshape(N_DP, group_rows, D)

    def step(totals, item):
        inputs, kinds, upstream = item

        def apply(values, params):
            return forward(values, kinds, params)
        result, pull = jax.vjp(apply, inputs, weights)
        input_grad, weight_grads = pull(upstream)
        totals = jax.tree.map(lambda left, right: left + right, totals, weight_grads)
        return (totals, (result, input_grad))
    start_sums = jax.tree.map(jnp.zeros_like, weights)
    totals, outputs = lax.scan(step, start_sums, (token_groups, kind_groups, grad_groups))
    results, input_grads = outputs
    return (results.reshape(TOKENS, D).astype(jnp.bfloat16), input_grads.reshape(TOKENS, D).astype(jnp.bfloat16), totals[0], totals[1], totals[2], totals[3], totals[4], totals[5], totals[6], totals[7], totals[8], totals[9], totals[10], totals[11], totals[12])
```

```python
import functools

import jax
import jax.numpy as jnp
from jax import lax
from jax.experimental import pallas as pl
from jax.experimental.pallas import tpu as pltpu
from jax.sharding import PartitionSpec as P

HEAD = 32
SIDE = 7
LOCAL_SIDE = 3
WIN = 49
SPAN = 2 * SIDE - 1
ENTRIES = SPAN * SPAN
CENTRE = (SIDE - 1) * SPAN + SIDE - 1
SLOTS = 64
TILE = 128
PACK = 4
GROUP = 4
LANES = 256
EPSILON = 1e-05
NEG_FILL = -1000000000.0
GELU_A = 0.7978845608028654
GELU_B = 0.044715
HIGHEST = lax.Precision.HIGHEST
MESH = pl.DeviceIdType.MESH
BF = jnp.bfloat16
F32 = jnp.float32


def dot(left, right, dims, precision=None):
    return lax.dot_general(
        left, right, (dims, ((), ())), preferred_element_type=F32, precision=precision
    )


def dot_nn(left, right, precision=None):
    return dot(left, right, ((1,), (0,)), precision)


def dot_nt(left, right, precision=None):
    return dot(left, right, ((1,), (1,)), precision)


def dot_tn(left, right, precision=None):
    return dot(left, right, ((0,), (0,)), precision)


def iota(shape, axis):
    return lax.broadcasted_iota(jnp.int32, shape, axis)


def one_hot(cond, dtype):
    return jnp.where(cond, 1.0, 0.0).astype(dtype)


def steps_of(values, width, count):
    total = jnp.zeros_like(values)
    for step in range(1, count):
        total = total + jnp.where(values >= step * width, 1, 0)
    return total


def shear(values, shift):
    moved = pltpu.roll(values, shift, axis=1)
    return pltpu.roll(moved, 0, axis=1, stride=1, stride_axis=0)


def split_two(values):
    high = values.astype(BF)
    return high, (values - high.astype(F32)).astype(BF)


def norm_parts(values):
    mean = jnp.mean(values, axis=-1, keepdims=True)
    centre = values - mean
    spread = jnp.mean(centre * centre, axis=-1, keepdims=True)
    scale = lax.rsqrt(spread + EPSILON)
    return centre * scale, scale


def norm_back(grad_normed, normed, scale):
    return scale * (
        grad_normed
        - jnp.mean(grad_normed, axis=-1, keepdims=True)
        - normed * jnp.mean(grad_normed * normed, axis=-1, keepdims=True)
    )


def slot_place(columns, windows, kinds):
    window = steps_of(columns, WIN, windows)
    slot = columns - WIN * window
    kind = jnp.zeros_like(columns)
    for w in range(windows):
        kind = jnp.where(window == w, kinds[w], kind)
    whole = slot + steps_of(slot, SIDE, SIDE)
    corner = slot + (8 - LOCAL_SIDE) * steps_of(slot, LOCAL_SIDE, LOCAL_SIDE)
    rest = slot + (8 * LOCAL_SIDE - LOCAL_SIDE * LOCAL_SIDE)
    local = jnp.where(slot < LOCAL_SIDE * LOCAL_SIDE, corner, rest)
    place = SLOTS * window + jnp.where(kind == 0, whole, local)
    live = jnp.where(kind == 0, WIN, LOCAL_SIDE * LOCAL_SIDE)
    inside = columns < WIN * windows
    return jnp.where(inside, place, -1), inside & (slot < live)


def body(
    dims,
    kind_ref,
    tok_ref,
    og_ref,
    n1g_ref,
    n1b_ref,
    qkvw_ref,
    qvb_ref,
    tab_ref,
    pw_ref,
    pb_ref,
    n2g_ref,
    n2b_ref,
    f1w_ref,
    f1b_ref,
    f2w_ref,
    f2b_ref,
    out_ref,
    tgrad_ref,
    vec_ref,
    qkvg_ref,
    qvg_ref,
    relg_ref,
    projg_ref,
    f1g_ref,
    f1bg_ref,
    f2g_ref,
    wa,
    wf,
    ft,
    sp,
    pk,
    xs,
    x1s,
    n1s,
    gs,
    stats,
    qb,
    fb,
    h1p,
    qs,
    ks,
    vs,
    at,
    pt,
    bias_whole,
    bias_local,
    hg,
    gg,
    ac,
    dp_s,
    ph,
    rc_h,
    rx_h,
    ph2,
    rc_o,
    rx_o,
    gabp,
    dqs,
    dks,
    dvs,
    dbias,
    dh1,
    ga,
    gf,
    rca,
    rxa,
    ry,
    rz,
    fin,
    sg,
    sg_in,
    sg_group,
    sem_ws,
    sem_wr,
    sem_bs,
    sem_br,
    sem_rs,
    sem_rr,
    sem_hs,
    sem_hr,
    sem_as,
    sem_ar,
    sem_ys,
    sem_yr,
    sem_fs,
    sem_fr,
    sem_ss,
    sem_sr,
    sem_gs,
    sem_gr,
):
    n_dp, n_mp, rows, windows, padded, width, block, hidden = dims
    groups = n_dp // GROUP
    places = SLOTS * windows
    z_count = n_mp // 2
    heads_here = block // HEAD
    tiles = width // TILE
    mp = lax.axis_index("mp")
    dp = lax.axis_index("dp")
    z = mp // 2
    y = mp % 2
    base = (dp // GROUP) * GROUP
    mine = dp % GROUP
    x = mine // 2
    c = mine % 2
    core_dl = x * 2 + (1 - c)
    x_dl = (1 - x) * 2 + c
    xc_dl = (1 - x) * 2 + (1 - c)
    to_core = (base + core_dl, mp)
    to_x = (base + x_dl, mp)
    to_y = (dp, z * 2 + (1 - y))

    def z_at(step):
        return (z + step) % z_count

    def to_z(step):
        return (dp, z_at(step) * 2 + y)

    def to_group(step):
        return ((dp + GROUP * step) % n_dp, mp)

    pending = []

    def send(src, dst, s_sem, r_sem, device):
        copy = pltpu.make_async_remote_copy(
            src_ref=src,
            dst_ref=dst,
            send_sem=s_sem,
            recv_sem=r_sem,
            device_id=device,
            device_id_type=MESH,
        )
        copy.start()
        pending.append(copy)
        return copy

    def forget(copy):
        pending[:] = [other for other in pending if other is not copy]

    def sent(copy):
        copy.wait_send()
        forget(copy)

    barrier = pltpu.get_barrier_semaphore()
    peers = [to_core, to_x, to_y]
    peers += [to_z(step) for step in range(1, z_count)]
    peers += [to_group(step) for step in range(1, groups)]
    for peer in peers:
        pl.semaphore_signal(barrier, inc=1, device_id=peer, device_id_type=MESH)

    own = pl.ds(pl.multiple_of(block * mp, 16), block)

    @pl.when(mine < 3)
    def _():
        wa[mine, own, :] = qkvw_ref[jnp.minimum(mine, 2)].T

    @pl.when(mine == 3)
    def _():
        wa[mine, own, :] = pw_ref[...]

    ft[...] = f1w_ref[...].T
    quarter = pl.ds(pl.multiple_of(block * mine, 16), block)
    wf[0, own, :] = ft[quarter, :]
    wf[1, own, :] = f2w_ref[quarter, :]

    pk[...] = jnp.zeros_like(pk)
    pk[0:heads_here, 0:ENTRIES] = tab_ref[...].T
    pk[3:5, 0:block] = qvb_ref[...]
    pk[5:6, :] = f1b_ref[...]
    sp[mp] = pk[...]

    pl.semaphore_wait(barrier, len(peers))

    def rows_of(other_z, other_y):
        return pl.ds(pl.multiple_of(block * (other_z * 2 + other_y), 16), block)

    class Gather:
        def __init__(self, index, buffer, part):
            self.index, self.buffer, self.part = index, buffer, part
            self.along_z, self.along_y = [None], []

        def forward_y(self, part):
            k = len(self.along_y)
            ref = self.buffer.at[part]
            self.along_y.append(
                send(ref, ref, sem_ws.at[self.index, z_count + k], sem_wr.at[self.index, z_count + k], to_y)
            )

        def start(self):
            ref = self.buffer.at[self.part(z, y)]
            for step in range(1, z_count):
                self.along_z.append(
                    send(
                        ref,
                        ref,
                        sem_ws.at[self.index, step - 1],
                        sem_wr.at[self.index, step - 1],
                        to_z(step),
                    )
                )
            self.forward_y(self.part(z, y))

        def arrive_z(self, step):
            self.along_z[step].wait_recv()
            part = self.part((z + z_count - step) % z_count, y)
            self.forward_y(part)
            return part

        def arrive_y(self, step):
            self.along_y[step].wait_recv()
            return self.part((z + z_count - step) % z_count, 1 - y)

    small = Gather(0, sp, lambda oz, oy: oz * 2 + oy)
    attn_w = Gather(1, wa.at[mine], rows_of)
    fc1_w = Gather(2, wf.at[0], rows_of)
    fc2_w = Gather(3, wf.at[1], rows_of)

    small.start()
    attn_w.start()

    def send_rows(ring, index, slot, device, k):
        return send(ring.at[slot], ring.at[slot], sem_rs.at[index, k], sem_rr.at[index, k], device)

    kinds = [kind_ref[mp * windows + w] for w in range(windows)]
    place_row, live_row = slot_place(iota((1, padded), 1), windows, kinds)
    place_col, live_col = slot_place(iota((padded, 1), 0), windows, kinds)
    spread = one_hot(iota((places, padded), 0) == place_row, BF)
    gather = one_hot(iota((padded, places), 1) == place_col, BF)
    row_live = jnp.where(live_col, 1.0, 0.0)

    xs[...] = jnp.zeros_like(xs)
    xs[0:rows, :] = tok_ref[...].astype(F32)
    gs[...] = jnp.zeros_like(gs)
    gs[0:rows, :] = og_ref[...].astype(F32)

    sg[...] = jnp.zeros_like(sg)
    masked = gs[...] * row_live
    sg[5:6, :] = jnp.sum(masked, axis=0, keepdims=True)
    gg[mine] = masked.astype(BF)
    gg_x = send_rows(gg, 0, mine, to_x, 0)
    gg_c0 = send_rows(gg, 0, mine, to_core, 1)

    normed_one, scale_one = norm_parts(xs[...])
    n1s[...] = normed_one
    stats[:, 0:1] = scale_one
    h1 = (normed_one * n1g_ref[...] + n1b_ref[...]).astype(BF)
    h1p[...] = dot_nn(spread, h1).astype(BF)

    for step in range(1, z_count):
        small.arrive_z(step)
    along_x = []

    def forward_x(part):
        k = len(along_x)
        ref = wa.at[mine].at[part]
        along_x.append(send(ref, ref, sem_bs.at[k], sem_br.at[k], to_x))

    forward_x(attn_w.part(z, y))
    for step in range(1, z_count):
        forward_x(attn_w.arrive_z(step))
    fc1_w.start()
    for step in range(z_count):
        small.arrive_y(step)
    for step in range(z_count):
        forward_x(attn_w.arrive_y(step))
    core_a = send(wa.at[mine], wa.at[mine], sem_bs.at[n_mp], sem_br.at[n_mp], to_core)

    lane = iota((1, width), 1)
    owner = steps_of(lane, block, n_mp)
    within = lane - block * owner
    pick_row = iota((n_mp, width), 0) == owner
    spots = iota((hidden, width), 0)

    def spread_row(row, offset):
        picked = dot_nn(sp[:, row, :], one_hot(spots == within + offset, F32), HIGHEST)
        return jnp.sum(jnp.where(pick_row, picked, 0.0), axis=0, keepdims=True)

    qb[0:1, :] = spread_row(3, 0)
    qb[1:2, :] = spread_row(4, 0)
    fb[0:1, :] = spread_row(5, block * mine)

    def table_place(cells, local):
        row, column = cells >> 3, cells & 7
        spot = SPAN * row + column
        if local:
            last = LOCAL_SIDE - 1
            dead = (row > last) | (column > last)
            spot = jnp.where(dead, SPAN * last + last, spot)
        return spot

    cell = iota((1, LANES), 1)
    cell_head, cell_spot = cell >> 6, cell & 63
    source = iota((PACK * TILE, LANES), 0)
    picks = []
    for local in (False, True):
        picks.append(one_hot(source == TILE * cell_head + table_place(cell_spot, local), BF))
    for tile in range(tiles):
        shifted = []
        for k in range(PACK):
            head = tile * PACK + k
            line = sp[head // heads_here, head % heads_here : head % heads_here + 1, 0:LANES]
            line = jnp.broadcast_to(line, (8, LANES))
            shifted.append(
                jnp.concatenate(
                    [
                        shear(line, (SPAN * r - CENTRE) % LANES)[:, 0:TILE]
                        for r in range(8)
                    ],
                    axis=0,
                )
            )
        high, low = split_two(jnp.concatenate(shifted, axis=1))
        bias_whole[tile] = dot_nn(high, picks[0]) + dot_nn(low, picks[0])
        bias_local[tile] = dot_nn(high, picks[1]) + dot_nn(low, picks[1])

    for step in range(1, z_count):
        fc1_w.arrive_z(step)
    fc2_w.start()

    for copy in along_x:
        copy.wait_recv()
    core_b = send(wa.at[x_dl], wa.at[x_dl], sem_bs.at[n_mp + 1], sem_br.at[n_mp + 1], to_core)
    gg_x.wait_recv()
    gg_c1 = send_rows(gg, 0, x_dl, to_core, 2)
    core_a.wait_recv()
    core_b.wait_recv()

    head_lane = iota((PACK * SLOTS, TILE), 1) >> 5
    head_mask = (iota((PACK * SLOTS, TILE), 0) >> 6) == head_lane
    key_place = iota((SLOTS, 1), 0)
    key_row, key_col = key_place >> 3, key_place & 7
    usable = []
    for w in range(windows):
        side = jnp.where(kinds[w] == 0, SIDE, LOCAL_SIDE)
        usable.append((key_row < side) & (key_col < side))

    def four(values):
        return jnp.where(head_mask, jnp.concatenate([values] * PACK, axis=0), 0.0).astype(BF)

    def fold(values):
        picked = jnp.where(head_mask, values, 0.0)
        total = picked[0:SLOTS]
        for k in range(1, PACK):
            total = total + picked[SLOTS * k : SLOTS * (k + 1)]
        return total

    def attend(tile, carry):
        cols = pl.ds(pl.multiple_of(tile * TILE, TILE), TILE)
        normed = h1p[...]
        q_tile = (dot_nt(normed, wa[0, cols, :]) + qb[0:1, cols]) * HEAD ** (-0.5)
        qs[tile] = q_tile.astype(BF)
        ks[tile] = dot_nt(normed, wa[1, cols, :]).astype(BF)
        vs[tile] = (dot_nt(normed, wa[2, cols, :]) + qb[1:2, cols]).astype(BF)
        for w in range(windows):
            part = pl.ds(SLOTS * w, SLOTS)
            scores = dot_nt(ks[tile, part, :], four(qs[tile, part, :].astype(F32)))
            bias = jnp.where(kinds[w] == 0, bias_whole[tile], bias_local[tile])
            scores = jnp.where(usable[w], scores + bias, NEG_FILL)
            raised = jnp.exp(scores - jnp.max(scores, axis=0, keepdims=True))
            probs = raised / jnp.sum(raised, axis=0, keepdims=True)
            pt[tile * windows + w] = probs
            at[tile, part, :] = fold(dot_tn(probs.astype(BF), vs[tile, part, :])).astype(BF)
        return carry

    lax.fori_loop(0, tiles // 2, attend, 0)
    for step in range(z_count):
        fc1_w.arrive_y(step)
    for step in range(1, z_count):
        fc2_w.arrive_z(step)
    lax.fori_loop(tiles // 2, tiles, attend, 0)

    attn = jnp.concatenate(
        [dot_nn(gather, at[tile]).astype(BF) for tile in range(tiles)], axis=1
    )
    x1 = xs[...] + (dot_nn(attn, wa[3]) + pb_ref[...]) * row_live
    x1s[...] = x1
    normed_two, scale_two = norm_parts(x1)
    hg[mine] = (normed_two * n2g_ref[...] + n2b_ref[...]).astype(BF)
    hg_x = send_rows(hg, 1, mine, to_x, 0)
    hg_c0 = send_rows(hg, 1, mine, to_core, 1)

    for step in range(z_count):
        fc2_w.arrive_y(step)

    def slot_rows(slot):
        return pl.ds(pl.multiple_of(padded * slot, 16), padded)

    def mlp(slot):
        pre = dot_nt(hg[slot], wf[0]) + fb[0:1, :]
        square = pre * pre
        bend = jnp.tanh(GELU_A * (pre + GELU_B * (square * pre)))
        ac[slot_rows(slot), :] = (0.5 * pre * (1.0 + bend)).astype(BF)
        slope = 0.5 * (1.0 + bend) + 0.5 * pre * (1.0 - bend * bend) * (
            GELU_A * (1.0 + 3.0 * GELU_B * square)
        )
        dpre = (dot_nt(gg[slot], wf[1]) * slope).astype(BF)
        dp_s[slot_rows(slot), :] = dpre
        ph[slot] = dot_nn(dpre, wf[0]).astype(BF)

    gg_c0.wait_recv()
    hg_c0.wait_recv()
    hg_x.wait_recv()
    hg_c1 = send_rows(hg, 1, x_dl, to_core, 2)
    gg_c1.wait_recv()
    hg_c1.wait_recv()
    mlp(xc_dl)
    ph_c0 = send(ph.at[xc_dl], rc_h.at[0], sem_hs.at[0, 0], sem_hr.at[0, 0], to_core)
    mlp(core_dl)
    ph_c1 = send(ph.at[core_dl], rc_h.at[1], sem_hs.at[0, 1], sem_hr.at[0, 1], to_core)
    mlp(x_dl)
    ph_c0.wait_recv()
    ph2[0] = (ph[x_dl].astype(F32) + rc_h[0].astype(F32)).astype(BF)
    ph_x = send(ph2.at[0], rx_h, sem_hs.at[0, 2], sem_hr.at[0, 2], to_x)
    mlp(mine)

    half_rows = width // 2
    tiles_half = tiles // 2

    def all_rows(ring):
        return ring[...].reshape(GROUP * padded, width)

    def fc1_grad(tile, carry):
        cols = pl.ds(pl.multiple_of(tile * TILE, TILE), TILE)
        left = dp_s[:, cols]
        gf[0, cols, :] = dot_tn(left, all_rows(hg)).astype(BF)
        return carry

    def fc2_grad(tile, carry):
        cols = pl.ds(pl.multiple_of(tile * TILE, TILE), TILE)
        left = ac[:, cols]
        gf[1, cols, :] = dot_tn(left, all_rows(gg)).astype(BF)
        return carry

    sg[pl.ds(8 + mine, 1), :] = jnp.sum(dp_s[...].astype(F32), axis=0, keepdims=True)

    along_y = {}

    def scatter_y(index, source, other_z):
        part = rows_of(other_z, 1 - y)
        along_y[index, other_z] = send(
            source.at[part],
            ry.at[index, other_z],
            sem_ys.at[index, other_z],
            sem_yr.at[index, other_z],
            to_y,
        )

    lax.fori_loop(0, tiles, fc2_grad, 0)
    for other_z in range(z_count):
        scatter_y(2, gf.at[1], other_z)

    ph_c1.wait_recv()
    ph_x.wait_recv()
    dh2 = ph[mine].astype(F32) + rc_h[1].astype(F32) + rx_h[...].astype(F32)
    sg[3:4, :] = jnp.sum(dh2 * normed_two, axis=0, keepdims=True)
    sg[4:5, :] = jnp.sum(dh2, axis=0, keepdims=True)
    dx1 = gs[...] + norm_back(dh2 * n2g_ref[...], normed_two, scale_two)
    gs[...] = dx1
    gab = dx1 * row_live
    sg[2:3, :] = jnp.sum(gab, axis=0, keepdims=True)
    gab = gab.astype(BF)
    gabp[...] = dot_nn(spread, gab).astype(BF)

    lax.fori_loop(0, tiles, fc1_grad, 0)
    for other_z in range(z_count):
        scatter_y(1, gf.at[0], other_z)

    dbias[...] = jnp.zeros_like(dbias)
    dh1[...] = jnp.zeros_like(dh1)

    def attend_back(tile, carry):
        cols = pl.ds(pl.multiple_of(tile * TILE, TILE), TILE)
        dattn = dot_nt(gabp[...], wa[3, cols, :])
        normed = h1p[...]
        total = jnp.zeros((SLOTS, LANES), F32)
        for w in range(windows):
            part = pl.ds(SLOTS * w, SLOTS)
            d_four = four(dattn[SLOTS * w : SLOTS * (w + 1)])
            q_four = four(qs[tile, part, :].astype(F32))
            probs = pt[tile * windows + w]
            dprob = dot_nt(vs[tile, part, :], d_four)
            weighed = probs * dprob
            ds = weighed - probs * jnp.sum(weighed, axis=0, keepdims=True)
            total = total + ds
            dsb = ds.astype(BF)
            dvs[tile, part, :] = dot_nn(probs.astype(BF), d_four).astype(BF)
            dks[tile, part, :] = dot_nn(dsb, q_four).astype(BF)
            dqs[tile, part, :] = (
                fold(dot_tn(dsb, ks[tile, part, :])) * HEAD ** (-0.5)
            ).astype(BF)
        dbias[tile] = total
        for s, grads in enumerate((dqs, dks, dvs)):
            ga[s, cols, :] = dot_tn(grads[tile], normed).astype(BF)
            dh1[...] += dot_nn(grads[tile], wa[s, cols, :])
        sg[6:7, cols] = jnp.sum(dqs[tile].astype(F32), axis=0, keepdims=True)
        sg[7:8, cols] = jnp.sum(dvs[tile].astype(F32), axis=0, keepdims=True)
        attn_tile = dot_nn(gather, at[tile]).astype(BF)
        ga[3, cols, :] = dot_tn(attn_tile, gab).astype(BF)
        return carry

    halves = [pl.ds(0, half_rows), pl.ds(half_rows, half_rows)]
    core_copies, x_copies = [], []

    def reduce_core(half):
        for k, slot in enumerate((xc_dl, core_dl)):
            core_copies.append(
                send(
                    ga.at[slot].at[halves[half]],
                    rca.at[k].at[halves[half]],
                    sem_as.at[half, k],
                    sem_ar.at[half, k],
                    to_core,
                )
            )

    def reduce_x(half):
        part = halves[half]
        core_copies[2 * half].wait_recv()
        rca[0, part, :] = (ga[x_dl, part, :].astype(F32) + rca[0, part, :].astype(F32)).astype(BF)
        x_copies.append(
            send(
                rca.at[0].at[part],
                rxa.at[part],
                sem_as.at[half, 2],
                sem_ar.at[half, 2],
                to_x,
            )
        )

    lax.fori_loop(0, tiles_half, attend_back, 0)
    reduce_core(0)

    def mlp_out(slot):
        ph[slot] = dot_nn(ac[slot_rows(slot), :], wf[1]).astype(BF)

    out_copies = []
    sent(ph_c0)
    sent(ph_c1)
    mlp_out(xc_dl)
    out_copies.append(send(ph.at[xc_dl], rc_o.at[0], sem_hs.at[1, 0], sem_hr.at[1, 0], to_core))
    mlp_out(core_dl)
    out_copies.append(send(ph.at[core_dl], rc_o.at[1], sem_hs.at[1, 1], sem_hr.at[1, 1], to_core))
    reduce_x(0)
    mlp_out(x_dl)
    out_copies[0].wait_recv()
    ph2[1] = (ph[x_dl].astype(F32) + rc_o[0].astype(F32)).astype(BF)
    lax.fori_loop(tiles_half, tiles, attend_back, 0)
    reduce_core(1)
    out_copies.append(send(ph2.at[1], rx_o, sem_hs.at[1, 2], sem_hr.at[1, 2], to_x))
    mlp_out(mine)

    along_z = {}

    def scatter_z(index, source):
        for other_z in range(z_count):
            along_y[index, other_z].wait_recv()
            part = rows_of(other_z, y)
            ry[index, other_z] = (
                ry[index, other_z].astype(F32) + source[part, :].astype(F32)
            ).astype(BF)
        for step in range(1, z_count):
            along_z[index, step] = send(
                ry.at[index, z_at(step)],
                rz.at[index, step - 1],
                sem_fs.at[index, step - 1],
                sem_fr.at[index, step - 1],
                to_z(step),
            )

    scatter_z(2, gf.at[1])
    reduce_x(1)
    scatter_z(1, gf.at[0])

    d_high = dh1[...].astype(BF)
    dh1c = dot_nn(gather, d_high)
    n1 = n1s[...]
    sg[0:1, :] = jnp.sum(dh1c * n1, axis=0, keepdims=True)
    sg[1:2, :] = jnp.sum(dh1c, axis=0, keepdims=True)
    dn = norm_back(dh1c * n1g_ref[...], n1, stats[:, 0:1])
    tgrad_ref[...] = (gs[...] + dn).astype(BF)[0:rows]

    back = one_hot(
        iota((LANES, PACK * TILE), 1)
        == TILE * (iota((LANES, 1), 0) >> 6)
        + (TILE - 1 - table_place(iota((LANES, 1), 0) & 63, False)),
        BF,
    )
    for tile in range(tiles):
        high, low = split_two(dbias[tile])
        wide = dot_nn(high, back) + dot_nn(low, back)
        for k in range(PACK):
            head = tile * PACK + k
            line = jnp.zeros((8, LANES), F32)
            for r in range(8):
                piece = wide[8 * r : 8 * (r + 1), TILE * k : TILE * (k + 1)]
                piece = jnp.concatenate([piece, jnp.zeros_like(piece)], axis=1)
                shift = LANES - 1 - CENTRE - (TILE - 1) + SPAN * r
                line = line + shear(piece, shift)
            row, spot = 12 + head // heads_here, LANES * (head % heads_here)
            sg[row : row + 1, spot : spot + LANES] = jnp.sum(line, axis=0, keepdims=True)

    def small_sum(stage, devices):
        copies = [
            send(
                sg,
                sg_in.at[stage + k],
                sem_ss.at[stage + k],
                sem_sr.at[stage + k],
                device,
            )
            for k, device in enumerate(devices)
        ]
        for copy in copies:
            copy.wait()
            forget(copy)
        total = sg[...]
        for k in range(len(devices)):
            total = total + sg_in[stage + k]
        sg[...] = total

    small_sum(0, [to_core])
    small_sum(1, [to_x])

    out_copies[1].wait_recv()
    out_copies[2].wait_recv()
    branch = ph[mine].astype(F32) + rc_o[1].astype(F32) + rx_o[...].astype(F32)
    out_ref[...] = (x1s[...] + (branch + f2b_ref[...]) * row_live).astype(BF)[0:rows]

    small_sum(2, [to_y])

    for half in range(2):
        part = halves[half]
        core_copies[2 * half + 1].wait_recv()
        x_copies[half].wait_recv()
        ga[mine, part, :] = (
            ga[mine, part, :].astype(F32)
            + rca[1, part, :].astype(F32)
            + rxa[part, :].astype(F32)
        ).astype(BF)
        for other_z in range(half * (z_count // 2), (half + 1) * (z_count // 2)):
            scatter_y(0, ga.at[mine], other_z)

    small_sum(3, [to_z(step) for step in range(1, z_count)])
    if groups > 1:
        small_sum(2 + z_count, [to_group(step) for step in range(1, groups)])

    final_copies = {}

    def finish(index):
        total = ry[index, z].astype(F32)
        for step in range(1, z_count):
            along_z[index, step].wait_recv()
            total = total + rz[index, step - 1].astype(F32)
        fin[index, mine] = total.astype(BF)
        if groups > 1:
            for step in range(1, groups):
                copy = send(
                    fin.at[index, mine],
                    sg_group.at[index, step - 1],
                    sem_gs.at[index, step - 1],
                    sem_gr.at[index, step - 1],
                    to_group(step),
                )
                copy.wait()
                forget(copy)
                total = total + sg_group[index, step - 1].astype(F32)
            fin[index, mine] = total.astype(BF)
        slot = fin.at[index, mine]
        sems = 3 + 3 * index
        final_copies[index, 0] = send(slot, slot, sem_fs.at[3, sems], sem_fr.at[3, sems], to_x)
        final_copies[index, 1] = send(
            slot, slot, sem_fs.at[3, sems + 1], sem_fr.at[3, sems + 1], to_core
        )

    def finish_core(index):
        final_copies[index, 0].wait_recv()
        slot = fin.at[index, x_dl]
        sems = 3 + 3 * index
        final_copies[index, 2] = send(
            slot, slot, sem_fs.at[3, sems + 2], sem_fr.at[3, sems + 2], to_core
        )

    def finish_wait(index):
        final_copies[index, 1].wait_recv()
        final_copies[index, 2].wait_recv()

    finish(2)
    finish(1)
    scatter_z(0, ga.at[mine])
    finish_core(2)
    finish_core(1)
    finish_wait(2)
    f2g_ref[...] = fin[2].reshape(hidden, width).astype(F32)
    finish_wait(1)
    f1g_ref[...] = fin[1].reshape(hidden, width).astype(F32).T

    vec_ref[...] = sg[0:8, :]
    pick = one_hot(iota((width, block), 0) == block * mp + iota((width, block), 1), F32)
    qvg_ref[...] = dot_nn(sg[0:8, :], pick, HIGHEST)[6:8]
    wide_lane = iota((width, hidden), 1)
    pick = one_hot(
        iota((width, hidden), 0) == block * mp + wide_lane - block * steps_of(wide_lane, block, hidden // block), F32
    )
    lines = dot_nn(sg[8:16, :], pick, HIGHEST)
    keep = iota((8, hidden), 0) == steps_of(iota((8, hidden), 1), block, hidden // block)
    f1bg_ref[...] = jnp.sum(jnp.where(keep, lines, 0.0), axis=0, keepdims=True)
    table = sg[pl.ds(12 + mp, 1), :]
    table = jnp.concatenate(
        [table[:, LANES * k : LANES * (k + 1)] for k in range(heads_here)]
        + [jnp.zeros((8 - heads_here, LANES), F32)],
        axis=0,
    )
    turn = one_hot(iota((176, LANES), 0) + iota((176, LANES), 1) == LANES - 1, F32)
    relg_ref[...] = dot_nt(turn, table, HIGHEST)[0:ENTRIES, 0:heads_here]

    finish(0)
    finish_core(0)
    finish_wait(0)
    for s in range(3):
        qkvg_ref[s] = fin[0, s].astype(F32).T
    projg_ref[...] = fin[0, 3].astype(F32)

    for copy in pending:
        copy.wait_send()


def solution(mesh):
    n_dp, n_mp = mesh.shape["dp"], mesh.shape["mp"]

    def shards(
        tokens,
        crop_kind,
        norm1_gain,
        norm1_bias,
        qkv_weight,
        qv_bias,
        rel_table,
        proj_weight,
        proj_bias,
        norm2_gain,
        norm2_bias,
        fc1_weight,
        fc1_bias,
        fc2_weight,
        fc2_bias,
        out_grad,
    ):
        rows, width = tokens.shape
        windows = rows // WIN
        padded = -(-rows // 16) * 16
        block = proj_weight.shape[0]
        hidden = fc2_weight.shape[0]
        heads_here = rel_table.shape[1]
        places = SLOTS * windows
        tiles = width // TILE
        z_count = n_mp // 2
        groups = n_dp // GROUP
        dims = (n_dp, n_mp, rows, windows, padded, width, block, hidden)

        def line(vector):
            return vector.reshape(1, -1)

        def full(*shape):
            return jax.ShapeDtypeStruct(shape, F32)

        vmem = pl.BlockSpec(memory_space=pltpu.VMEM)
        dma = pltpu.SemaphoreType.DMA
        results = pl.pallas_call(
            functools.partial(body, dims),
            out_shape=[
                jax.ShapeDtypeStruct((rows, width), BF),
                jax.ShapeDtypeStruct((rows, width), BF),
                full(8, width),
                full(3, width, block),
                full(2, block),
                full(ENTRIES, heads_here),
                full(block, width),
                full(width, hidden),
                full(1, hidden),
                full(hidden, width),
            ],
            in_specs=[pl.BlockSpec(memory_space=pltpu.SMEM)] + [vmem] * 15,
            out_specs=[vmem] * 10,
            scratch_shapes=[
                pltpu.VMEM((GROUP, width, width), BF),
                pltpu.VMEM((2, width, width), BF),
                pltpu.VMEM((hidden, width), BF),
                pltpu.VMEM((n_mp, 8, hidden), F32),
                pltpu.VMEM((8, hidden), F32),
                pltpu.VMEM((padded, width), F32),
                pltpu.VMEM((padded, width), F32),
                pltpu.VMEM((padded, width), F32),
                pltpu.VMEM((padded, width), F32),
                pltpu.VMEM((padded, TILE), F32),
                pltpu.VMEM((8, width), F32),
                pltpu.VMEM((8, width), F32),
                pltpu.VMEM((places, width), BF),
                pltpu.VMEM((tiles, places, TILE), BF),
                pltpu.VMEM((tiles, places, TILE), BF),
                pltpu.VMEM((tiles, places, TILE), BF),
                pltpu.VMEM((tiles, places, TILE), BF),
                pltpu.VMEM((tiles * windows, SLOTS, LANES), F32),
                pltpu.VMEM((tiles, SLOTS, LANES), F32),
                pltpu.VMEM((tiles, SLOTS, LANES), F32),
                pltpu.VMEM((GROUP, padded, width), BF),
                pltpu.VMEM((GROUP, padded, width), BF),
                pltpu.VMEM((GROUP * padded, width), BF),
                pltpu.VMEM((GROUP * padded, width), BF),
                pltpu.VMEM((GROUP, padded, width), BF),
                pltpu.VMEM((2, padded, width), BF),
                pltpu.VMEM((padded, width), BF),
                pltpu.VMEM((2, padded, width), BF),
                pltpu.VMEM((2, padded, width), BF),
                pltpu.VMEM((padded, width), BF),
                pltpu.VMEM((places, width), BF),
                pltpu.VMEM((tiles, places, TILE), BF),
                pltpu.VMEM((tiles, places, TILE), BF),
                pltpu.VMEM((tiles, places, TILE), BF),
                pltpu.VMEM((tiles, SLOTS, LANES), F32),
                pltpu.VMEM((places, width), F32),
                pltpu.VMEM((GROUP, width, width), BF),
                pltpu.VMEM((2, width, width), BF),
                pltpu.VMEM((2, width, width), BF),
                pltpu.VMEM((width, width), BF),
                pltpu.VMEM((3, z_count, block, width), BF),
                pltpu.VMEM((3, z_count - 1, block, width), BF),
                pltpu.VMEM((3, GROUP, block, width), BF),
                pltpu.VMEM((24, width), F32),
                pltpu.VMEM((2 + z_count + groups, 24, width), F32),
                pltpu.VMEM((3, max(groups - 1, 1), block, width), BF),
                dma((4, 2 * z_count + 2)),
                dma((4, 2 * z_count + 2)),
                dma((n_mp + 2,)),
                dma((n_mp + 2,)),
                dma((2, 3)),
                dma((2, 3)),
                dma((2, 3)),
                dma((2, 3)),
                dma((2, 3)),
                dma((2, 3)),
                dma((3, z_count)),
                dma((3, z_count)),
                dma((4, 12)),
                dma((4, 12)),
                dma((2 + z_count + groups,)),
                dma((2 + z_count + groups,)),
                dma((3, max(groups - 1, 1))),
                dma((3, max(groups - 1, 1))),
            ],
            compiler_params=pltpu.CompilerParams(
                collective_id=0, has_side_effects=True, vmem_limit_bytes=63 * 2**20
            ),
        )(
            crop_kind,
            tokens,
            out_grad,
            line(norm1_gain),
            line(norm1_bias),
            qkv_weight,
            qv_bias,
            rel_table,
            proj_weight,
            line(proj_bias),
            line(norm2_gain),
            line(norm2_bias),
            fc1_weight,
            line(fc1_bias),
            fc2_weight,
            line(fc2_bias),
        )
        block_out, tokens_grad, vec, qkvg, qvg, relg, projg, f1g, f1bg, f2g = results
        return (
            block_out,
            tokens_grad,
            vec[0],
            vec[1],
            qkvg,
            qvg,
            relg,
            projg,
            vec[2],
            vec[3],
            vec[4],
            f1g,
            f1bg.reshape(-1),
            f2g,
            vec[5],
        )

    in_specs = (
        P(("dp", "mp"), None),
        P("dp"),
        P(),
        P(),
        P(None, None, "mp"),
        P(None, "mp"),
        P(None, "mp"),
        P("mp", None),
        P(),
        P(),
        P(),
        P(None, "mp"),
        P("mp"),
        P("mp", None),
        P(),
        P(("dp", "mp"), None),
    )
    out_specs = (
        P(("dp", "mp"), None),
        P(("dp", "mp"), None),
        P(),
        P(),
        P(None, None, "mp"),
        P(None, "mp"),
        P(None, "mp"),
        P("mp", None),
        P(),
        P(),
        P(),
        P(None, "mp"),
        P("mp"),
        P("mp", None),
        P(),
    )
    return jax.shard_map(shards, mesh=mesh, in_specs=in_specs, out_specs=out_specs, check_vma=False)
```

```python
import functools

import jax
import jax.numpy as jnp
from jax import lax
from jax.experimental import pallas as pl
from jax.experimental.pallas import tpu as pltpu
from jax.sharding import PartitionSpec as P

HEAD = 32
SIDE = 7
LOCAL_SIDE = 3
WIN = 49
SPAN = 2 * SIDE - 1
ENTRIES = SPAN * SPAN
CENTRE = (SIDE - 1) * SPAN + SIDE - 1
SLOTS = 64
TILE = 128
PACK = 4
GROUP = 4
LANES = 256
EPSILON = 1e-05
NEG_FILL = -1000000000.0
GELU_A = 0.7978845608028654
GELU_B = 0.044715
HIGHEST = lax.Precision.HIGHEST
MESH = pl.DeviceIdType.MESH
BF = jnp.bfloat16
F32 = jnp.float32


def dot(left, right, dims, precision=None):
    return lax.dot_general(
        left, right, (dims, ((), ())), preferred_element_type=F32, precision=precision
    )


def dot_nn(left, right, precision=None):
    return dot(left, right, ((1,), (0,)), precision)


def dot_nt(left, right, precision=None):
    return dot(left, right, ((1,), (1,)), precision)


def dot_tn(left, right, precision=None):
    return dot(left, right, ((0,), (0,)), precision)


def iota(shape, axis):
    return lax.broadcasted_iota(jnp.int32, shape, axis)


def one_hot(cond, dtype):
    return jnp.where(cond, 1.0, 0.0).astype(dtype)


def steps_of(values, width, count):
    total = jnp.zeros_like(values)
    for step in range(1, count):
        total = total + jnp.where(values >= step * width, 1, 0)
    return total


def shear(values, shift):
    moved = pltpu.roll(values, shift, axis=1)
    return pltpu.roll(moved, 0, axis=1, stride=1, stride_axis=0)


def split_two(values):
    high = values.astype(BF)
    return high, (values - high.astype(F32)).astype(BF)


def flat_row(ref):
    return ref[...].reshape(1, -1)


def norm_parts(values):
    mean = jnp.mean(values, axis=-1, keepdims=True)
    centre = values - mean
    spread = jnp.mean(centre * centre, axis=-1, keepdims=True)
    scale = lax.rsqrt(spread + EPSILON)
    return centre * scale, scale


def norm_back(grad_normed, normed, scale):
    return scale * (
        grad_normed
        - jnp.mean(grad_normed, axis=-1, keepdims=True)
        - normed * jnp.mean(grad_normed * normed, axis=-1, keepdims=True)
    )


def slot_place(columns, windows, kinds):
    window = steps_of(columns, WIN, windows)
    slot = columns - WIN * window
    kind = jnp.zeros_like(columns)
    for w in range(windows):
        kind = jnp.where(window == w, kinds[w], kind)
    whole = slot + steps_of(slot, SIDE, SIDE)
    corner = slot + (8 - LOCAL_SIDE) * steps_of(slot, LOCAL_SIDE, LOCAL_SIDE)
    rest = slot + (8 * LOCAL_SIDE - LOCAL_SIDE * LOCAL_SIDE)
    local = jnp.where(slot < LOCAL_SIDE * LOCAL_SIDE, corner, rest)
    place = SLOTS * window + jnp.where(kind == 0, whole, local)
    live = jnp.where(kind == 0, WIN, LOCAL_SIDE * LOCAL_SIDE)
    inside = columns < WIN * windows
    return jnp.where(inside, place, -1), inside & (slot < live)


def body(
    dims,
    kind_ref,
    tok_ref,
    og_ref,
    n1g_ref,
    n1b_ref,
    qkvw_ref,
    qvb_ref,
    tab_ref,
    pw_ref,
    pb_ref,
    n2g_ref,
    n2b_ref,
    f1w_ref,
    f1b_ref,
    f2w_ref,
    f2b_ref,
    out_ref,
    tgrad_ref,
    vec_ref,
    small_ref,
    fin_ref,
    wa,
    wf,
    ft,
    sp,
    pk,
    xs,
    x1s,
    n1s,
    gs,
    stats,
    qb,
    fb,
    h1p,
    qs,
    ks,
    vs,
    at,
    pt,
    bias_whole,
    bias_local,
    hg,
    gg,
    ac,
    dp_s,
    ph,
    rc_h,
    rx_h,
    ph2,
    rc_o,
    rx_o,
    gabp,
    dqs,
    dks,
    dvs,
    dbias,
    dh1,
    ga,
    gf,
    rca,
    rxa,
    ry_a,
    rz_a,
    ry_m,
    rz_m,
    fin,
    fin_a,
    fin_x,
    group_m,
    group_a,
    sg,
    sg_in,
    sem_ws,
    sem_wr,
    sem_bs,
    sem_br,
    sem_rs,
    sem_rr,
    sem_hs,
    sem_hr,
    sem_as,
    sem_ar,
    sem_ys,
    sem_yr,
    sem_zs,
    sem_zr,
    sem_fs,
    sem_fr,
    sem_ss,
    sem_sr,
    sem_gs,
    sem_gr,
):
    n_dp, n_mp, rows, windows, padded, width, block, hidden = dims
    groups = n_dp // GROUP
    places = SLOTS * windows
    z_count = n_mp // 2
    heads_here = block // HEAD
    tiles = width // TILE
    half_width = width // 2
    mp = lax.axis_index("mp")
    dp = lax.axis_index("dp")
    z = mp // 2
    y = mp % 2
    base = (dp // GROUP) * GROUP
    mine = dp % GROUP
    x = mine // 2
    c = mine % 2
    core_dl = x * 2 + (1 - c)
    x_dl = (1 - x) * 2 + c
    xc_dl = (1 - x) * 2 + (1 - c)
    to_core = (base + core_dl, mp)
    to_x = (base + x_dl, mp)
    to_y = (dp, z * 2 + (1 - y))
    near = 2 * x
    far = 2 - 2 * x

    def z_at(step):
        return (z + step) % z_count

    def to_z(step):
        return (dp, z_at(step) * 2 + y)

    def to_group(step):
        return ((dp + GROUP * step) % n_dp, mp)

    pending = []

    def remote(src, dst, s_sem, r_sem, device):
        return pltpu.make_async_remote_copy(
            src_ref=src,
            dst_ref=dst,
            send_sem=s_sem,
            recv_sem=r_sem,
            device_id=device,
            device_id_type=MESH,
        )

    def send(src, dst, s_sem, r_sem, device, when=None):
        copy = remote(src, dst, s_sem, r_sem, device)
        if when is None:
            copy.start()
        else:
            pl.when(when)(copy.start)
        pending.append((copy, when))
        return copy

    def forget(copy):
        pending[:] = [other for other in pending if other[0] is not copy]

    def sent(copy):
        copy.wait_send()
        forget(copy)

    barrier = pltpu.get_barrier_semaphore()
    peers = [to_core, to_x, to_y]
    peers += [to_z(step) for step in range(1, z_count)]
    peers += [to_group(step) for step in range(1, groups)]
    for peer in peers:
        pl.semaphore_signal(barrier, inc=1, device_id=peer, device_id_type=MESH)

    own = pl.ds(pl.multiple_of(block * mp, 16), block)
    my_cols = pl.ds(pl.multiple_of(half_width * c, TILE), half_width)
    her_cols = pl.ds(pl.multiple_of(half_width * (1 - c), TILE), half_width)
    for s in range(3):
        wa[s, own, my_cols] = qkvw_ref[s, :, my_cols]
    wa[3, own, my_cols] = pw_ref[:, my_cols]

    pk[...] = jnp.zeros_like(pk)
    pk[0:heads_here, 0:ENTRIES] = tab_ref[...]
    pk[3:5, 0:block] = qvb_ref[...]
    pk[5:6, :] = flat_row(f1b_ref)
    sp[mp] = pk[...]

    pl.semaphore_wait(barrier, len(peers))

    def rows_of(other_z, other_y):
        return pl.ds(pl.multiple_of(block * (other_z * 2 + other_y), 16), block)

    relayed = z_count == 4
    if relayed:
        order = [2, jnp.where(z == 0, 3, 1), jnp.where(z == 0, 1, 3)]
    else:
        order = list(range(1, z_count))
    inner = (z == 1) | (z == 2)

    def spread_z(buffer, part, index, first):
        ref = buffer.at[part]
        for step in range(1, z_count):
            far_end = {1: z != 3, 2: None, 3: z != 0}[step] if relayed else None
            k = first + step - 1
            send(ref, ref, sem_ws.at[index, k], sem_wr.at[index, k], to_z(step), far_end)

    def arrived_z(buffer, part_of, index, first, place):
        step = order[place]
        part = part_of((z + z_count - step) % z_count)
        ref = buffer.at[part]
        k = first + step - 1
        remote(ref, ref, sem_ws.at[index, k], sem_wr.at[index, k], to_y).wait_recv()
        if relayed and place == 0:
            last = 2 * (z - 1)
            send(
                ref,
                ref,
                sem_ws.at[index, first + 3],
                sem_wr.at[index, first + last],
                (dp, 3 * (z - 1) * 2 + y),
                inner,
            )
        return part

    class Gather:
        def __init__(self, index, buffer, part):
            self.index, self.buffer, self.part = index, buffer, part

        def forward_y(self, part, step):
            k = z_count + step
            ref = self.buffer.at[part]
            send(ref, ref, sem_ws.at[self.index, k], sem_wr.at[self.index, k], to_y)

        def start_y(self):
            self.forward_y(self.part(z, y), 0)

        def start_z(self):
            spread_z(self.buffer, self.part(z, y), self.index, 0)

        def arrive_z(self, place):
            part = arrived_z(self.buffer, lambda oz: self.part(oz, y), self.index, 0, place)
            self.forward_y(part, order[place])
            return part

        def arrive_y(self, place):
            step = 0 if place == 0 else order[place - 1]
            part = self.part((z + z_count - step) % z_count, 1 - y)
            ref = self.buffer.at[part]
            k = z_count + step
            remote(ref, ref, sem_ws.at[self.index, k], sem_wr.at[self.index, k], to_y).wait_recv()
            return part

    class GatherLong:
        def __init__(self, index, buffer, part):
            self.index, self.buffer, self.part = index, buffer, part

        def pair(self):
            ref = self.buffer.at[self.part(z, y)]
            k = 2 * z_count
            return ref, ref, sem_ws.at[self.index, k], sem_wr.at[self.index, k], to_y

        def start_y(self):
            send(*self.pair())

        def start_z(self):
            spread_z(self.buffer, self.part(z, y), self.index, 0)

        def arrive_y(self):
            remote(*self.pair()).wait_recv()
            spread_z(self.buffer, self.part(z, 1 - y), self.index, z_count)

        def arrive_z(self, place):
            for column in range(2):
                other_y = y if column == 0 else 1 - y
                arrived_z(
                    self.buffer,
                    lambda oz: self.part(oz, other_y),
                    self.index,
                    z_count * column,
                    place,
                )

    def half_block(other_z, other_y):
        return rows_of(other_z, other_y), my_cols

    def whole_block(other_z, other_y):
        return (rows_of(other_z, other_y),)

    def quarter_block(other_z, other_y):
        start = block * (other_z * 2 + other_y) + (block // 2) * x
        return pl.ds(pl.multiple_of(start, 16), block // 2), my_cols

    def left_block(other_z, other_y):
        return rows_of(other_z, other_y), pl.ds(0, half_width)

    def right_block(other_z, other_y):
        return rows_of(other_z, other_y), pl.ds(half_width, half_width)

    small = Gather(0, sp, lambda oz, oy: (oz * 2 + oy,))
    near_w = Gather(1, wa.at[near], half_block)
    key_w = Gather(2, wa.at[1], half_block)
    proj_w = Gather(3, wa.at[3], quarter_block)
    fc1_w = Gather(4, wf.at[0], whole_block)
    fc2_w = Gather(5, wf.at[1], left_block)
    fc2_long = GatherLong(6, wf.at[1], right_block)
    later_z, later_y = range(z_count - 1), range(1, z_count)

    for part in (small, near_w, key_w):
        part.start_z()
        part.start_y()

    def send_rows(ring, index, slot, device, k):
        return send(ring.at[slot], ring.at[slot], sem_rs.at[index, k], sem_rr.at[index, k], device)

    kinds = [kind_ref[mp * windows + w] for w in range(windows)]
    place_row, _ = slot_place(iota((1, padded), 1), windows, kinds)
    place_col, live_col = slot_place(iota((padded, 1), 0), windows, kinds)
    spread = one_hot(iota((places, padded), 0) == place_row, BF)
    gather = one_hot(iota((padded, places), 1) == place_col, BF)
    row_live = jnp.where(live_col, 1.0, 0.0)

    gs[...] = jnp.zeros_like(gs)
    gs[0:rows, :] = og_ref[...].astype(F32)
    sg[...] = jnp.zeros_like(sg)
    masked = gs[...] * row_live
    gg[mine] = masked.astype(BF)
    gg_x = send_rows(gg, 0, mine, to_x, 0)
    gg_c0 = send_rows(gg, 0, mine, to_core, 1)
    sg[5:6, :] = jnp.sum(masked, axis=0, keepdims=True)

    xs[...] = jnp.zeros_like(xs)
    xs[0:rows, :] = tok_ref[...].astype(F32)
    normed_one, scale_one = norm_parts(xs[...])
    n1s[...] = normed_one
    stats[:, 0:1] = scale_one
    h1 = (normed_one * flat_row(n1g_ref) + flat_row(n1b_ref)).astype(BF)
    h1p[...] = dot_nn(spread, h1).astype(BF)

    along_x, proj_x = [], []

    def forward_x(part):
        k = len(along_x)
        ref = wa.at[near].at[part]
        along_x.append(send(ref, ref, sem_bs.at[k], sem_br.at[k], to_x))

    def forward_proj(part):
        k = n_mp + 4 + len(proj_x)
        ref = wa.at[3].at[part]
        proj_x.append(send(ref, ref, sem_bs.at[k], sem_br.at[k], to_x))

    ft[...] = f1w_ref[...].T
    quarter = pl.ds(pl.multiple_of(block * mine, 16), block)
    wf[0, own, :] = ft[quarter, :]
    wf[1, own, :] = f2w_ref[quarter, :]
    fc1_w.start_y()
    for place in later_z:
        small.arrive_z(place)
    forward_x(near_w.arrive_y(0))
    for place in later_z:
        forward_x(near_w.arrive_z(place))
        key_w.arrive_z(place)
        if place == 0:
            fc1_w.start_z()
            proj_w.start_z()
            proj_w.start_y()
    fc2_long.start_y()
    fc2_w.start_y()

    for place in range(z_count):
        small.arrive_y(place)
    lane = iota((1, width), 1)
    owner = steps_of(lane, block, n_mp)
    within = lane - block * owner
    pick_row = iota((n_mp, width), 0) == owner
    spots = iota((hidden, width), 0)

    def spread_row(row, offset):
        picked = dot_nn(sp[:, row, :], one_hot(spots == within + offset, F32), HIGHEST)
        return jnp.sum(jnp.where(pick_row, picked, 0.0), axis=0, keepdims=True)

    qb[0:1, :] = spread_row(3, 0)
    qb[1:2, :] = spread_row(4, 0)
    fb[0:1, :] = spread_row(5, block * mine)

    def table_place(cells, local):
        row, column = cells >> 3, cells & 7
        spot = SPAN * row + column
        if local:
            last = LOCAL_SIDE - 1
            dead = (row > last) | (column > last)
            spot = jnp.where(dead, SPAN * last + last, spot)
        return spot

    cell = iota((1, LANES), 1)
    cell_head, cell_spot = cell >> 6, cell & 63
    source = iota((PACK * TILE, LANES), 0)
    picks = []
    for local in (False, True):
        picks.append(one_hot(source == TILE * cell_head + table_place(cell_spot, local), BF))

    def bias_of(tile):
        shifted = []
        for k in range(PACK):
            head = tile * PACK + k
            line = sp[head // heads_here, head % heads_here : head % heads_here + 1, 0:LANES]
            line = jnp.broadcast_to(line, (8, LANES))
            shifted.append(
                jnp.concatenate(
                    [
                        shear(line, (SPAN * r - CENTRE) % LANES)[:, 0:TILE]
                        for r in range(8)
                    ],
                    axis=0,
                )
            )
        high, low = split_two(jnp.concatenate(shifted, axis=1))
        bias_whole[tile] = dot_nn(high, picks[0]) + dot_nn(low, picks[0])
        bias_local[tile] = dot_nn(high, picks[1]) + dot_nn(low, picks[1])

    for tile in range(tiles // 2):
        bias_of(tile)
    for place in later_y:
        forward_x(near_w.arrive_y(place))
        key_w.arrive_y(place)

    def core_half(index, slot, device_cols):
        ref = wa.at[slot, :, device_cols]
        return send(ref, ref, sem_bs.at[n_mp + index], sem_br.at[n_mp + index], to_core)

    key_w.arrive_y(0)
    core_near = core_half(0, near, my_cols)
    core_key = core_half(1, 1, my_cols)
    for place in later_z:
        fc1_w.arrive_z(place)
        forward_proj(proj_w.arrive_z(place))
        if place == 0:
            fc2_long.start_z()
            fc2_long.arrive_y()
            fc2_w.start_z()
    for tile in range(tiles // 2, tiles):
        bias_of(tile)
    for copy in along_x:
        copy.wait_recv()
    core_far = core_half(2, far, my_cols)
    gg_x.wait_recv()
    gg_c1 = send_rows(gg, 0, x_dl, to_core, 2)
    core_near.wait_recv()
    core_key.wait_recv()
    core_far.wait_recv()

    head_lane = iota((PACK * SLOTS, TILE), 1) >> 5
    head_mask = (iota((PACK * SLOTS, TILE), 0) >> 6) == head_lane
    key_place = iota((SLOTS, 1), 0)
    key_row, key_col = key_place >> 3, key_place & 7
    usable = []
    for w in range(windows):
        side = jnp.where(kinds[w] == 0, SIDE, LOCAL_SIDE)
        usable.append((key_row < side) & (key_col < side))

    def four(values):
        return jnp.where(head_mask, jnp.concatenate([values] * PACK, axis=0), 0.0).astype(BF)

    def fold(values):
        picked = jnp.where(head_mask, values, 0.0)
        total = picked[0:SLOTS]
        for k in range(1, PACK):
            total = total + picked[SLOTS * k : SLOTS * (k + 1)]
        return total

    def attend(tile, carry):
        cols = pl.ds(pl.multiple_of(tile * TILE, TILE), TILE)
        normed = h1p[...]
        q_tile = (dot_nt(normed, wa[0, cols, :]) + qb[0:1, cols]) * HEAD ** (-0.5)
        qs[tile] = q_tile.astype(BF)
        ks[tile] = dot_nt(normed, wa[1, cols, :]).astype(BF)
        vs[tile] = (dot_nt(normed, wa[2, cols, :]) + qb[1:2, cols]).astype(BF)
        for w in range(windows):
            part = pl.ds(SLOTS * w, SLOTS)
            scores = dot_nt(ks[tile, part, :], four(qs[tile, part, :].astype(F32)))
            bias = jnp.where(kinds[w] == 0, bias_whole[tile], bias_local[tile])
            scores = jnp.where(usable[w], scores + bias, NEG_FILL)
            raised = jnp.exp(scores - jnp.max(scores, axis=0, keepdims=True))
            probs = raised / jnp.sum(raised, axis=0, keepdims=True)
            pt[tile * windows + w] = probs
            at[tile, part, :] = fold(dot_tn(probs.astype(BF), vs[tile, part, :])).astype(BF)
        return carry

    third = tiles // 3
    lax.fori_loop(0, third, attend, 0)
    for place in range(z_count):
        forward_proj(proj_w.arrive_y(place))
    lax.fori_loop(third, 2 * third, attend, 0)
    for place in later_z:
        fc2_w.arrive_z(place)
        fc2_long.arrive_z(place)
    for copy in proj_x:
        copy.wait_recv()
    core_proj = core_half(3, 3, my_cols)
    lax.fori_loop(2 * third, tiles, attend, 0)
    core_proj.wait_recv()

    attn = jnp.concatenate(
        [dot_nn(gather, at[tile]).astype(BF) for tile in range(tiles)], axis=1
    )
    x1 = xs[...] + (dot_nn(attn, wa[3]) + flat_row(pb_ref)) * row_live
    x1s[...] = x1
    normed_two, scale_two = norm_parts(x1)
    hg[mine] = (normed_two * flat_row(n2g_ref) + flat_row(n2b_ref)).astype(BF)
    hg_x = send_rows(hg, 1, mine, to_x, 0)
    hg_c0 = send_rows(hg, 1, mine, to_core, 1)

    for place in range(z_count):
        fc1_w.arrive_y(place)
    for place in range(z_count):
        fc2_w.arrive_y(place)

    def slot_rows(slot):
        return pl.ds(pl.multiple_of(padded * slot, 16), padded)

    def mlp(slot):
        pre = dot_nt(hg[slot], wf[0]) + fb[0:1, :]
        square = pre * pre
        bend = jnp.tanh(GELU_A * (pre + GELU_B * (square * pre)))
        ac[slot_rows(slot), :] = (0.5 * pre * (1.0 + bend)).astype(BF)
        slope = 0.5 * (1.0 + bend) + 0.5 * pre * (1.0 - bend * bend) * (
            GELU_A * (1.0 + 3.0 * GELU_B * square)
        )
        dpre = (dot_nt(gg[slot], wf[1]) * slope).astype(BF)
        dp_s[slot_rows(slot), :] = dpre
        ph[slot] = dot_nn(dpre, wf[0]).astype(BF)

    mlp(mine)
    gg_c0.wait_recv()
    hg_c0.wait_recv()
    hg_x.wait_recv()
    hg_c1 = send_rows(hg, 1, x_dl, to_core, 2)
    mlp(core_dl)
    ph_c1 = send(ph.at[core_dl], rc_h.at[1], sem_hs.at[0, 1], sem_hr.at[0, 1], to_core)
    gg_c1.wait_recv()
    hg_c1.wait_recv()
    mlp(xc_dl)
    ph_c0 = send(ph.at[xc_dl], rc_h.at[0], sem_hs.at[0, 0], sem_hr.at[0, 0], to_core)
    mlp(x_dl)
    ph_c0.wait_recv()
    ph2[0] = (ph[x_dl].astype(F32) + rc_h[0].astype(F32)).astype(BF)
    ph_x = send(ph2.at[0], rx_h, sem_hs.at[0, 2], sem_hr.at[0, 2], to_x)

    tiles_half = tiles // 2
    z_half = z_count // 2
    along_y, along_z = {}, {}
    sums = {
        0: (ga.at[near], my_cols, ry_a.at[0], rz_a.at[0]),
        1: (ga.at[1], my_cols, ry_a.at[1], rz_a.at[1]),
        2: (ga.at[3], my_cols, ry_a.at[2], rz_a.at[2]),
        3: (gf.at[0], slice(None), ry_m.at[0], rz_m.at[0]),
        4: (gf.at[1], slice(None), ry_m.at[1], rz_m.at[1]),
    }

    def scatter_y(index, half):
        source, cols, landing, _ = sums[index]
        for other_z in range(half * z_half, (half + 1) * z_half):
            along_y[index, other_z] = send(
                source.at[rows_of(other_z, 1 - y), cols],
                landing.at[other_z],
                sem_ys.at[index, other_z],
                sem_yr.at[index, other_z],
                to_y,
            )

    def scatter_z(index):
        source, cols, landing, far_landing = sums[index]
        for other_z in range(z_count):
            along_y[index, other_z].wait_recv()
            landing[other_z] = (
                landing[other_z].astype(F32) + source[rows_of(other_z, y), cols].astype(F32)
            ).astype(BF)
        for step in range(1, z_count):
            along_z[index, step] = send(
                landing.at[z_at(step)],
                far_landing.at[step - 1],
                sem_zs.at[index, step - 1],
                sem_zr.at[index, step - 1],
                to_z(step),
            )

    def all_rows(ring):
        return ring[...].reshape(GROUP * padded, width)

    def fc1_grad(tile, carry):
        cols = pl.ds(pl.multiple_of(tile * TILE, TILE), TILE)
        gf[0, cols, :] = dot_tn(dp_s[:, cols], all_rows(hg)).astype(BF)
        return carry

    def fc2_grad(tile, carry):
        cols = pl.ds(pl.multiple_of(tile * TILE, TILE), TILE)
        gf[1, cols, :] = dot_tn(ac[:, cols], all_rows(gg)).astype(BF)
        return carry

    lax.fori_loop(0, tiles_half, fc2_grad, 0)
    scatter_y(4, 0)
    lax.fori_loop(tiles_half, tiles, fc2_grad, 0)
    scatter_y(4, 1)
    sg[pl.ds(8 + mine, 1), :] = jnp.sum(dp_s[...].astype(F32), axis=0, keepdims=True)

    ph_c1.wait_recv()
    ph_x.wait_recv()
    dh2 = ph[mine].astype(F32) + rc_h[1].astype(F32) + rx_h[...].astype(F32)
    sg[3:4, :] = jnp.sum(dh2 * normed_two, axis=0, keepdims=True)
    sg[4:5, :] = jnp.sum(dh2, axis=0, keepdims=True)
    dx1 = gs[...] + norm_back(dh2 * flat_row(n2g_ref), normed_two, scale_two)
    gs[...] = dx1
    gab = dx1 * row_live
    sg[2:3, :] = jnp.sum(gab, axis=0, keepdims=True)
    gab = gab.astype(BF)
    gabp[...] = dot_nn(spread, gab).astype(BF)

    dbias[...] = jnp.zeros_like(dbias)
    dh1[...] = jnp.zeros_like(dh1)

    def attend_back(tile, carry):
        cols = pl.ds(pl.multiple_of(tile * TILE, TILE), TILE)
        dattn = dot_nt(gabp[...], wa[3, cols, :])
        normed = h1p[...]
        total = jnp.zeros((SLOTS, LANES), F32)
        for w in range(windows):
            part = pl.ds(SLOTS * w, SLOTS)
            d_four = four(dattn[SLOTS * w : SLOTS * (w + 1)])
            q_four = four(qs[tile, part, :].astype(F32))
            probs = pt[tile * windows + w]
            dprob = dot_nt(vs[tile, part, :], d_four)
            weighed = probs * dprob
            ds = weighed - probs * jnp.sum(weighed, axis=0, keepdims=True)
            total = total + ds
            dsb = ds.astype(BF)
            dvs[tile, part, :] = dot_nn(probs.astype(BF), d_four).astype(BF)
            dks[tile, part, :] = dot_nn(dsb, q_four).astype(BF)
            dqs[tile, part, :] = (
                fold(dot_tn(dsb, ks[tile, part, :])) * HEAD ** (-0.5)
            ).astype(BF)
        dbias[tile] = total
        for s, grads in enumerate((dqs, dks, dvs)):
            ga[s, cols, :] = dot_tn(grads[tile], normed).astype(BF)
            dh1[...] += dot_nn(grads[tile], wa[s, cols, :])
        sg[6:7, cols] = jnp.sum(dqs[tile].astype(F32), axis=0, keepdims=True)
        sg[7:8, cols] = jnp.sum(dvs[tile].astype(F32), axis=0, keepdims=True)
        attn_tile = dot_nn(gather, at[tile]).astype(BF)
        ga[3, cols, :] = dot_tn(attn_tile, gab).astype(BF)
        return carry

    half_rows = width // 2
    halves = [pl.ds(0, half_rows), pl.ds(half_rows, half_rows)]
    core_copies, x_copies = [], []

    def reduce_core(half):
        core_copies.append(
            send(
                ga.at[:, halves[half], her_cols],
                rca.at[:, halves[half], :],
                sem_as.at[half, 0],
                sem_ar.at[half, 0],
                to_core,
            )
        )

    def add_core(slot, part):
        ga[slot, part, my_cols] = (
            ga[slot, part, my_cols].astype(F32) + rca[slot, part, :].astype(F32)
        ).astype(BF)

    def reduce_x(half):
        part = halves[half]
        core_copies[half].wait_recv()
        add_core(far, part)
        x_copies.append(
            send(
                ga.at[far, part, my_cols],
                rxa.at[part],
                sem_as.at[half, 1],
                sem_ar.at[half, 1],
                to_x,
            )
        )
        add_core(3, part)
        scatter_y(2, half)
        add_core(1, part)
        scatter_y(1, half)
        add_core(near, part)

    lax.fori_loop(0, tiles_half, attend_back, 0)
    reduce_core(0)
    lax.fori_loop(0, tiles, fc1_grad, 0)
    scatter_y(3, 0)
    scatter_y(3, 1)
    reduce_x(0)
    scatter_z(4)
    lax.fori_loop(tiles_half, tiles, attend_back, 0)
    reduce_core(1)

    def mlp_out(slot):
        ph[slot] = dot_nn(ac[slot_rows(slot), :], wf[1]).astype(BF)

    out_copies = []
    sent(ph_c0)
    sent(ph_c1)
    mlp_out(xc_dl)
    out_copies.append(send(ph.at[xc_dl], rc_o.at[0], sem_hs.at[1, 0], sem_hr.at[1, 0], to_core))
    mlp_out(core_dl)
    out_copies.append(send(ph.at[core_dl], rc_o.at[1], sem_hs.at[1, 1], sem_hr.at[1, 1], to_core))
    reduce_x(1)
    mlp_out(x_dl)
    out_copies[0].wait_recv()
    ph2[1] = (ph[x_dl].astype(F32) + rc_o[0].astype(F32)).astype(BF)
    out_copies.append(send(ph2.at[1], rx_o, sem_hs.at[1, 2], sem_hr.at[1, 2], to_x))
    mlp_out(mine)

    dh1c = dot_nn(gather, dh1[...].astype(BF))
    n1 = n1s[...]
    sg[0:1, :] = jnp.sum(dh1c * n1, axis=0, keepdims=True)
    sg[1:2, :] = jnp.sum(dh1c, axis=0, keepdims=True)
    dn = norm_back(dh1c * flat_row(n1g_ref), n1, stats[:, 0:1])
    tgrad_ref[...] = (gs[...] + dn).astype(BF)[0:rows]

    back = one_hot(
        iota((LANES, PACK * TILE), 1)
        == TILE * (iota((LANES, 1), 0) >> 6)
        + (TILE - 1 - table_place(iota((LANES, 1), 0) & 63, False)),
        BF,
    )
    for tile in range(tiles):
        high, low = split_two(dbias[tile])
        wide = dot_nn(high, back) + dot_nn(low, back)
        for k in range(PACK):
            head = tile * PACK + k
            line = jnp.zeros((8, LANES), F32)
            for r in range(8):
                piece = wide[8 * r : 8 * (r + 1), TILE * k : TILE * (k + 1)]
                piece = jnp.concatenate([piece, jnp.zeros_like(piece)], axis=1)
                shift = LANES - 1 - CENTRE - (TILE - 1) + SPAN * r
                line = line + shear(piece, shift)
            row, spot = 12 + head // heads_here, LANES * (head % heads_here)
            sg[row : row + 1, spot : spot + LANES] = jnp.sum(line, axis=0, keepdims=True)

    def small_start(stage, devices):
        return stage, [
            send(sg, sg_in.at[stage + k], sem_ss.at[stage + k], sem_sr.at[stage + k], device)
            for k, device in enumerate(devices)
        ]

    def small_end(started):
        stage, copies = started
        for copy in copies:
            copy.wait_recv()
            sent(copy)
        total = sg[...]
        for k in range(len(copies)):
            total = total + sg_in[stage + k]
        sg[...] = total

    smalls = small_start(0, [to_core])

    for half in range(2):
        x_copies[half].wait_recv()
        part = halves[half]
        ga[near, part, my_cols] = (
            ga[near, part, my_cols].astype(F32) + rxa[part, :].astype(F32)
        ).astype(BF)
        scatter_y(0, half)

    small_end(smalls)
    smalls = small_start(1, [to_x])

    out_copies[1].wait_recv()
    out_copies[2].wait_recv()
    branch = ph[mine].astype(F32) + rc_o[1].astype(F32) + rx_o[...].astype(F32)
    out_ref[...] = (x1s[...] + (branch + flat_row(f2b_ref)) * row_live).astype(BF)[0:rows]

    small_end(smalls)
    smalls = small_start(2, [to_y])

    scatter_z(2)
    scatter_z(3)
    small_end(smalls)
    smalls = small_start(3, [to_z(step) for step in range(1, z_count)])
    scatter_z(1)

    def total_z(index):
        landing, far_landing = sums[index][2:]
        total = landing[z].astype(F32)
        for step in range(1, z_count):
            along_z[index, step].wait_recv()
            total = total + far_landing[step - 1].astype(F32)
        return total.astype(BF)

    def swap(ref, dst, index, device):
        return send(ref, dst, sem_fs.at[index], sem_fr.at[index], device)

    def over_groups(ref, landing, index):
        for step in range(1, groups):
            k = index * (groups - 1) + step - 1
            copy = send(ref, landing.at[step - 1], sem_gs.at[k], sem_gr.at[k], to_group(step))
            copy.wait_recv()
            sent(copy)
        if groups > 1:
            total = ref[...].astype(F32)
            for step in range(1, groups):
                total = total + landing[step - 1].astype(F32)
            ref[...] = total.astype(BF)

    final = {}
    for k, index in enumerate((4, 3)):
        fin[1 - k, mine] = total_z(index)
        slot = fin.at[1 - k, mine]
        over_groups(slot, group_m.at[1 - k], k)
        final[index, 0] = swap(slot, slot, 3 * k, to_x)
        final[index, 1] = swap(slot, slot, 3 * k + 1, to_core)
    for k, (index, slot) in enumerate(((2, 3), (1, 1))):
        fin_a[slot, :, my_cols] = total_z(index)
        final[index, 0] = swap(fin_a.at[slot, :, my_cols], fin_x.at[k], 6 + k, to_x)
    scatter_z(0)
    for k, index in enumerate((4, 3)):
        final[index, 0].wait_recv()
        slot = fin.at[1 - k, x_dl]
        final[index, 2] = swap(slot, slot, 3 * k + 2, to_core)
    for index in (4, 3):
        final[index, 1].wait_recv()
        final[index, 2].wait_recv()
    fin_ref[1] = fin[0]
    fin_ref[2] = fin[1]
    for k, (index, slot) in enumerate(((2, 3), (1, 1))):
        final[index, 0].wait_recv()
        sent(final[index, 0])
        fin_a[slot, :, my_cols] = (
            fin_a[slot, :, my_cols].astype(F32) + fin_x[k].astype(F32)
        ).astype(BF)
        over_groups(fin_a.at[slot, :, my_cols], group_a.at[k], 2 + k)

    small_end(smalls)
    if groups > 1:
        small_end(small_start(2 + z_count, [to_group(step) for step in range(1, groups)]))

    vec_ref[...] = sg[0:8, :]
    pick = one_hot(iota((width, block), 0) == block * mp + iota((width, block), 1), F32)
    small_ref[0:8, 0:block] = dot_nn(sg[0:8, :], pick, HIGHEST)
    wide_lane = iota((width, hidden), 1)
    pick = one_hot(
        iota((width, hidden), 0)
        == block * mp + wide_lane - block * steps_of(wide_lane, block, hidden // block),
        F32,
    )
    lines = dot_nn(sg[8:16, :], pick, HIGHEST)
    keep = iota((8, hidden), 0) == steps_of(iota((8, hidden), 1), block, hidden // block)
    small_ref[8:9, :] = jnp.sum(jnp.where(keep, lines, 0.0), axis=0, keepdims=True)
    table = sg[pl.ds(12 + mp, 1), :]
    table = jnp.concatenate(
        [table[:, LANES * k : LANES * (k + 1)] for k in range(heads_here)]
        + [jnp.zeros((8 - heads_here, LANES), F32)],
        axis=0,
    )
    turn = one_hot(iota((LANES, LANES), 0) + iota((LANES, LANES), 1) == LANES - 1, F32)
    small_ref[16:24, 0:LANES] = dot_nn(table, turn, HIGHEST)

    fin_a[near, :, my_cols] = total_z(0)
    slot = fin_a.at[near, :, my_cols]
    over_groups(slot, group_a.at[2], 4)
    near_x = swap(slot, slot, 8, to_x)
    near_x.wait_recv()
    slots = fin_a.at[:, :, my_cols]
    swap(slots, slots, 9, to_core).wait_recv()
    fin_ref[0] = fin_a[...]

    for copy, when in pending:
        if when is None:
            copy.wait_send()
        else:
            pl.when(when)(copy.wait_send)


def unpack(
    out_in,
    tgrad_in,
    vec_in,
    small_in,
    fin_in,
    out_ref,
    tgrad_ref,
    n1g_ref,
    n1b_ref,
    qkvg_ref,
    qvg_ref,
    relg_ref,
    projg_ref,
    pbg_ref,
    n2g_ref,
    n2b_ref,
    f1g_ref,
    f1bg_ref,
    f2g_ref,
    f2bg_ref,
):
    hidden, width = f2g_ref.shape
    out_ref[...] = out_in[...]
    tgrad_ref[...] = tgrad_in[...]
    for k, ref in enumerate((n1g_ref, n1b_ref, pbg_ref, n2g_ref, n2b_ref, f2bg_ref)):
        ref[...] = vec_in[k : k + 1, :].reshape(width)
    for s in range(3):
        qkvg_ref[s] = fin_in[0, s].astype(F32)
    projg_ref[...] = fin_in[0, 3].astype(F32)
    f1g_ref[...] = fin_in[1].reshape(hidden, width).astype(F32).T
    f2g_ref[...] = fin_in[2].reshape(hidden, width).astype(F32)
    qvg_ref[...] = small_in[6:8, 0 : qvg_ref.shape[1]]
    f1bg_ref[...] = small_in[8:9, :].reshape(hidden)
    relg_ref[...] = small_in[16 : 16 + relg_ref.shape[0], 0:ENTRIES]


def solution(mesh):
    n_dp, n_mp = mesh.shape["dp"], mesh.shape["mp"]

    def shards(
        tokens,
        crop_kind,
        norm1_gain,
        norm1_bias,
        qkv_weight,
        qv_bias,
        rel_table,
        proj_weight,
        proj_bias,
        norm2_gain,
        norm2_bias,
        fc1_weight,
        fc1_bias,
        fc2_weight,
        fc2_bias,
        out_grad,
    ):
        rows, width = tokens.shape
        windows = rows // WIN
        padded = -(-rows // 16) * 16
        block = proj_weight.shape[0]
        hidden = fc2_weight.shape[0]
        heads_here = rel_table.shape[1]
        places = SLOTS * windows
        tiles = width // TILE
        z_count = n_mp // 2
        groups = n_dp // GROUP
        dims = (n_dp, n_mp, rows, windows, padded, width, block, hidden)

        def full(*shape):
            return jax.ShapeDtypeStruct(shape, F32)

        vmem = pl.BlockSpec(memory_space=pltpu.VMEM)
        dma = pltpu.SemaphoreType.DMA
        results = pl.pallas_call(
            functools.partial(body, dims),
            out_shape=[
                jax.ShapeDtypeStruct((rows, width), BF),
                jax.ShapeDtypeStruct((rows, width), BF),
                full(8, width),
                full(24, hidden),
                jax.ShapeDtypeStruct((3, GROUP, block, width), BF),
            ],
            in_specs=[pl.BlockSpec(memory_space=pltpu.SMEM)] + [vmem] * 15,
            out_specs=[vmem] * 5,
            scratch_shapes=[
                pltpu.VMEM((GROUP, width, width), BF),
                pltpu.VMEM((2, width, width), BF),
                pltpu.VMEM((hidden, width), BF),
                pltpu.VMEM((n_mp, 8, hidden), F32),
                pltpu.VMEM((8, hidden), F32),
                pltpu.VMEM((padded, width), F32),
                pltpu.VMEM((padded, width), F32),
                pltpu.VMEM((padded, width), F32),
                pltpu.VMEM((padded, width), F32),
                pltpu.VMEM((padded, TILE), F32),
                pltpu.VMEM((8, width), F32),
                pltpu.VMEM((8, width), F32),
                pltpu.VMEM((places, width), BF),
                pltpu.VMEM((tiles, places, TILE), BF),
                pltpu.VMEM((tiles, places, TILE), BF),
                pltpu.VMEM((tiles, places, TILE), BF),
                pltpu.VMEM((tiles, places, TILE), BF),
                pltpu.VMEM((tiles * windows, SLOTS, LANES), F32),
                pltpu.VMEM((tiles, SLOTS, LANES), F32),
                pltpu.VMEM((tiles, SLOTS, LANES), F32),
                pltpu.VMEM((GROUP, padded, width), BF),
                pltpu.VMEM((GROUP, padded, width), BF),
                pltpu.VMEM((GROUP * padded, width), BF),
                pltpu.VMEM((GROUP * padded, width), BF),
                pltpu.VMEM((GROUP, padded, width), BF),
                pltpu.VMEM((2, padded, width), BF),
                pltpu.VMEM((padded, width), BF),
                pltpu.VMEM((2, padded, width), BF),
                pltpu.VMEM((2, padded, width), BF),
                pltpu.VMEM((padded, width), BF),
                pltpu.VMEM((places, width), BF),
                pltpu.VMEM((tiles, places, TILE), BF),
                pltpu.VMEM((tiles, places, TILE), BF),
                pltpu.VMEM((tiles, places, TILE), BF),
                pltpu.VMEM((tiles, SLOTS, LANES), F32),
                pltpu.VMEM((places, width), F32),
                pltpu.VMEM((GROUP, width, width), BF),
                pltpu.VMEM((2, width, width), BF),
                pltpu.VMEM((GROUP, width, width // 2), BF),
                pltpu.VMEM((width, width // 2), BF),
                pltpu.VMEM((3, z_count, block, width // 2), BF),
                pltpu.VMEM((3, z_count - 1, block, width // 2), BF),
                pltpu.VMEM((2, z_count, block, width), BF),
                pltpu.VMEM((2, z_count - 1, block, width), BF),
                pltpu.VMEM((2, GROUP, block, width), BF),
                pltpu.VMEM((GROUP, block, width), BF),
                pltpu.VMEM((2, block, width // 2), BF),
                pltpu.VMEM((2, max(groups - 1, 1), block, width), BF),
                pltpu.VMEM((3, max(groups - 1, 1), block, width // 2), BF),
                pltpu.VMEM((24, width), F32),
                pltpu.VMEM((2 + z_count + groups, 24, width), F32),
                dma((7, 2 * z_count + 1)),
                dma((7, 2 * z_count + 1)),
                dma((2 * n_mp + 4,)),
                dma((2 * n_mp + 4,)),
                dma((2, 3)),
                dma((2, 3)),
                dma((2, 3)),
                dma((2, 3)),
                dma((2, 2)),
                dma((2, 2)),
                dma((5, z_count)),
                dma((5, z_count)),
                dma((5, z_count)),
                dma((5, z_count)),
                dma((10,)),
                dma((10,)),
                dma((2 + z_count + groups,)),
                dma((2 + z_count + groups,)),
                dma((5 * max(groups - 1, 1),)),
                dma((5 * max(groups - 1, 1),)),
            ],
            compiler_params=pltpu.CompilerParams(
                collective_id=0, has_side_effects=True, vmem_limit_bytes=63 * 2**20
            ),
        )(
            crop_kind,
            tokens,
            out_grad,
            norm1_gain,
            norm1_bias,
            jnp.swapaxes(qkv_weight, 1, 2),
            qv_bias,
            rel_table.T,
            proj_weight,
            proj_bias,
            norm2_gain,
            norm2_bias,
            fc1_weight,
            fc1_bias,
            fc2_weight,
            fc2_bias,
        )
        results = pl.pallas_call(
            unpack,
            out_shape=[
                jax.ShapeDtypeStruct((rows, width), BF),
                jax.ShapeDtypeStruct((rows, width), BF),
                full(width),
                full(width),
                full(3, block, width),
                full(2, block),
                full(heads_here, ENTRIES),
                full(block, width),
                full(width),
                full(width),
                full(width),
                full(width, hidden),
                full(hidden),
                full(hidden, width),
                full(width),
            ],
            in_specs=[vmem] * 5,
            out_specs=[vmem] * 15,
        )(*results)
        results = list(results)
        results[4] = jnp.swapaxes(results[4], 1, 2)
        results[6] = results[6].T
        return tuple(results)

    in_specs = (
        P(("dp", "mp"), None),
        P("dp"),
        P(),
        P(),
        P(None, None, "mp"),
        P(None, "mp"),
        P(None, "mp"),
        P("mp", None),
        P(),
        P(),
        P(),
        P(None, "mp"),
        P("mp"),
        P("mp", None),
        P(),
        P(("dp", "mp"), None),
    )
    out_specs = (
        P(("dp", "mp"), None),
        P(("dp", "mp"), None),
        P(),
        P(),
        P(None, None, "mp"),
        P(None, "mp"),
        P(None, "mp"),
        P("mp", None),
        P(),
        P(),
        P(),
        P(None, "mp"),
        P("mp"),
        P("mp", None),
        P(),
    )
    return jax.shard_map(shards, mesh=mesh, in_specs=in_specs, out_specs=out_specs, check_vma=False)
```

```python
import functools

import jax
import jax.numpy as jnp
from jax import lax
from jax.experimental import pallas as pl
from jax.experimental.pallas import tpu as pltpu
from jax.sharding import PartitionSpec as P

HEAD = 32
SIDE = 7
LOCAL_SIDE = 3
WIN = 49
SPAN = 2 * SIDE - 1
ENTRIES = SPAN * SPAN
CENTRE = (SIDE - 1) * SPAN + SIDE - 1
SLOTS = 64
TILE = 128
PACK = 4
GROUP = 4
LANES = 256
EPSILON = 1e-05
NEG_FILL = -1000000000.0
GELU_A = 0.7978845608028654
GELU_B = 0.044715
HIGHEST = lax.Precision.HIGHEST
MESH = pl.DeviceIdType.MESH
BF = jnp.bfloat16
F32 = jnp.float32


def dot(left, right, dims, precision=None):
    return lax.dot_general(
        left, right, (dims, ((), ())), preferred_element_type=F32, precision=precision
    )


def dot_nn(left, right, precision=None):
    return dot(left, right, ((1,), (0,)), precision)


def dot_nt(left, right, precision=None):
    return dot(left, right, ((1,), (1,)), precision)


def dot_tn(left, right, precision=None):
    return dot(left, right, ((0,), (0,)), precision)


def iota(shape, axis):
    return lax.broadcasted_iota(jnp.int32, shape, axis)


def one_hot(cond, dtype):
    return jnp.where(cond, 1.0, 0.0).astype(dtype)


def steps_of(values, width, count):
    total = jnp.zeros_like(values)
    for step in range(1, count):
        total = total + jnp.where(values >= step * width, 1, 0)
    return total


def shear(values, shift):
    moved = pltpu.roll(values, shift, axis=1)
    return pltpu.roll(moved, 0, axis=1, stride=1, stride_axis=0)


def split_two(values):
    high = values.astype(BF)
    return high, (values - high.astype(F32)).astype(BF)


def flat_row(ref):
    return ref[...].reshape(1, -1)


def norm_parts(values):
    mean = jnp.mean(values, axis=-1, keepdims=True)
    centre = values - mean
    spread = jnp.mean(centre * centre, axis=-1, keepdims=True)
    scale = lax.rsqrt(spread + EPSILON)
    return centre * scale, scale


def norm_back(grad_normed, normed, scale):
    return scale * (
        grad_normed
        - jnp.mean(grad_normed, axis=-1, keepdims=True)
        - normed * jnp.mean(grad_normed * normed, axis=-1, keepdims=True)
    )


def slot_place(columns, windows, kinds):
    window = steps_of(columns, WIN, windows)
    slot = columns - WIN * window
    kind = jnp.zeros_like(columns)
    for w in range(windows):
        kind = jnp.where(window == w, kinds[w], kind)
    whole = slot + steps_of(slot, SIDE, SIDE)
    corner = slot + (8 - LOCAL_SIDE) * steps_of(slot, LOCAL_SIDE, LOCAL_SIDE)
    rest = slot + (8 * LOCAL_SIDE - LOCAL_SIDE * LOCAL_SIDE)
    local = jnp.where(slot < LOCAL_SIDE * LOCAL_SIDE, corner, rest)
    place = SLOTS * window + jnp.where(kind == 0, whole, local)
    live = jnp.where(kind == 0, WIN, LOCAL_SIDE * LOCAL_SIDE)
    inside = columns < WIN * windows
    return jnp.where(inside, place, -1), inside & (slot < live)


def body(
    dims,
    kind_ref,
    tok_ref,
    og_ref,
    n1g_ref,
    n1b_ref,
    qkvw_ref,
    qvb_ref,
    tab_ref,
    pw_ref,
    pb_ref,
    n2g_ref,
    n2b_ref,
    f1w_ref,
    f1b_ref,
    f2w_ref,
    f2b_ref,
    out_ref,
    tgrad_ref,
    vec_ref,
    small_ref,
    fin_ref,
    wa,
    wf,
    ft,
    sp,
    pk,
    xs,
    x1s,
    n1s,
    gs,
    stats,
    qb,
    fb,
    h1p,
    qs,
    ks,
    vs,
    at,
    pt,
    bias_whole,
    bias_local,
    hg,
    gg,
    ac,
    dp_s,
    ph,
    rc_h,
    rx_h,
    ph2,
    rc_o,
    rx_o,
    gabp,
    dqs,
    dks,
    dvs,
    dbias,
    dh1,
    ga,
    gf,
    rca,
    rxa,
    ry,
    rz,
    rr,
    fin,
    fin_a,
    fin_x,
    group_m,
    group_a,
    sg,
    sg_in,
    sem_ws,
    sem_wr,
    sem_bs,
    sem_br,
    sem_rs,
    sem_rr,
    sem_hs,
    sem_hr,
    sem_as,
    sem_ar,
    sem_ys,
    sem_yr,
    sem_zs,
    sem_zr,
    sem_fs,
    sem_fr,
    sem_ss,
    sem_sr,
    sem_gs,
    sem_gr,
):
    n_dp, n_mp, rows, windows, padded, width, block, hidden = dims
    groups = n_dp // GROUP
    places = SLOTS * windows
    z_count = n_mp // 2
    heads_here = block // HEAD
    tiles = width // TILE
    half_width = width // 2
    mp = lax.axis_index("mp")
    dp = lax.axis_index("dp")
    z = mp // 2
    y = mp % 2
    base = (dp // GROUP) * GROUP
    mine = dp % GROUP
    x = mine // 2
    c = mine % 2
    core_dl = x * 2 + (1 - c)
    x_dl = (1 - x) * 2 + c
    xc_dl = (1 - x) * 2 + (1 - c)
    to_core = (base + core_dl, mp)
    to_x = (base + x_dl, mp)
    to_y = (dp, z * 2 + (1 - y))
    near = 2 * x
    far = 2 - 2 * x

    def z_at(step):
        return (z + step) % z_count

    def to_z(step):
        return (dp, z_at(step) * 2 + y)

    def to_group(step):
        return ((dp + GROUP * step) % n_dp, mp)

    pending = []

    def remote(src, dst, s_sem, r_sem, device):
        return pltpu.make_async_remote_copy(
            src_ref=src,
            dst_ref=dst,
            send_sem=s_sem,
            recv_sem=r_sem,
            device_id=device,
            device_id_type=MESH,
        )

    def send(src, dst, s_sem, r_sem, device, when=None):
        copy = remote(src, dst, s_sem, r_sem, device)
        if when is None:
            copy.start()
        else:
            pl.when(when)(copy.start)
        pending.append((copy, when))
        return copy

    def forget(copy):
        pending[:] = [other for other in pending if other[0] is not copy]

    def sent(copy):
        copy.wait_send()
        forget(copy)

    barrier = pltpu.get_barrier_semaphore()
    peers = [to_core, to_x, to_y]
    peers += [to_z(step) for step in range(1, z_count)]
    peers += [to_group(step) for step in range(1, groups)]
    for peer in peers:
        pl.semaphore_signal(barrier, inc=1, device_id=peer, device_id_type=MESH)

    own = pl.ds(pl.multiple_of(block * mp, 16), block)
    my_cols = pl.ds(pl.multiple_of(half_width * c, TILE), half_width)
    her_cols = pl.ds(pl.multiple_of(half_width * (1 - c), TILE), half_width)
    for s in range(3):
        wa[s, own, my_cols] = qkvw_ref[s, :, my_cols]
    wa[3, own, my_cols] = pw_ref[:, my_cols]

    pk[...] = jnp.zeros_like(pk)
    pk[0:heads_here, 0:ENTRIES] = tab_ref[...]
    pk[3:5, 0:block] = qvb_ref[...]
    pk[5:6, :] = flat_row(f1b_ref)
    sp[mp] = pk[...]

    pl.semaphore_wait(barrier, len(peers))

    def rows_of(other_z, other_y):
        return pl.ds(pl.multiple_of(block * (other_z * 2 + other_y), 16), block)

    relayed = z_count == 4
    if relayed:
        order = [2, jnp.where(z == 0, 3, 1), jnp.where(z == 0, 1, 3)]
    else:
        order = list(range(1, z_count))
    inner = (z == 1) | (z == 2)

    def spread_z(buffer, part, index, first):
        ref = buffer.at[part]
        for step in range(1, z_count):
            far_end = {1: z != 3, 2: None, 3: z != 0}[step] if relayed else None
            k = first + step - 1
            send(ref, ref, sem_ws.at[index, k], sem_wr.at[index, k], to_z(step), far_end)

    def arrived_z(buffer, part_of, index, first, place):
        step = order[place]
        part = part_of((z + z_count - step) % z_count)
        ref = buffer.at[part]
        k = first + step - 1
        remote(ref, ref, sem_ws.at[index, k], sem_wr.at[index, k], to_y).wait_recv()
        if relayed and place == 0:
            last = 2 * (z - 1)
            send(
                ref,
                ref,
                sem_ws.at[index, first + 3],
                sem_wr.at[index, first + last],
                (dp, 3 * (z - 1) * 2 + y),
                inner,
            )
        return part

    class Gather:
        def __init__(self, index, buffer, part):
            self.index, self.buffer, self.part = index, buffer, part

        def forward_y(self, part, step):
            k = z_count + step
            ref = self.buffer.at[part]
            send(ref, ref, sem_ws.at[self.index, k], sem_wr.at[self.index, k], to_y)

        def start_y(self):
            self.forward_y(self.part(z, y), 0)

        def start_z(self):
            spread_z(self.buffer, self.part(z, y), self.index, 0)

        def arrive_z(self, place):
            part = arrived_z(self.buffer, lambda oz: self.part(oz, y), self.index, 0, place)
            self.forward_y(part, order[place])
            return part

        def arrive_y(self, place):
            step = 0 if place == 0 else order[place - 1]
            part = self.part((z + z_count - step) % z_count, 1 - y)
            ref = self.buffer.at[part]
            k = z_count + step
            remote(ref, ref, sem_ws.at[self.index, k], sem_wr.at[self.index, k], to_y).wait_recv()
            return part

    class GatherLong:
        def __init__(self, index, buffer, part):
            self.index, self.buffer, self.part = index, buffer, part

        def pair(self):
            ref = self.buffer.at[self.part(z, y)]
            k = 2 * z_count
            return ref, ref, sem_ws.at[self.index, k], sem_wr.at[self.index, k], to_y

        def start_y(self):
            send(*self.pair())

        def start_z(self):
            spread_z(self.buffer, self.part(z, y), self.index, 0)

        def arrive_y(self):
            remote(*self.pair()).wait_recv()
            spread_z(self.buffer, self.part(z, 1 - y), self.index, z_count)

        def arrive_z(self, place):
            for column in range(2):
                other_y = y if column == 0 else 1 - y
                arrived_z(
                    self.buffer,
                    lambda oz: self.part(oz, other_y),
                    self.index,
                    z_count * column,
                    place,
                )

    def half_block(other_z, other_y):
        return rows_of(other_z, other_y), my_cols

    def whole_block(other_z, other_y):
        return (rows_of(other_z, other_y),)

    def quarter_block(other_z, other_y):
        start = block * (other_z * 2 + other_y) + (block // 2) * x
        return pl.ds(pl.multiple_of(start, 16), block // 2), my_cols

    def left_block(other_z, other_y):
        return rows_of(other_z, other_y), pl.ds(0, half_width)

    def right_block(other_z, other_y):
        return rows_of(other_z, other_y), pl.ds(half_width, half_width)

    small = Gather(0, sp, lambda oz, oy: (oz * 2 + oy,))
    near_w = Gather(1, wa.at[near], half_block)
    key_w = Gather(2, wa.at[1], half_block)
    proj_w = Gather(3, wa.at[3], quarter_block)
    fc1_w = Gather(4, wf.at[0], whole_block)
    fc2_w = Gather(5, wf.at[1], left_block)
    fc2_long = GatherLong(6, wf.at[1], right_block)
    later_z, later_y = range(z_count - 1), range(1, z_count)

    for part in (near_w, key_w, proj_w, small):
        part.start_z()
        part.start_y()
    ft[...] = f1w_ref[...].T
    quarter = pl.ds(pl.multiple_of(block * mine, 16), block)
    wf[0, own, :] = ft[quarter, :]
    wf[1, own, :] = f2w_ref[quarter, :]

    def send_rows(ring, index, slot, device, k):
        return send(ring.at[slot], ring.at[slot], sem_rs.at[index, k], sem_rr.at[index, k], device)

    kinds = [kind_ref[mp * windows + w] for w in range(windows)]
    place_row, _ = slot_place(iota((1, padded), 1), windows, kinds)
    place_col, live_col = slot_place(iota((padded, 1), 0), windows, kinds)
    spread = one_hot(iota((places, padded), 0) == place_row, BF)
    gather = one_hot(iota((padded, places), 1) == place_col, BF)
    row_live = jnp.where(live_col, 1.0, 0.0)

    gs[...] = jnp.zeros_like(gs)
    gs[0:rows, :] = og_ref[...].astype(F32)
    sg[...] = jnp.zeros_like(sg)
    masked = gs[...] * row_live
    gg[mine] = masked.astype(BF)
    gg_c0 = send_rows(gg, 0, mine, to_core, 1)
    sg[5:6, :] = jnp.sum(masked, axis=0, keepdims=True)

    xs[...] = jnp.zeros_like(xs)
    xs[0:rows, :] = tok_ref[...].astype(F32)
    normed_one, scale_one = norm_parts(xs[...])
    n1s[...] = normed_one
    stats[:, 0:1] = scale_one
    h1 = (normed_one * flat_row(n1g_ref) + flat_row(n1b_ref)).astype(BF)
    h1p[...] = dot_nn(spread, h1).astype(BF)

    along_x, proj_x = [], []

    def forward_x(part):
        k = len(along_x)
        ref = wa.at[near].at[part]
        along_x.append(send(ref, ref, sem_bs.at[k], sem_br.at[k], to_x))

    def forward_proj(part):
        k = n_mp + 4 + len(proj_x)
        ref = wa.at[3].at[part]
        proj_x.append(send(ref, ref, sem_bs.at[k], sem_br.at[k], to_x))

    forward_x(near_w.arrive_y(0))

    def core_half(index, slot):
        ref = wa.at[slot, :, my_cols]
        return send(ref, ref, sem_bs.at[n_mp + index], sem_br.at[n_mp + index], to_core)

    forward_x(near_w.arrive_z(0))
    fc1_w.start_z()
    for place in later_z[1:]:
        forward_x(near_w.arrive_z(place))
    for place in later_z:
        key_w.arrive_z(place)
        forward_proj(proj_w.arrive_z(place))
    for part in (fc1_w, fc2_w, fc2_long):
        part.start_y()
    for place in later_z:
        small.arrive_z(place)
    for place in later_y:
        forward_x(near_w.arrive_y(place))
    fc1_w.arrive_z(0)
    fc2_w.start_z()
    for place in range(z_count):
        forward_proj(proj_w.arrive_y(place))
    gg_x = send_rows(gg, 0, mine, to_x, 0)
    for place in later_z[1:]:
        fc1_w.arrive_z(place)
    fc2_long.arrive_y()
    fc2_long.start_z()
    for place in range(z_count):
        key_w.arrive_y(place)
    core_near = core_half(0, near)
    core_key = core_half(1, 1)
    for place in range(z_count):
        small.arrive_y(place)
    lane = iota((1, width), 1)
    owner = steps_of(lane, block, n_mp)
    within = lane - block * owner
    pick_row = iota((n_mp, width), 0) == owner
    spots = iota((hidden, width), 0)

    def spread_row(row, offset):
        picked = dot_nn(sp[:, row, :], one_hot(spots == within + offset, F32), HIGHEST)
        return jnp.sum(jnp.where(pick_row, picked, 0.0), axis=0, keepdims=True)

    qb[0:1, :] = spread_row(3, 0)
    qb[1:2, :] = spread_row(4, 0)
    fb[0:1, :] = spread_row(5, block * mine)

    def table_place(cells, local):
        row, column = cells >> 3, cells & 7
        spot = SPAN * row + column
        if local:
            last = LOCAL_SIDE - 1
            dead = (row > last) | (column > last)
            spot = jnp.where(dead, SPAN * last + last, spot)
        return spot

    cell = iota((1, LANES), 1)
    cell_head, cell_spot = cell >> 6, cell & 63
    source = iota((PACK * TILE, LANES), 0)
    picks = []
    for local in (False, True):
        picks.append(one_hot(source == TILE * cell_head + table_place(cell_spot, local), BF))

    def bias_of(tile):
        shifted = []
        for k in range(PACK):
            head = tile * PACK + k
            line = sp[head // heads_here, head % heads_here : head % heads_here + 1, 0:LANES]
            line = jnp.broadcast_to(line, (8, LANES))
            shifted.append(
                jnp.concatenate(
                    [
                        shear(line, (SPAN * r - CENTRE) % LANES)[:, 0:TILE]
                        for r in range(8)
                    ],
                    axis=0,
                )
            )
        high, low = split_two(jnp.concatenate(shifted, axis=1))
        bias_whole[tile] = dot_nn(high, picks[0]) + dot_nn(low, picks[0])
        bias_local[tile] = dot_nn(high, picks[1]) + dot_nn(low, picks[1])

    for tile in range(tiles):
        bias_of(tile)
    for copy in along_x:
        copy.wait_recv()
    core_far = core_half(2, far)
    core_near.wait_recv()
    core_key.wait_recv()
    core_far.wait_recv()

    head_lane = iota((PACK * SLOTS, TILE), 1) >> 5
    head_mask = (iota((PACK * SLOTS, TILE), 0) >> 6) == head_lane
    key_place = iota((SLOTS, 1), 0)
    key_row, key_col = key_place >> 3, key_place & 7
    usable = []
    for w in range(windows):
        side = jnp.where(kinds[w] == 0, SIDE, LOCAL_SIDE)
        usable.append((key_row < side) & (key_col < side))

    def four(values):
        return jnp.where(head_mask, jnp.concatenate([values] * PACK, axis=0), 0.0).astype(BF)

    def fold(values):
        picked = jnp.where(head_mask, values, 0.0)
        total = picked[0:SLOTS]
        for k in range(1, PACK):
            total = total + picked[SLOTS * k : SLOTS * (k + 1)]
        return total

    def attend(tile, carry):
        cols = pl.ds(pl.multiple_of(tile * TILE, TILE), TILE)
        normed = h1p[...]
        q_tile = (dot_nt(normed, wa[0, cols, :]) + qb[0:1, cols]) * HEAD ** (-0.5)
        qs[tile] = q_tile.astype(BF)
        ks[tile] = dot_nt(normed, wa[1, cols, :]).astype(BF)
        vs[tile] = (dot_nt(normed, wa[2, cols, :]) + qb[1:2, cols]).astype(BF)
        for w in range(windows):
            part = pl.ds(SLOTS * w, SLOTS)
            scores = dot_nt(ks[tile, part, :], four(qs[tile, part, :].astype(F32)))
            bias = jnp.where(kinds[w] == 0, bias_whole[tile], bias_local[tile])
            scores = jnp.where(usable[w], scores + bias, NEG_FILL)
            raised = jnp.exp(scores - jnp.max(scores, axis=0, keepdims=True))
            probs = raised / jnp.sum(raised, axis=0, keepdims=True)
            pt[tile * windows + w] = probs
            at[tile, part, :] = fold(dot_tn(probs.astype(BF), vs[tile, part, :])).astype(BF)
        return carry

    third = tiles // 3
    lax.fori_loop(0, third, attend, 0)
    for place in later_z:
        fc2_w.arrive_z(place)
    gg_x.wait_recv()
    gg_c1 = send_rows(gg, 0, x_dl, to_core, 2)
    lax.fori_loop(third, 2 * third, attend, 0)
    for copy in proj_x:
        copy.wait_recv()
    core_proj = core_half(3, 3)
    lax.fori_loop(2 * third, tiles, attend, 0)
    core_proj.wait_recv()

    attn = jnp.concatenate(
        [dot_nn(gather, at[tile]).astype(BF) for tile in range(tiles)], axis=1
    )
    x1 = xs[...] + (dot_nn(attn, wa[3]) + flat_row(pb_ref)) * row_live
    x1s[...] = x1
    normed_two, scale_two = norm_parts(x1)
    hg[mine] = (normed_two * flat_row(n2g_ref) + flat_row(n2b_ref)).astype(BF)
    hg_x = send_rows(hg, 1, mine, to_x, 0)
    hg_c0 = send_rows(hg, 1, mine, to_core, 1)

    for place in later_z:
        fc2_long.arrive_z(place)
    for place in range(z_count):
        fc1_w.arrive_y(place)
    for place in range(z_count):
        fc2_w.arrive_y(place)

    def slot_rows(slot):
        return pl.ds(pl.multiple_of(padded * slot, 16), padded)

    def mlp(slot):
        pre = dot_nt(hg[slot], wf[0]) + fb[0:1, :]
        square = pre * pre
        bend = jnp.tanh(GELU_A * (pre + GELU_B * (square * pre)))
        ac[slot_rows(slot), :] = (0.5 * pre * (1.0 + bend)).astype(BF)
        slope = 0.5 * (1.0 + bend) + 0.5 * pre * (1.0 - bend * bend) * (
            GELU_A * (1.0 + 3.0 * GELU_B * square)
        )
        dpre = (dot_nt(gg[slot], wf[1]) * slope).astype(BF)
        dp_s[slot_rows(slot), :] = dpre
        ph[slot] = dot_nn(dpre, wf[0]).astype(BF)

    mlp(mine)
    gg_c0.wait_recv()
    hg_c0.wait_recv()
    hg_x.wait_recv()
    hg_c1 = send_rows(hg, 1, x_dl, to_core, 2)
    mlp(core_dl)
    ph_c1 = send(ph.at[core_dl], rc_h.at[1], sem_hs.at[0, 1], sem_hr.at[0, 1], to_core)
    gg_c1.wait_recv()
    hg_c1.wait_recv()
    mlp(xc_dl)
    ph_c0 = send(ph.at[xc_dl], rc_h.at[0], sem_hs.at[0, 0], sem_hr.at[0, 0], to_core)
    mlp(x_dl)
    ph_c0.wait_recv()
    ph2[0] = (ph[x_dl].astype(F32) + rc_h[0].astype(F32)).astype(BF)
    ph_x = send(ph2.at[0], rx_h, sem_hs.at[0, 2], sem_hr.at[0, 2], to_x)

    tiles_half = tiles // 2
    z_half = z_count // 2

    def add_to(ref, *others):
        total = ref[...].astype(F32)
        for other in others:
            total = total + other[...].astype(F32)
        ref[...] = total.astype(BF)

    class Line:
        def __init__(self, index, part, relay):
            self.index, self.part = index, part
            self.relay = relay and relayed

        def recv(self, step):
            return rz.at[self.index, step - 1]

        def sems(self, k, r):
            return sem_zs.at[self.index, k], sem_zr.at[self.index, r]

        def over(self):
            return remote(
                self.part(z_count - 1 - z),
                rr.at[self.index],
                *self.sems(3, 3),
                (dp, (1 + z // 3) * 2 + y),
            )

        def far(self):
            return remote(self.part(z_at(2)), self.recv(2), *self.sems(1, 1), to_z(2))

        def start(self):
            if not self.relay:
                for step in range(1, z_count):
                    send(
                        self.part(z_at(step)),
                        self.recv(step),
                        *self.sems(step - 1, step - 1),
                        to_z(step),
                    )
                return
            outer = jnp.logical_not(inner)
            copy = self.over()
            pl.when(outer)(copy.start)
            pending.append((copy, outer))
            for step, when in ((1, z != 3), (3, z != 0)):
                send(
                    self.part(z_at(step)),
                    self.recv(step),
                    *self.sems(step - 1, step - 1),
                    to_z(step),
                    when,
                )
            pl.when(outer)(self.far().start)

        def middle(self):
            if self.relay:

                @pl.when(inner)
                def _():
                    self.over().wait_recv()
                    add_to(self.part(z_at(2)), rr.at[self.index])
                    self.far().start()

                pending.append((self.far(), None))

        def total(self):
            whens = [z != 0, None, z != z_count - 1] if self.relay else [None] * (z_count - 1)
            ref = self.part(z)
            for step in range(1, z_count):
                copy = remote(ref, self.recv(step), *self.sems(step - 1, step - 1), to_y)

                def take(copy=copy, step=step):
                    copy.wait_recv()
                    add_to(ref, self.recv(step))

                if whens[step - 1] is None:
                    take()
                else:
                    pl.when(whens[step - 1])(take)
            return ref

    class YFirst:
        def __init__(self, index, source, cols, relay):
            self.index, self.source, self.cols = index, source, cols
            self.line = Line(index, lambda oz: ry.at[index, oz], relay)
            self.along_y = {}

        def scatter(self, half):
            for oz in range(half * z_half, (half + 1) * z_half):
                self.along_y[oz] = send(
                    self.source.at[rows_of(oz, 1 - y), self.cols],
                    ry.at[self.index, oz],
                    sem_ys.at[self.index, oz],
                    sem_yr.at[self.index, oz],
                    to_y,
                )

        def start_z(self):
            for oz in range(z_count):
                self.along_y[oz].wait_recv()
                add_to(ry.at[self.index, oz], self.source.at[rows_of(oz, y), self.cols])
            self.line.start()

        def middle(self):
            self.line.middle()

        def total(self):
            return self.line.total()

    class ZFirst:
        def __init__(self, index, source, cols):
            self.index = index
            self.lines = [
                Line(index + k, lambda oz, oy=oy: source.at[rows_of(oz, oy), cols], True)
                for k, oy in enumerate((1 - y, y))
            ]

        def start_z(self):
            for line in self.lines:
                line.start()

        def middle(self):
            for line in self.lines:
                line.middle()

        def start_y(self):
            self.copy = send(
                self.lines[0].total(),
                ry.at[self.index, 0],
                sem_ys.at[self.index, 0],
                sem_yr.at[self.index, 0],
                to_y,
            )

        def total(self):
            ref = self.lines[1].total()
            self.copy.wait_recv()
            add_to(ref, ry.at[self.index, 0])
            return ref

    left_cols, right_cols = pl.ds(0, half_width), pl.ds(half_width, half_width)
    sum_near = YFirst(0, ga.at[near], my_cols, False)
    sum_key = YFirst(1, ga.at[1], my_cols, True)
    sum_proj = YFirst(2, ga.at[3], my_cols, True)
    sum_fc1 = [YFirst(3, gf.at[0], left_cols, True), YFirst(4, gf.at[0], right_cols, True)]
    sum_fc2 = [YFirst(5, gf.at[1], left_cols, True), ZFirst(6, gf.at[1], right_cols)]

    def all_rows(ring):
        return ring[...].reshape(GROUP * padded, width)

    def fc1_grad(tile, carry):
        cols = pl.ds(pl.multiple_of(tile * TILE, TILE), TILE)
        gf[0, cols, :] = dot_tn(dp_s[:, cols], all_rows(hg)).astype(BF)
        return carry

    def fc2_grad(tile, carry):
        cols = pl.ds(pl.multiple_of(tile * TILE, TILE), TILE)
        gf[1, cols, :] = dot_tn(ac[:, cols], all_rows(gg)).astype(BF)
        return carry

    lax.fori_loop(0, tiles_half, fc2_grad, 0)
    sum_fc2[0].scatter(0)
    lax.fori_loop(tiles_half, tiles, fc2_grad, 0)
    sum_fc2[1].start_z()
    sum_fc2[0].scatter(1)
    lax.fori_loop(0, tiles_half, fc1_grad, 0)
    for part in sum_fc1:
        part.scatter(0)
    lax.fori_loop(tiles_half, tiles, fc1_grad, 0)
    for part in sum_fc1:
        part.scatter(1)
    sg[pl.ds(8 + mine, 1), :] = jnp.sum(dp_s[...].astype(F32), axis=0, keepdims=True)

    ph_c1.wait_recv()
    ph_x.wait_recv()
    dh2 = ph[mine].astype(F32) + rc_h[1].astype(F32) + rx_h[...].astype(F32)
    sg[3:4, :] = jnp.sum(dh2 * normed_two, axis=0, keepdims=True)
    sg[4:5, :] = jnp.sum(dh2, axis=0, keepdims=True)
    dx1 = gs[...] + norm_back(dh2 * flat_row(n2g_ref), normed_two, scale_two)
    gs[...] = dx1
    gab = dx1 * row_live
    sg[2:3, :] = jnp.sum(gab, axis=0, keepdims=True)
    gab = gab.astype(BF)
    gabp[...] = dot_nn(spread, gab).astype(BF)
    for tile in range(tiles):
        ga[3, TILE * tile : TILE * (tile + 1), :] = dot_tn(
            attn[:, TILE * tile : TILE * (tile + 1)], gab
        ).astype(BF)

    core_copies, x_copies = [], []

    def to_core_sum(source, landing, k):
        core_copies.append(send(source, landing, sem_as.at[k, 0], sem_ar.at[k, 0], to_core))

    to_core_sum(ga.at[3, :, her_cols], rca.at[3], 2)
    sum_fc2[1].middle()

    dbias[...] = jnp.zeros_like(dbias)
    dh1[...] = jnp.zeros_like(dh1)

    def attend_back(tile, carry):
        cols = pl.ds(pl.multiple_of(tile * TILE, TILE), TILE)
        dattn = dot_nt(gabp[...], wa[3, cols, :])
        normed = h1p[...]
        total = jnp.zeros((SLOTS, LANES), F32)
        for w in range(windows):
            part = pl.ds(SLOTS * w, SLOTS)
            d_four = four(dattn[SLOTS * w : SLOTS * (w + 1)])
            q_four = four(qs[tile, part, :].astype(F32))
            probs = pt[tile * windows + w]
            dprob = dot_nt(vs[tile, part, :], d_four)
            weighed = probs * dprob
            ds = weighed - probs * jnp.sum(weighed, axis=0, keepdims=True)
            total = total + ds
            dsb = ds.astype(BF)
            dvs[tile, part, :] = dot_nn(probs.astype(BF), d_four).astype(BF)
            dks[tile, part, :] = dot_nn(dsb, q_four).astype(BF)
            dqs[tile, part, :] = (
                fold(dot_tn(dsb, ks[tile, part, :])) * HEAD ** (-0.5)
            ).astype(BF)
        dbias[tile] = total
        for s, grads in enumerate((dqs, dks, dvs)):
            ga[s, cols, :] = dot_tn(grads[tile], normed).astype(BF)
            dh1[...] += dot_nn(grads[tile], wa[s, cols, :])
        sg[6:7, cols] = jnp.sum(dqs[tile].astype(F32), axis=0, keepdims=True)
        sg[7:8, cols] = jnp.sum(dvs[tile].astype(F32), axis=0, keepdims=True)
        return carry

    half_rows = width // 2
    halves = [pl.ds(0, half_rows), pl.ds(half_rows, half_rows)]

    def add_core(slot, part):
        add_to(ga.at[slot, part, my_cols], rca.at[slot, part, :])

    def reduce_core(half):
        part = halves[half]
        to_core_sum(ga.at[pl.ds(0, 3), part, her_cols], rca.at[pl.ds(0, 3), part, :], half)

    def reduce_x(half):
        part = halves[half]
        core_copies[1 + half].wait_recv()
        add_core(far, part)
        x_copies.append(
            send(
                ga.at[far, part, my_cols],
                rxa.at[part],
                sem_as.at[half, 1],
                sem_ar.at[half, 1],
                to_x,
            )
        )
        add_core(1, part)
        sum_key.scatter(half)
        add_core(near, part)

    lax.fori_loop(0, tiles_half, attend_back, 0)
    reduce_core(0)
    core_copies[0].wait_recv()
    add_core(3, slice(None))
    sum_proj.scatter(0)
    sum_proj.scatter(1)
    reduce_x(0)
    sum_fc2[0].start_z()
    lax.fori_loop(tiles_half, tiles, attend_back, 0)
    reduce_core(1)

    def mlp_out(slot):
        ph[slot] = dot_nn(ac[slot_rows(slot), :], wf[1]).astype(BF)

    def near_y(half):
        x_copies[half].wait_recv()
        add_to(ga.at[near, halves[half], my_cols], rxa.at[halves[half]])
        sum_near.scatter(half)

    out_copies = []
    sent(ph_c0)
    sent(ph_c1)
    mlp_out(xc_dl)
    out_copies.append(send(ph.at[xc_dl], rc_o.at[0], sem_hs.at[1, 0], sem_hr.at[1, 0], to_core))
    reduce_x(1)
    mlp_out(core_dl)
    out_copies.append(send(ph.at[core_dl], rc_o.at[1], sem_hs.at[1, 1], sem_hr.at[1, 1], to_core))
    mlp_out(x_dl)
    near_y(0)
    sum_fc2[0].middle()
    sum_fc2[1].start_y()

    dh1c = dot_nn(gather, dh1[...].astype(BF))
    n1 = n1s[...]
    sg[0:1, :] = jnp.sum(dh1c * n1, axis=0, keepdims=True)
    sg[1:2, :] = jnp.sum(dh1c, axis=0, keepdims=True)
    dn = norm_back(dh1c * flat_row(n1g_ref), n1, stats[:, 0:1])
    tgrad_ref[...] = (gs[...] + dn).astype(BF)[0:rows]

    back = one_hot(
        iota((LANES, PACK * TILE), 1)
        == TILE * (iota((LANES, 1), 0) >> 6)
        + (TILE - 1 - table_place(iota((LANES, 1), 0) & 63, False)),
        BF,
    )
    for tile in range(tiles):
        high, low = split_two(dbias[tile])
        wide = dot_nn(high, back) + dot_nn(low, back)
        for k in range(PACK):
            head = tile * PACK + k
            line = jnp.zeros((8, LANES), F32)
            for r in range(8):
                piece = wide[8 * r : 8 * (r + 1), TILE * k : TILE * (k + 1)]
                piece = jnp.concatenate([piece, jnp.zeros_like(piece)], axis=1)
                shift = LANES - 1 - CENTRE - (TILE - 1) + SPAN * r
                line = line + shear(piece, shift)
            row, spot = 12 + head // heads_here, LANES * (head % heads_here)
            sg[row : row + 1, spot : spot + LANES] = jnp.sum(line, axis=0, keepdims=True)

    last_small = 1 + z_count + groups

    def small_start(stage, ref, devices):
        cols = slice(None) if ref is sg else my_cols
        return ref, [sg_in.at[stage + k, :, cols] for k in range(len(devices))], [
            send(
                ref,
                sg_in.at[stage + k, :, cols],
                sem_ss.at[stage + k],
                sem_sr.at[stage + k],
                device,
            )
            for k, device in enumerate(devices)
        ]

    def small_end(started):
        ref, landings, copies = started
        for copy in copies:
            copy.wait_recv()
            sent(copy)
        total = ref[...]
        for landing in landings:
            total = total + landing[...]
        ref[...] = total

    def swap(ref, dst, index, device):
        return send(ref, dst, sem_fs.at[index], sem_fr.at[index], device)

    def over_groups(ref, landing, index):
        for step in range(1, groups):
            k = index * (groups - 1) + step - 1
            copy = send(ref, landing.at[step - 1], sem_gs.at[k], sem_gr.at[k], to_group(step))
            copy.wait_recv()
            sent(copy)
        if groups > 1:
            add_to(ref, *[landing.at[step - 1] for step in range(1, groups)])

    final = {}

    def finish(which, parts):
        for part, cols in zip(parts, (left_cols, right_cols), strict=True):
            fin[which, mine, :, cols] = part.total()[...]
        slot = fin.at[which, mine]
        over_groups(slot, group_m.at[which], which)
        final[which, 0] = swap(slot, slot, 3 * which, to_x)
        final[which, 1] = swap(slot, slot, 3 * which + 1, to_core)

    def finish_core(which):
        final[which, 0].wait_recv()
        slot = fin.at[which, x_dl]
        final[which, 2] = swap(slot, slot, 3 * which + 2, to_core)

    def finish_out(which):
        final[which, 1].wait_recv()
        final[which, 2].wait_recv()
        fin_ref[1 + which] = fin[which]

    def share_x(k, slot, part):
        fin_a[slot, :, my_cols] = part.total()[...]
        final[2, k] = swap(fin_a.at[slot, :, my_cols], fin_x.at[k], 6 + k, to_x)

    def shared_x(k, slot):
        final[2, k].wait_recv()
        sent(final[2, k])
        ref = fin_a.at[slot, :, my_cols]
        add_to(ref, fin_x.at[k])
        over_groups(ref, group_a.at[k], 2 + k)

    smalls = small_start(0, sg, [to_core])
    for part in sum_fc1:
        part.start_z()
    near_y(1)
    small_end(smalls)
    smalls = small_start(1, sg, [to_x])
    out_copies[0].wait_recv()
    ph2[1] = (ph[x_dl].astype(F32) + rc_o[0].astype(F32)).astype(BF)
    out_copies.append(send(ph2.at[1], rx_o, sem_hs.at[1, 2], sem_hr.at[1, 2], to_x))
    mlp_out(mine)
    small_end(smalls)
    sg_half = sg.at[:, my_cols]
    smalls = small_start(2, sg_half, [to_y])
    sum_proj.start_z()
    for part in sum_fc1:
        part.middle()
    finish(1, sum_fc2)
    small_end(smalls)
    smalls = small_start(3, sg_half, [to_z(step) for step in range(1, z_count)])
    sum_key.start_z()
    sum_proj.middle()
    finish(0, sum_fc1)
    finish_core(1)

    out_copies[1].wait_recv()
    out_copies[2].wait_recv()
    branch = ph[mine].astype(F32) + rc_o[1].astype(F32) + rx_o[...].astype(F32)
    out_ref[...] = (x1s[...] + (branch + flat_row(f2b_ref)) * row_live).astype(BF)[0:rows]

    sum_key.middle()
    small_end(smalls)
    if groups > 1:
        small_end(
            small_start(
                2 + z_count, sg_half, [to_group(step) for step in range(1, groups)]
            )
        )
    small_last = send(
        sg_half,
        sg_in.at[last_small, :, my_cols],
        sem_ss.at[last_small],
        sem_sr.at[last_small],
        to_core,
    )
    sum_near.start_z()
    share_x(0, 3, sum_proj)
    finish_core(0)
    share_x(1, 1, sum_key)
    small_last.wait_recv()
    sg[:, her_cols] = sg_in[last_small, :, her_cols]
    finish_out(1)
    shared_x(0, 3)

    vec_ref[...] = sg[0:8, :]
    pick = one_hot(iota((width, block), 0) == block * mp + iota((width, block), 1), F32)
    small_ref[0:8, 0:block] = dot_nn(sg[0:8, :], pick, HIGHEST)
    wide_lane = iota((width, hidden), 1)
    pick = one_hot(
        iota((width, hidden), 0)
        == block * mp + wide_lane - block * steps_of(wide_lane, block, hidden // block),
        F32,
    )
    lines = dot_nn(sg[8:16, :], pick, HIGHEST)
    keep = iota((8, hidden), 0) == steps_of(iota((8, hidden), 1), block, hidden // block)
    small_ref[8:9, :] = jnp.sum(jnp.where(keep, lines, 0.0), axis=0, keepdims=True)
    table = sg[pl.ds(12 + mp, 1), :]
    table = jnp.concatenate(
        [table[:, LANES * k : LANES * (k + 1)] for k in range(heads_here)]
        + [jnp.zeros((8 - heads_here, LANES), F32)],
        axis=0,
    )
    turn = one_hot(iota((LANES, LANES), 0) + iota((LANES, LANES), 1) == LANES - 1, F32)
    small_ref[16:24, 0:LANES] = dot_nn(table, turn, HIGHEST)

    finish_out(0)
    shared_x(1, 1)
    fin_a[near, :, my_cols] = sum_near.total()[...]
    slot = fin_a.at[near, :, my_cols]
    over_groups(slot, group_a.at[2], 4)
    near_x = swap(slot, slot, 8, to_x)
    near_x.wait_recv()
    slots = fin_a.at[:, :, my_cols]
    swap(slots, slots, 9, to_core).wait_recv()
    fin_ref[0] = fin_a[...]

    for copy, when in pending:
        if when is None:
            copy.wait_send()
        else:
            pl.when(when)(copy.wait_send)


def unpack(
    out_in,
    tgrad_in,
    vec_in,
    small_in,
    fin_in,
    out_ref,
    tgrad_ref,
    n1g_ref,
    n1b_ref,
    qkvg_ref,
    qvg_ref,
    relg_ref,
    projg_ref,
    pbg_ref,
    n2g_ref,
    n2b_ref,
    f1g_ref,
    f1bg_ref,
    f2g_ref,
    f2bg_ref,
):
    hidden, width = f2g_ref.shape
    out_ref[...] = out_in[...]
    tgrad_ref[...] = tgrad_in[...]
    for k, ref in enumerate((n1g_ref, n1b_ref, pbg_ref, n2g_ref, n2b_ref, f2bg_ref)):
        ref[...] = vec_in[k : k + 1, :].reshape(width)
    for s in range(3):
        qkvg_ref[s] = fin_in[0, s].astype(F32)
    projg_ref[...] = fin_in[0, 3].astype(F32)
    f1g_ref[...] = fin_in[1].reshape(hidden, width).astype(F32).T
    f2g_ref[...] = fin_in[2].reshape(hidden, width).astype(F32)
    qvg_ref[...] = small_in[6:8, 0 : qvg_ref.shape[1]]
    f1bg_ref[...] = small_in[8:9, :].reshape(hidden)
    relg_ref[...] = small_in[16 : 16 + relg_ref.shape[0], 0:ENTRIES]


def solution(mesh):
    n_dp, n_mp = mesh.shape["dp"], mesh.shape["mp"]

    def shards(
        tokens,
        crop_kind,
        norm1_gain,
        norm1_bias,
        qkv_weight,
        qv_bias,
        rel_table,
        proj_weight,
        proj_bias,
        norm2_gain,
        norm2_bias,
        fc1_weight,
        fc1_bias,
        fc2_weight,
        fc2_bias,
        out_grad,
    ):
        rows, width = tokens.shape
        windows = rows // WIN
        padded = -(-rows // 16) * 16
        block = proj_weight.shape[0]
        hidden = fc2_weight.shape[0]
        heads_here = rel_table.shape[1]
        places = SLOTS * windows
        tiles = width // TILE
        z_count = n_mp // 2
        groups = n_dp // GROUP
        dims = (n_dp, n_mp, rows, windows, padded, width, block, hidden)

        def full(*shape):
            return jax.ShapeDtypeStruct(shape, F32)

        vmem = pl.BlockSpec(memory_space=pltpu.VMEM)
        dma = pltpu.SemaphoreType.DMA
        results = pl.pallas_call(
            functools.partial(body, dims),
            out_shape=[
                jax.ShapeDtypeStruct((rows, width), BF),
                jax.ShapeDtypeStruct((rows, width), BF),
                full(8, width),
                full(24, hidden),
                jax.ShapeDtypeStruct((3, GROUP, block, width), BF),
            ],
            in_specs=[pl.BlockSpec(memory_space=pltpu.SMEM)] + [vmem] * 15,
            out_specs=[vmem] * 5,
            scratch_shapes=[
                pltpu.VMEM((GROUP, width, width), BF),
                pltpu.VMEM((2, width, width), BF),
                pltpu.VMEM((hidden, width), BF),
                pltpu.VMEM((n_mp, 8, hidden), F32),
                pltpu.VMEM((8, hidden), F32),
                pltpu.VMEM((padded, width), F32),
                pltpu.VMEM((padded, width), F32),
                pltpu.VMEM((padded, width), F32),
                pltpu.VMEM((padded, width), F32),
                pltpu.VMEM((padded, TILE), F32),
                pltpu.VMEM((8, width), F32),
                pltpu.VMEM((8, width), F32),
                pltpu.VMEM((places, width), BF),
                pltpu.VMEM((tiles, places, TILE), BF),
                pltpu.VMEM((tiles, places, TILE), BF),
                pltpu.VMEM((tiles, places, TILE), BF),
                pltpu.VMEM((tiles, places, TILE), BF),
                pltpu.VMEM((tiles * windows, SLOTS, LANES), F32),
                pltpu.VMEM((tiles, SLOTS, LANES), F32),
                pltpu.VMEM((tiles, SLOTS, LANES), F32),
                pltpu.VMEM((GROUP, padded, width), BF),
                pltpu.VMEM((GROUP, padded, width), BF),
                pltpu.VMEM((GROUP * padded, width), BF),
                pltpu.VMEM((GROUP * padded, width), BF),
                pltpu.VMEM((GROUP, padded, width), BF),
                pltpu.VMEM((2, padded, width), BF),
                pltpu.VMEM((padded, width), BF),
                pltpu.VMEM((2, padded, width), BF),
                pltpu.VMEM((2, padded, width), BF),
                pltpu.VMEM((padded, width), BF),
                pltpu.VMEM((places, width), BF),
                pltpu.VMEM((tiles, places, TILE), BF),
                pltpu.VMEM((tiles, places, TILE), BF),
                pltpu.VMEM((tiles, places, TILE), BF),
                pltpu.VMEM((tiles, SLOTS, LANES), F32),
                pltpu.VMEM((places, width), F32),
                pltpu.VMEM((GROUP, width, width), BF),
                pltpu.VMEM((2, width, width), BF),
                pltpu.VMEM((GROUP, width, width // 2), BF),
                pltpu.VMEM((width, width // 2), BF),
                pltpu.VMEM((7, z_count, block, width // 2), BF),
                pltpu.VMEM((8, z_count - 1, block, width // 2), BF),
                pltpu.VMEM((8, block, width // 2), BF),
                pltpu.VMEM((2, GROUP, block, width), BF),
                pltpu.VMEM((GROUP, block, width), BF),
                pltpu.VMEM((2, block, width // 2), BF),
                pltpu.VMEM((2, max(groups - 1, 1), block, width), BF),
                pltpu.VMEM((3, max(groups - 1, 1), block, width // 2), BF),
                pltpu.VMEM((24, width), F32),
                pltpu.VMEM((2 + z_count + groups, 24, width), F32),
                dma((7, 2 * z_count + 1)),
                dma((7, 2 * z_count + 1)),
                dma((2 * n_mp + 4,)),
                dma((2 * n_mp + 4,)),
                dma((2, 3)),
                dma((2, 3)),
                dma((2, 3)),
                dma((2, 3)),
                dma((3, 2)),
                dma((3, 2)),
                dma((7, z_count)),
                dma((7, z_count)),
                dma((8, 4)),
                dma((8, 4)),
                dma((10,)),
                dma((10,)),
                dma((2 + z_count + groups,)),
                dma((2 + z_count + groups,)),
                dma((5 * max(groups - 1, 1),)),
                dma((5 * max(groups - 1, 1),)),
            ],
            compiler_params=pltpu.CompilerParams(
                collective_id=0, has_side_effects=True, vmem_limit_bytes=63 * 2**20
            ),
        )(
            crop_kind,
            tokens,
            out_grad,
            norm1_gain,
            norm1_bias,
            jnp.swapaxes(qkv_weight, 1, 2),
            qv_bias,
            rel_table.T,
            proj_weight,
            proj_bias,
            norm2_gain,
            norm2_bias,
            fc1_weight,
            fc1_bias,
            fc2_weight,
            fc2_bias,
        )
        results = pl.pallas_call(
            unpack,
            out_shape=[
                jax.ShapeDtypeStruct((rows, width), BF),
                jax.ShapeDtypeStruct((rows, width), BF),
                full(width),
                full(width),
                full(3, block, width),
                full(2, block),
                full(heads_here, ENTRIES),
                full(block, width),
                full(width),
                full(width),
                full(width),
                full(width, hidden),
                full(hidden),
                full(hidden, width),
                full(width),
            ],
            in_specs=[vmem] * 5,
            out_specs=[vmem] * 15,
        )(*results)
        results = list(results)
        results[4] = jnp.swapaxes(results[4], 1, 2)
        results[6] = results[6].T
        return tuple(results)

    in_specs = (
        P(("dp", "mp"), None),
        P("dp"),
        P(),
        P(),
        P(None, None, "mp"),
        P(None, "mp"),
        P(None, "mp"),
        P("mp", None),
        P(),
        P(),
        P(),
        P(None, "mp"),
        P("mp"),
        P("mp", None),
        P(),
        P(("dp", "mp"), None),
    )
    out_specs = (
        P(("dp", "mp"), None),
        P(("dp", "mp"), None),
        P(),
        P(),
        P(None, None, "mp"),
        P(None, "mp"),
        P(None, "mp"),
        P("mp", None),
        P(),
        P(),
        P(),
        P(None, "mp"),
        P("mp"),
        P("mp", None),
        P(),
    )
    return jax.shard_map(shards, mesh=mesh, in_specs=in_specs, out_specs=out_specs, check_vma=False)
```

```python
import functools

import jax
import jax.numpy as jnp
from jax import lax
from jax.experimental import pallas as pl
from jax.experimental.pallas import tpu as pltpu
from jax.sharding import PartitionSpec as P

HEAD = 32
SIDE = 7
LOCAL_SIDE = 3
WIN = 49
SPAN = 2 * SIDE - 1
ENTRIES = SPAN * SPAN
CENTRE = (SIDE - 1) * SPAN + SIDE - 1
SLOTS = 64
TILE = 128
PACK = 4
GROUP = 4
LANES = 256
EPSILON = 1e-05
NEG_FILL = -1000000000.0
GELU_A = 0.7978845608028654
GELU_B = 0.044715
HIGHEST = lax.Precision.HIGHEST
MESH = pl.DeviceIdType.MESH
BF = jnp.bfloat16
F32 = jnp.float32


def dot(left, right, dims, precision=None):
    return lax.dot_general(
        left, right, (dims, ((), ())), preferred_element_type=F32, precision=precision
    )


def dot_nn(left, right, precision=None):
    return dot(left, right, ((1,), (0,)), precision)


def dot_nt(left, right, precision=None):
    return dot(left, right, ((1,), (1,)), precision)


def dot_tn(left, right, precision=None):
    return dot(left, right, ((0,), (0,)), precision)


def iota(shape, axis):
    return lax.broadcasted_iota(jnp.int32, shape, axis)


def one_hot(cond, dtype):
    return jnp.where(cond, 1.0, 0.0).astype(dtype)


def steps_of(values, width, count):
    total = jnp.zeros_like(values)
    for step in range(1, count):
        total = total + jnp.where(values >= step * width, 1, 0)
    return total


def shear(values, shift):
    moved = pltpu.roll(values, shift, axis=1)
    return pltpu.roll(moved, 0, axis=1, stride=1, stride_axis=0)


def split_two(values):
    high = values.astype(BF)
    return high, (values - high.astype(F32)).astype(BF)


def flat_row(ref):
    return ref[...].reshape(1, -1)


def norm_parts(values):
    mean = jnp.mean(values, axis=-1, keepdims=True)
    centre = values - mean
    spread = jnp.mean(centre * centre, axis=-1, keepdims=True)
    scale = lax.rsqrt(spread + EPSILON)
    return centre * scale, scale


def norm_back(grad_normed, normed, scale):
    return scale * (
        grad_normed
        - jnp.mean(grad_normed, axis=-1, keepdims=True)
        - normed * jnp.mean(grad_normed * normed, axis=-1, keepdims=True)
    )


def slot_place(columns, windows, kinds):
    window = steps_of(columns, WIN, windows)
    slot = columns - WIN * window
    kind = jnp.zeros_like(columns)
    for w in range(windows):
        kind = jnp.where(window == w, kinds[w], kind)
    whole = slot + steps_of(slot, SIDE, SIDE)
    corner = slot + (8 - LOCAL_SIDE) * steps_of(slot, LOCAL_SIDE, LOCAL_SIDE)
    rest = slot + (8 * LOCAL_SIDE - LOCAL_SIDE * LOCAL_SIDE)
    local = jnp.where(slot < LOCAL_SIDE * LOCAL_SIDE, corner, rest)
    place = SLOTS * window + jnp.where(kind == 0, whole, local)
    live = jnp.where(kind == 0, WIN, LOCAL_SIDE * LOCAL_SIDE)
    inside = columns < WIN * windows
    return jnp.where(inside, place, -1), inside & (slot < live)


def body(
    dims,
    kind_ref,
    tok_ref,
    og_ref,
    n1g_ref,
    n1b_ref,
    qkvw_ref,
    qvb_ref,
    tab_ref,
    pw_ref,
    pb_ref,
    n2g_ref,
    n2b_ref,
    f1w_ref,
    f1b_ref,
    f2w_ref,
    f2b_ref,
    out_ref,
    tgrad_ref,
    vec_ref,
    small_ref,
    fin_ref,
    wa,
    wf,
    ft,
    sp,
    pk,
    xs,
    x1s,
    n1s,
    gs,
    stats,
    qb,
    fb,
    h1p,
    qs,
    ks,
    vs,
    at,
    pt,
    bias_whole,
    bias_local,
    hg,
    gg,
    ac,
    dp_s,
    ph,
    rc_h,
    rx_h,
    ph2,
    rc_o,
    rx_o,
    gabp,
    dqs,
    dks,
    dvs,
    dbias,
    dh1,
    ga,
    gf,
    rca,
    rxa,
    ry,
    rz,
    rr,
    fin,
    fin_a,
    fin_x,
    group_m,
    group_a,
    sg,
    sg_in,
    sem_ws,
    sem_wr,
    sem_bs,
    sem_br,
    sem_rs,
    sem_rr,
    sem_hs,
    sem_hr,
    sem_as,
    sem_ar,
    sem_ys,
    sem_yr,
    sem_zs,
    sem_zr,
    sem_fs,
    sem_fr,
    sem_ss,
    sem_sr,
    sem_gs,
    sem_gr,
):
    n_dp, n_mp, rows, windows, padded, width, block, hidden = dims
    groups = n_dp // GROUP
    places = SLOTS * windows
    z_count = n_mp // 2
    heads_here = block // HEAD
    tiles = width // TILE
    half_width = width // 2
    mp = lax.axis_index("mp")
    dp = lax.axis_index("dp")
    z = mp // 2
    y = mp % 2
    base = (dp // GROUP) * GROUP
    mine = dp % GROUP
    x = mine // 2
    c = mine % 2
    core_dl = x * 2 + (1 - c)
    x_dl = (1 - x) * 2 + c
    xc_dl = (1 - x) * 2 + (1 - c)
    to_core = (base + core_dl, mp)
    to_x = (base + x_dl, mp)
    to_y = (dp, z * 2 + (1 - y))
    near = 2 * x
    far = 2 - 2 * x

    def z_at(step):
        return (z + step) % z_count

    def to_z(step):
        return (dp, z_at(step) * 2 + y)

    def to_group(step):
        return ((dp + GROUP * step) % n_dp, mp)

    pending = []

    def remote(src, dst, s_sem, r_sem, device):
        return pltpu.make_async_remote_copy(
            src_ref=src,
            dst_ref=dst,
            send_sem=s_sem,
            recv_sem=r_sem,
            device_id=device,
            device_id_type=MESH,
        )

    def send(src, dst, s_sem, r_sem, device, when=None):
        copy = remote(src, dst, s_sem, r_sem, device)
        if when is None:
            copy.start()
        else:
            pl.when(when)(copy.start)
        pending.append((copy, when))
        return copy

    def forget(copy):
        pending[:] = [other for other in pending if other[0] is not copy]

    def sent(copy):
        copy.wait_send()
        forget(copy)

    barrier = pltpu.get_barrier_semaphore()
    peers = [to_core, to_x, to_y]
    peers += [to_z(step) for step in range(1, z_count)]
    peers += [to_group(step) for step in range(1, groups)]
    for peer in peers:
        pl.semaphore_signal(barrier, inc=1, device_id=peer, device_id_type=MESH)

    own = pl.ds(pl.multiple_of(block * mp, 16), block)
    my_cols = pl.ds(pl.multiple_of(half_width * c, TILE), half_width)
    her_cols = pl.ds(pl.multiple_of(half_width * (1 - c), TILE), half_width)
    for s in range(3):
        wa[s, own, my_cols] = qkvw_ref[s, :, my_cols]
    wa[3, own, my_cols] = pw_ref[:, my_cols]

    pk[...] = jnp.zeros_like(pk)
    pk[0:heads_here, 0:ENTRIES] = tab_ref[...]
    pk[3:5, 0:block] = qvb_ref[...]
    pk[5:6, :] = flat_row(f1b_ref)
    sp[mp] = pk[...]

    pl.semaphore_wait(barrier, len(peers))

    def rows_of(other_z, other_y):
        return pl.ds(pl.multiple_of(block * (other_z * 2 + other_y), 16), block)

    relayed = z_count == 4
    if relayed:
        order = [2, jnp.where(z == 0, 3, 1), jnp.where(z == 0, 1, 3)]
    else:
        order = list(range(1, z_count))
    inner = (z == 1) | (z == 2)

    def spread_z(buffer, part, index, first):
        ref = buffer.at[part]
        for step in range(1, z_count):
            far_end = {1: z != 3, 2: None, 3: z != 0}[step] if relayed else None
            k = first + step - 1
            send(ref, ref, sem_ws.at[index, k], sem_wr.at[index, k], to_z(step), far_end)

    def arrived_z(buffer, part_of, index, first, place):
        step = order[place]
        part = part_of((z + z_count - step) % z_count)
        ref = buffer.at[part]
        k = first + step - 1
        remote(ref, ref, sem_ws.at[index, k], sem_wr.at[index, k], to_y).wait_recv()
        if relayed and place == 0:
            last = 2 * (z - 1)
            send(
                ref,
                ref,
                sem_ws.at[index, first + 3],
                sem_wr.at[index, first + last],
                (dp, 3 * (z - 1) * 2 + y),
                inner,
            )
        return part

    class Gather:
        def __init__(self, index, buffer, part):
            self.index, self.buffer, self.part = index, buffer, part

        def forward_y(self, part, step):
            k = z_count + step
            ref = self.buffer.at[part]
            send(ref, ref, sem_ws.at[self.index, k], sem_wr.at[self.index, k], to_y)

        def start_y(self):
            self.forward_y(self.part(z, y), 0)

        def start_z(self):
            spread_z(self.buffer, self.part(z, y), self.index, 0)

        def arrive_z(self, place):
            part = arrived_z(self.buffer, lambda oz: self.part(oz, y), self.index, 0, place)
            self.forward_y(part, order[place])
            return part

        def arrive_y(self, place):
            step = 0 if place == 0 else order[place - 1]
            part = self.part((z + z_count - step) % z_count, 1 - y)
            ref = self.buffer.at[part]
            k = z_count + step
            remote(ref, ref, sem_ws.at[self.index, k], sem_wr.at[self.index, k], to_y).wait_recv()
            return part

    class GatherLong:
        def __init__(self, index, buffer, part):
            self.index, self.buffer, self.part = index, buffer, part

        def pair(self):
            ref = self.buffer.at[self.part(z, y)]
            k = 2 * z_count
            return ref, ref, sem_ws.at[self.index, k], sem_wr.at[self.index, k], to_y

        def start_y(self):
            send(*self.pair())

        def start_z(self):
            spread_z(self.buffer, self.part(z, y), self.index, 0)

        def arrive_y(self):
            remote(*self.pair()).wait_recv()
            spread_z(self.buffer, self.part(z, 1 - y), self.index, z_count)

        def arrive_z(self, place):
            for column in range(2):
                other_y = y if column == 0 else 1 - y
                arrived_z(
                    self.buffer,
                    lambda oz: self.part(oz, other_y),
                    self.index,
                    z_count * column,
                    place,
                )

    def half_block(other_z, other_y):
        return rows_of(other_z, other_y), my_cols

    def whole_block(other_z, other_y):
        return (rows_of(other_z, other_y),)

    def quarter_block(other_z, other_y):
        start = block * (other_z * 2 + other_y) + (block // 2) * x
        return pl.ds(pl.multiple_of(start, 16), block // 2), my_cols

    def left_block(other_z, other_y):
        return rows_of(other_z, other_y), pl.ds(0, half_width)

    def right_block(other_z, other_y):
        return rows_of(other_z, other_y), pl.ds(half_width, half_width)

    small = Gather(0, sp, lambda oz, oy: (oz * 2 + oy,))
    near_w = Gather(1, wa.at[near], half_block)
    key_w = Gather(2, wa.at[1], half_block)
    proj_w = Gather(3, wa.at[3], quarter_block)
    fc1_w = Gather(4, wf.at[0], whole_block)
    fc2_w = Gather(5, wf.at[1], left_block)
    fc2_long = GatherLong(6, wf.at[1], right_block)
    later_z, later_y = range(z_count - 1), range(1, z_count)

    for part in (near_w, key_w, proj_w, small):
        part.start_z()
        part.start_y()
    ft[...] = f1w_ref[...].T
    quarter = pl.ds(pl.multiple_of(block * mine, 16), block)
    wf[0, own, :] = ft[quarter, :]
    wf[1, own, :] = f2w_ref[quarter, :]

    def send_rows(ring, index, slot, device, k):
        return send(ring.at[slot], ring.at[slot], sem_rs.at[index, k], sem_rr.at[index, k], device)

    kinds = [kind_ref[mp * windows + w] for w in range(windows)]
    place_row, _ = slot_place(iota((1, padded), 1), windows, kinds)
    place_col, live_col = slot_place(iota((padded, 1), 0), windows, kinds)
    spread = one_hot(iota((places, padded), 0) == place_row, BF)
    gather = one_hot(iota((padded, places), 1) == place_col, BF)
    row_live = jnp.where(live_col, 1.0, 0.0)

    gs[...] = jnp.zeros_like(gs)
    gs[0:rows, :] = og_ref[...].astype(F32)
    sg[...] = jnp.zeros_like(sg)
    masked = gs[...] * row_live
    gg[mine] = masked.astype(BF)
    gg_c0 = send_rows(gg, 0, mine, to_core, 1)
    sg[5:6, :] = jnp.sum(masked, axis=0, keepdims=True)

    xs[...] = jnp.zeros_like(xs)
    xs[0:rows, :] = tok_ref[...].astype(F32)
    normed_one, scale_one = norm_parts(xs[...])
    n1s[...] = normed_one
    stats[:, 0:1] = scale_one
    h1 = (normed_one * flat_row(n1g_ref) + flat_row(n1b_ref)).astype(BF)
    h1p[...] = dot_nn(spread, h1).astype(BF)

    along_x, proj_x = [], []

    def forward_x(part):
        k = len(along_x)
        ref = wa.at[near].at[part]
        along_x.append(send(ref, ref, sem_bs.at[k], sem_br.at[k], to_x))

    def forward_proj(part):
        k = n_mp + 4 + len(proj_x)
        ref = wa.at[3].at[part]
        proj_x.append(send(ref, ref, sem_bs.at[k], sem_br.at[k], to_x))

    forward_x(near_w.arrive_y(0))

    def core_half(index, slot):
        ref = wa.at[slot, :, my_cols]
        return send(ref, ref, sem_bs.at[n_mp + index], sem_br.at[n_mp + index], to_core)

    forward_x(near_w.arrive_z(0))
    fc1_w.start_z()
    for place in later_z[1:]:
        forward_x(near_w.arrive_z(place))
    for place in later_z:
        key_w.arrive_z(place)
        forward_proj(proj_w.arrive_z(place))
    for part in (fc1_w, fc2_w, fc2_long):
        part.start_y()
    for place in later_z:
        small.arrive_z(place)
    for place in later_y:
        forward_x(near_w.arrive_y(place))
    fc1_w.arrive_z(0)
    fc2_w.start_z()
    for place in range(z_count):
        forward_proj(proj_w.arrive_y(place))
    gg_x = send_rows(gg, 0, mine, to_x, 0)
    for place in later_z[1:]:
        fc1_w.arrive_z(place)
    fc2_long.arrive_y()
    fc2_long.start_z()
    for place in range(z_count):
        key_w.arrive_y(place)
    core_near = core_half(0, near)
    core_key = core_half(1, 1)
    for place in range(z_count):
        small.arrive_y(place)
    lane = iota((1, width), 1)
    owner = steps_of(lane, block, n_mp)
    within = lane - block * owner
    pick_row = iota((n_mp, width), 0) == owner
    spots = iota((hidden, width), 0)

    def spread_row(row, offset):
        picked = dot_nn(sp[:, row, :], one_hot(spots == within + offset, F32), HIGHEST)
        return jnp.sum(jnp.where(pick_row, picked, 0.0), axis=0, keepdims=True)

    qb[0:1, :] = spread_row(3, 0)
    qb[1:2, :] = spread_row(4, 0)
    fb[0:1, :] = spread_row(5, block * mine)

    def table_place(cells, local):
        row, column = cells >> 3, cells & 7
        spot = SPAN * row + column
        if local:
            last = LOCAL_SIDE - 1
            dead = (row > last) | (column > last)
            spot = jnp.where(dead, SPAN * last + last, spot)
        return spot

    cell = iota((1, LANES), 1)
    cell_head, cell_spot = cell >> 6, cell & 63
    source = iota((PACK * TILE, LANES), 0)
    picks = []
    for local in (False, True):
        picks.append(one_hot(source == TILE * cell_head + table_place(cell_spot, local), BF))

    def bias_of(tile):
        shifted = []
        for k in range(PACK):
            head = tile * PACK + k
            line = sp[head // heads_here, head % heads_here : head % heads_here + 1, 0:LANES]
            line = jnp.broadcast_to(line, (8, LANES))
            shifted.append(
                jnp.concatenate(
                    [
                        shear(line, (SPAN * r - CENTRE) % LANES)[:, 0:TILE]
                        for r in range(8)
                    ],
                    axis=0,
                )
            )
        high, low = split_two(jnp.concatenate(shifted, axis=1))
        bias_whole[tile] = dot_nn(high, picks[0]) + dot_nn(low, picks[0])
        bias_local[tile] = dot_nn(high, picks[1]) + dot_nn(low, picks[1])

    for tile in range(tiles):
        bias_of(tile)
    for copy in along_x:
        copy.wait_recv()
    core_far = core_half(2, far)
    core_near.wait_recv()
    core_key.wait_recv()
    core_far.wait_recv()

    head_lane = iota((PACK * SLOTS, TILE), 1) >> 5
    head_mask = (iota((PACK * SLOTS, TILE), 0) >> 6) == head_lane
    key_place = iota((SLOTS, 1), 0)
    key_row, key_col = key_place >> 3, key_place & 7
    usable = []
    for w in range(windows):
        side = jnp.where(kinds[w] == 0, SIDE, LOCAL_SIDE)
        usable.append((key_row < side) & (key_col < side))

    def four(values):
        return jnp.where(head_mask, jnp.concatenate([values] * PACK, axis=0), 0.0).astype(BF)

    def fold(values):
        picked = jnp.where(head_mask, values, 0.0)
        total = picked[0:SLOTS]
        for k in range(1, PACK):
            total = total + picked[SLOTS * k : SLOTS * (k + 1)]
        return total

    def attend(tile, carry):
        cols = pl.ds(pl.multiple_of(tile * TILE, TILE), TILE)
        normed = h1p[...]
        q_tile = (dot_nt(normed, wa[0, cols, :]) + qb[0:1, cols]) * HEAD ** (-0.5)
        qs[tile] = q_tile.astype(BF)
        ks[tile] = dot_nt(normed, wa[1, cols, :]).astype(BF)
        vs[tile] = (dot_nt(normed, wa[2, cols, :]) + qb[1:2, cols]).astype(BF)
        for w in range(windows):
            part = pl.ds(SLOTS * w, SLOTS)
            scores = dot_nt(ks[tile, part, :], four(qs[tile, part, :].astype(F32)))
            bias = jnp.where(kinds[w] == 0, bias_whole[tile], bias_local[tile])
            scores = jnp.where(usable[w], scores + bias, NEG_FILL)
            raised = jnp.exp(scores - jnp.max(scores, axis=0, keepdims=True))
            probs = raised / jnp.sum(raised, axis=0, keepdims=True)
            pt[tile * windows + w] = probs
            at[tile, part, :] = fold(dot_tn(probs.astype(BF), vs[tile, part, :])).astype(BF)
        return carry

    third = tiles // 3
    lax.fori_loop(0, third, attend, 0)
    for place in later_z:
        fc2_w.arrive_z(place)
    gg_x.wait_recv()
    gg_c1 = send_rows(gg, 0, x_dl, to_core, 2)
    lax.fori_loop(third, 2 * third, attend, 0)
    for copy in proj_x:
        copy.wait_recv()
    core_proj = core_half(3, 3)
    lax.fori_loop(2 * third, tiles, attend, 0)
    core_proj.wait_recv()

    attn = jnp.concatenate(
        [dot_nn(gather, at[tile]).astype(BF) for tile in range(tiles)], axis=1
    )
    x1 = xs[...] + (dot_nn(attn, wa[3]) + flat_row(pb_ref)) * row_live
    x1s[...] = x1
    normed_two, scale_two = norm_parts(x1)
    hg[mine] = (normed_two * flat_row(n2g_ref) + flat_row(n2b_ref)).astype(BF)
    hg_x = send_rows(hg, 1, mine, to_x, 0)
    hg_c0 = send_rows(hg, 1, mine, to_core, 1)

    for place in later_z:
        fc2_long.arrive_z(place)
    for place in range(z_count):
        fc1_w.arrive_y(place)
    for place in range(z_count):
        fc2_w.arrive_y(place)

    def slot_rows(slot):
        return pl.ds(pl.multiple_of(padded * slot, 16), padded)

    def mlp(slot):
        pre = dot_nt(hg[slot], wf[0]) + fb[0:1, :]
        square = pre * pre
        bend = jnp.tanh(GELU_A * (pre + GELU_B * (square * pre)))
        ac[slot_rows(slot), :] = (0.5 * pre * (1.0 + bend)).astype(BF)
        slope = 0.5 * (1.0 + bend) + 0.5 * pre * (1.0 - bend * bend) * (
            GELU_A * (1.0 + 3.0 * GELU_B * square)
        )
        dpre = (dot_nt(gg[slot], wf[1]) * slope).astype(BF)
        dp_s[slot_rows(slot), :] = dpre
        ph[slot] = dot_nn(dpre, wf[0]).astype(BF)

    mlp(mine)
    gg_c0.wait_recv()
    hg_c0.wait_recv()
    hg_x.wait_recv()
    hg_c1 = send_rows(hg, 1, x_dl, to_core, 2)
    mlp(core_dl)
    ph_c1 = send(ph.at[core_dl], rc_h.at[1], sem_hs.at[0, 1], sem_hr.at[0, 1], to_core)
    gg_c1.wait_recv()
    hg_c1.wait_recv()
    mlp(xc_dl)
    ph_c0 = send(ph.at[xc_dl], rc_h.at[0], sem_hs.at[0, 0], sem_hr.at[0, 0], to_core)
    mlp(x_dl)
    ph_c0.wait_recv()
    ph2[0] = (ph[x_dl].astype(F32) + rc_h[0].astype(F32)).astype(BF)
    ph_x = send(ph2.at[0], rx_h, sem_hs.at[0, 2], sem_hr.at[0, 2], to_x)

    tiles_half = tiles // 2
    z_half = z_count // 2

    def add_to(ref, *others):
        total = ref[...].astype(F32)
        for other in others:
            total = total + other[...].astype(F32)
        ref[...] = total.astype(BF)

    class Line:
        def __init__(self, index, part, relay):
            self.index, self.part = index, part
            self.relay = relay and relayed

        def recv(self, step):
            return rz.at[self.index, step - 1]

        def sems(self, k, r):
            return sem_zs.at[self.index, k], sem_zr.at[self.index, r]

        def over(self):
            return remote(
                self.part(z_count - 1 - z),
                rr.at[self.index],
                *self.sems(3, 3),
                (dp, (1 + z // 3) * 2 + y),
            )

        def far(self):
            return remote(self.part(z_at(2)), self.recv(2), *self.sems(1, 1), to_z(2))

        def start(self):
            if not self.relay:
                for step in range(1, z_count):
                    send(
                        self.part(z_at(step)),
                        self.recv(step),
                        *self.sems(step - 1, step - 1),
                        to_z(step),
                    )
                return
            outer = jnp.logical_not(inner)
            copy = self.over()
            pl.when(outer)(copy.start)
            pending.append((copy, outer))
            for step, when in ((1, z != 3), (3, z != 0)):
                send(
                    self.part(z_at(step)),
                    self.recv(step),
                    *self.sems(step - 1, step - 1),
                    to_z(step),
                    when,
                )
            pl.when(outer)(self.far().start)

        def middle(self):
            if self.relay:

                @pl.when(inner)
                def _():
                    self.over().wait_recv()
                    add_to(self.part(z_at(2)), rr.at[self.index])
                    self.far().start()

                pending.append((self.far(), None))

        def total(self):
            whens = [z != 0, None, z != z_count - 1] if self.relay else [None] * (z_count - 1)
            ref = self.part(z)
            for step in range(1, z_count):
                copy = remote(ref, self.recv(step), *self.sems(step - 1, step - 1), to_y)

                def take(copy=copy, step=step):
                    copy.wait_recv()
                    add_to(ref, self.recv(step))

                if whens[step - 1] is None:
                    take()
                else:
                    pl.when(whens[step - 1])(take)
            return ref

    class YFirst:
        def __init__(self, index, source, cols, relay):
            self.index, self.source, self.cols = index, source, cols
            self.line = Line(index, lambda oz: ry.at[index, oz], relay)
            self.along_y = {}

        def scatter(self, half):
            for oz in range(half * z_half, (half + 1) * z_half):
                self.along_y[oz] = send(
                    self.source.at[rows_of(oz, 1 - y), self.cols],
                    ry.at[self.index, oz],
                    sem_ys.at[self.index, oz],
                    sem_yr.at[self.index, oz],
                    to_y,
                )

        def start_z(self):
            for oz in range(z_count):
                self.along_y[oz].wait_recv()
                add_to(ry.at[self.index, oz], self.source.at[rows_of(oz, y), self.cols])
            self.line.start()

        def middle(self):
            self.line.middle()

        def total(self):
            return self.line.total()

    class ZFirst:
        def __init__(self, index, source, cols):
            self.index = index
            self.lines = [
                Line(index + k, lambda oz, oy=oy: source.at[rows_of(oz, oy), cols], True)
                for k, oy in enumerate((1 - y, y))
            ]

        def start_z(self):
            for line in self.lines:
                line.start()

        def middle(self):
            for line in self.lines:
                line.middle()

        def start_y(self):
            self.copy = send(
                self.lines[0].total(),
                ry.at[self.index, 0],
                sem_ys.at[self.index, 0],
                sem_yr.at[self.index, 0],
                to_y,
            )

        def total(self):
            ref = self.lines[1].total()
            self.copy.wait_recv()
            add_to(ref, ry.at[self.index, 0])
            return ref

    left_cols, right_cols = pl.ds(0, half_width), pl.ds(half_width, half_width)
    sum_near = YFirst(0, ga.at[near], my_cols, True)
    sum_key = YFirst(1, ga.at[1], my_cols, True)
    sum_proj = YFirst(2, ga.at[3], my_cols, True)
    sum_fc1 = [YFirst(3, gf.at[0], left_cols, True), YFirst(4, gf.at[0], right_cols, True)]
    sum_fc2 = [YFirst(5, gf.at[1], left_cols, True), ZFirst(6, gf.at[1], right_cols)]

    def all_rows(ring):
        return ring[...].reshape(GROUP * padded, width)

    def fc1_grad(tile, carry):
        cols = pl.ds(pl.multiple_of(tile * TILE, TILE), TILE)
        gf[0, cols, :] = dot_tn(dp_s[:, cols], all_rows(hg)).astype(BF)
        return carry

    def fc2_grad(tile, carry):
        cols = pl.ds(pl.multiple_of(tile * TILE, TILE), TILE)
        gf[1, cols, :] = dot_tn(ac[:, cols], all_rows(gg)).astype(BF)
        return carry

    lax.fori_loop(0, tiles_half, fc2_grad, 0)
    sum_fc2[0].scatter(0)
    lax.fori_loop(tiles_half, tiles, fc2_grad, 0)
    sum_fc2[1].start_z()
    sum_fc2[0].scatter(1)
    lax.fori_loop(0, tiles_half, fc1_grad, 0)
    for part in sum_fc1:
        part.scatter(0)
    lax.fori_loop(tiles_half, tiles, fc1_grad, 0)
    for part in sum_fc1:
        part.scatter(1)
    sg[pl.ds(8 + mine, 1), :] = jnp.sum(dp_s[...].astype(F32), axis=0, keepdims=True)

    ph_c1.wait_recv()
    ph_x.wait_recv()
    dh2 = ph[mine].astype(F32) + rc_h[1].astype(F32) + rx_h[...].astype(F32)
    sg[3:4, :] = jnp.sum(dh2 * normed_two, axis=0, keepdims=True)
    sg[4:5, :] = jnp.sum(dh2, axis=0, keepdims=True)
    dx1 = gs[...] + norm_back(dh2 * flat_row(n2g_ref), normed_two, scale_two)
    gs[...] = dx1
    gab = dx1 * row_live
    sg[2:3, :] = jnp.sum(gab, axis=0, keepdims=True)
    gab = gab.astype(BF)
    gabp[...] = dot_nn(spread, gab).astype(BF)
    for tile in range(tiles):
        ga[3, TILE * tile : TILE * (tile + 1), :] = dot_tn(
            attn[:, TILE * tile : TILE * (tile + 1)], gab
        ).astype(BF)

    core_copies, x_copies = [], []

    def to_core_sum(source, landing, k):
        core_copies.append(send(source, landing, sem_as.at[k, 0], sem_ar.at[k, 0], to_core))

    to_core_sum(ga.at[3, :, her_cols], rca.at[3], 2)
    sum_fc2[1].middle()

    dbias[...] = jnp.zeros_like(dbias)
    dh1[...] = jnp.zeros_like(dh1)

    def attend_back(tile, carry):
        cols = pl.ds(pl.multiple_of(tile * TILE, TILE), TILE)
        dattn = dot_nt(gabp[...], wa[3, cols, :])
        normed = h1p[...]
        total = jnp.zeros((SLOTS, LANES), F32)
        for w in range(windows):
            part = pl.ds(SLOTS * w, SLOTS)
            d_four = four(dattn[SLOTS * w : SLOTS * (w + 1)])
            q_four = four(qs[tile, part, :].astype(F32))
            probs = pt[tile * windows + w]
            dprob = dot_nt(vs[tile, part, :], d_four)
            weighed = probs * dprob
            ds = weighed - probs * jnp.sum(weighed, axis=0, keepdims=True)
            total = total + ds
            dsb = ds.astype(BF)
            dvs[tile, part, :] = dot_nn(probs.astype(BF), d_four).astype(BF)
            dks[tile, part, :] = dot_nn(dsb, q_four).astype(BF)
            dqs[tile, part, :] = (
                fold(dot_tn(dsb, ks[tile, part, :])) * HEAD ** (-0.5)
            ).astype(BF)
        dbias[tile] = total
        for s, grads in enumerate((dqs, dks, dvs)):
            ga[s, cols, :] = dot_tn(grads[tile], normed).astype(BF)
            dh1[...] += dot_nn(grads[tile], wa[s, cols, :])
        sg[6:7, cols] = jnp.sum(dqs[tile].astype(F32), axis=0, keepdims=True)
        sg[7:8, cols] = jnp.sum(dvs[tile].astype(F32), axis=0, keepdims=True)
        return carry

    half_rows = width // 2
    halves = [pl.ds(0, half_rows), pl.ds(half_rows, half_rows)]

    def add_core(slot, part):
        add_to(ga.at[slot, part, my_cols], rca.at[slot, part, :])

    def reduce_core(half):
        part = halves[half]
        to_core_sum(ga.at[pl.ds(0, 3), part, her_cols], rca.at[pl.ds(0, 3), part, :], half)

    def reduce_x(half):
        part = halves[half]
        core_copies[1 + half].wait_recv()
        add_core(far, part)
        x_copies.append(
            send(
                ga.at[far, part, my_cols],
                rxa.at[part],
                sem_as.at[half, 1],
                sem_ar.at[half, 1],
                to_x,
            )
        )
        add_core(1, part)
        sum_key.scatter(half)
        add_core(near, part)

    lax.fori_loop(0, tiles_half, attend_back, 0)
    reduce_core(0)
    core_copies[0].wait_recv()
    add_core(3, slice(None))
    sum_proj.scatter(0)
    sum_proj.scatter(1)
    reduce_x(0)
    sum_fc2[0].start_z()
    lax.fori_loop(tiles_half, tiles, attend_back, 0)
    reduce_core(1)

    def mlp_out(slot):
        ph[slot] = dot_nn(ac[slot_rows(slot), :], wf[1]).astype(BF)

    def near_y(half):
        x_copies[half].wait_recv()
        add_to(ga.at[near, halves[half], my_cols], rxa.at[halves[half]])
        sum_near.scatter(half)

    out_copies = []
    sent(ph_c0)
    sent(ph_c1)
    mlp_out(xc_dl)
    out_copies.append(send(ph.at[xc_dl], rc_o.at[0], sem_hs.at[1, 0], sem_hr.at[1, 0], to_core))
    reduce_x(1)
    mlp_out(core_dl)
    out_copies.append(send(ph.at[core_dl], rc_o.at[1], sem_hs.at[1, 1], sem_hr.at[1, 1], to_core))
    mlp_out(x_dl)
    near_y(0)
    sum_fc2[0].middle()
    sum_fc2[1].start_y()

    dh1c = dot_nn(gather, dh1[...].astype(BF))
    n1 = n1s[...]
    sg[0:1, :] = jnp.sum(dh1c * n1, axis=0, keepdims=True)
    sg[1:2, :] = jnp.sum(dh1c, axis=0, keepdims=True)
    dn = norm_back(dh1c * flat_row(n1g_ref), n1, stats[:, 0:1])
    tgrad_ref[...] = (gs[...] + dn).astype(BF)[0:rows]

    back = one_hot(
        iota((LANES, PACK * TILE), 1)
        == TILE * (iota((LANES, 1), 0) >> 6)
        + (TILE - 1 - table_place(iota((LANES, 1), 0) & 63, False)),
        BF,
    )
    for tile in range(tiles):
        high, low = split_two(dbias[tile])
        wide = dot_nn(high, back) + dot_nn(low, back)
        for k in range(PACK):
            head = tile * PACK + k
            line = jnp.zeros((8, LANES), F32)
            for r in range(8):
                piece = wide[8 * r : 8 * (r + 1), TILE * k : TILE * (k + 1)]
                piece = jnp.concatenate([piece, jnp.zeros_like(piece)], axis=1)
                shift = LANES - 1 - CENTRE - (TILE - 1) + SPAN * r
                line = line + shear(piece, shift)
            row, spot = 12 + head // heads_here, LANES * (head % heads_here)
            sg[row : row + 1, spot : spot + LANES] = jnp.sum(line, axis=0, keepdims=True)

    last_small = 1 + z_count + groups

    def small_start(stage, ref, devices):
        cols = slice(None) if ref is sg else my_cols
        return ref, [sg_in.at[stage + k, :, cols] for k in range(len(devices))], [
            send(
                ref,
                sg_in.at[stage + k, :, cols],
                sem_ss.at[stage + k],
                sem_sr.at[stage + k],
                device,
            )
            for k, device in enumerate(devices)
        ]

    def small_end(started):
        ref, landings, copies = started
        for copy in copies:
            copy.wait_recv()
            sent(copy)
        total = ref[...]
        for landing in landings:
            total = total + landing[...]
        ref[...] = total

    def swap(ref, dst, index, device):
        return send(ref, dst, sem_fs.at[index], sem_fr.at[index], device)

    def over_groups(ref, landing, index):
        for step in range(1, groups):
            k = index * (groups - 1) + step - 1
            copy = send(ref, landing.at[step - 1], sem_gs.at[k], sem_gr.at[k], to_group(step))
            copy.wait_recv()
            sent(copy)
        if groups > 1:
            add_to(ref, *[landing.at[step - 1] for step in range(1, groups)])

    final = {}

    def finish(which, parts):
        for part, cols in zip(parts, (left_cols, right_cols), strict=True):
            fin[which, mine, :, cols] = part.total()[...]
        slot = fin.at[which, mine]
        over_groups(slot, group_m.at[which], which)
        final[which, 0] = swap(slot, slot, 3 * which, to_x)
        final[which, 1] = swap(slot, slot, 3 * which + 1, to_core)

    def finish_core(which):
        final[which, 0].wait_recv()
        slot = fin.at[which, x_dl]
        final[which, 2] = swap(slot, slot, 3 * which + 2, to_core)

    def finish_out(which):
        final[which, 1].wait_recv()
        final[which, 2].wait_recv()
        fin_ref[1 + which] = fin[which]

    def share_x(k, slot, part):
        fin_a[slot, :, my_cols] = part.total()[...]
        final[2, k] = swap(fin_a.at[slot, :, my_cols], fin_x.at[k], 6 + k, to_x)

    def shared_x(k, slot):
        final[2, k].wait_recv()
        sent(final[2, k])
        ref = fin_a.at[slot, :, my_cols]
        add_to(ref, fin_x.at[k])
        over_groups(ref, group_a.at[k], 2 + k)

    smalls = small_start(0, sg, [to_core])
    for part in sum_fc1:
        part.start_z()
    near_y(1)
    small_end(smalls)
    smalls = small_start(1, sg, [to_x])
    out_copies[0].wait_recv()
    ph2[1] = (ph[x_dl].astype(F32) + rc_o[0].astype(F32)).astype(BF)
    out_copies.append(send(ph2.at[1], rx_o, sem_hs.at[1, 2], sem_hr.at[1, 2], to_x))
    mlp_out(mine)
    small_end(smalls)
    sg_half = sg.at[:, my_cols]
    smalls = small_start(2, sg_half, [to_y])
    sum_proj.start_z()
    for part in sum_fc1:
        part.middle()
    finish(1, sum_fc2)
    small_end(smalls)
    smalls = small_start(3, sg_half, [to_z(step) for step in range(1, z_count)])
    sum_key.start_z()
    sum_proj.middle()
    finish(0, sum_fc1)
    finish_core(1)

    out_copies[1].wait_recv()
    out_copies[2].wait_recv()
    branch = ph[mine].astype(F32) + rc_o[1].astype(F32) + rx_o[...].astype(F32)
    out_ref[...] = (x1s[...] + (branch + flat_row(f2b_ref)) * row_live).astype(BF)[0:rows]

    sum_key.middle()
    small_end(smalls)
    if groups > 1:
        small_end(
            small_start(
                2 + z_count, sg_half, [to_group(step) for step in range(1, groups)]
            )
        )
    small_last = send(
        sg_half,
        sg_in.at[last_small, :, my_cols],
        sem_ss.at[last_small],
        sem_sr.at[last_small],
        to_core,
    )
    sum_near.start_z()
    share_x(0, 3, sum_proj)
    finish_core(0)
    sum_near.middle()
    share_x(1, 1, sum_key)
    small_last.wait_recv()
    sg[:, her_cols] = sg_in[last_small, :, her_cols]
    finish_out(1)
    shared_x(0, 3)

    vec_ref[...] = sg[0:8, :]
    pick = one_hot(iota((width, block), 0) == block * mp + iota((width, block), 1), F32)
    small_ref[0:8, 0:block] = dot_nn(sg[0:8, :], pick, HIGHEST)
    wide_lane = iota((width, hidden), 1)
    pick = one_hot(
        iota((width, hidden), 0)
        == block * mp + wide_lane - block * steps_of(wide_lane, block, hidden // block),
        F32,
    )
    lines = dot_nn(sg[8:16, :], pick, HIGHEST)
    keep = iota((8, hidden), 0) == steps_of(iota((8, hidden), 1), block, hidden // block)
    small_ref[8:9, :] = jnp.sum(jnp.where(keep, lines, 0.0), axis=0, keepdims=True)
    table = sg[pl.ds(12 + mp, 1), :]
    table = jnp.concatenate(
        [table[:, LANES * k : LANES * (k + 1)] for k in range(heads_here)]
        + [jnp.zeros((8 - heads_here, LANES), F32)],
        axis=0,
    )
    turn = one_hot(iota((LANES, LANES), 0) + iota((LANES, LANES), 1) == LANES - 1, F32)
    small_ref[16:24, 0:LANES] = dot_nn(table, turn, HIGHEST)

    finish_out(0)
    shared_x(1, 1)
    fin_a[near, :, my_cols] = sum_near.total()[...]
    slot = fin_a.at[near, :, my_cols]
    over_groups(slot, group_a.at[2], 4)
    near_x = swap(slot, slot, 8, to_x)
    near_x.wait_recv()
    slots = fin_a.at[:, :, my_cols]
    swap(slots, slots, 9, to_core).wait_recv()
    fin_ref[0] = fin_a[...]

    for copy, when in pending:
        if when is None:
            copy.wait_send()
        else:
            pl.when(when)(copy.wait_send)


def unpack(
    out_in,
    tgrad_in,
    vec_in,
    small_in,
    fin_in,
    out_ref,
    tgrad_ref,
    n1g_ref,
    n1b_ref,
    qkvg_ref,
    qvg_ref,
    relg_ref,
    projg_ref,
    pbg_ref,
    n2g_ref,
    n2b_ref,
    f1g_ref,
    f1bg_ref,
    f2g_ref,
    f2bg_ref,
):
    hidden, width = f2g_ref.shape
    out_ref[...] = out_in[...]
    tgrad_ref[...] = tgrad_in[...]
    for k, ref in enumerate((n1g_ref, n1b_ref, pbg_ref, n2g_ref, n2b_ref, f2bg_ref)):
        ref[...] = vec_in[k : k + 1, :].reshape(width)
    for s in range(3):
        qkvg_ref[s] = fin_in[0, s].astype(F32)
    projg_ref[...] = fin_in[0, 3].astype(F32)
    f1g_ref[...] = fin_in[1].reshape(hidden, width).astype(F32).T
    f2g_ref[...] = fin_in[2].reshape(hidden, width).astype(F32)
    qvg_ref[...] = small_in[6:8, 0 : qvg_ref.shape[1]]
    f1bg_ref[...] = small_in[8:9, :].reshape(hidden)
    relg_ref[...] = small_in[16 : 16 + relg_ref.shape[0], 0:ENTRIES]


def solution(mesh):
    n_dp, n_mp = mesh.shape["dp"], mesh.shape["mp"]

    def shards(
        tokens,
        crop_kind,
        norm1_gain,
        norm1_bias,
        qkv_weight,
        qv_bias,
        rel_table,
        proj_weight,
        proj_bias,
        norm2_gain,
        norm2_bias,
        fc1_weight,
        fc1_bias,
        fc2_weight,
        fc2_bias,
        out_grad,
    ):
        rows, width = tokens.shape
        windows = rows // WIN
        padded = -(-rows // 16) * 16
        block = proj_weight.shape[0]
        hidden = fc2_weight.shape[0]
        heads_here = rel_table.shape[1]
        places = SLOTS * windows
        tiles = width // TILE
        z_count = n_mp // 2
        groups = n_dp // GROUP
        dims = (n_dp, n_mp, rows, windows, padded, width, block, hidden)

        def full(*shape):
            return jax.ShapeDtypeStruct(shape, F32)

        vmem = pl.BlockSpec(memory_space=pltpu.VMEM)
        dma = pltpu.SemaphoreType.DMA
        results = pl.pallas_call(
            functools.partial(body, dims),
            out_shape=[
                jax.ShapeDtypeStruct((rows, width), BF),
                jax.ShapeDtypeStruct((rows, width), BF),
                full(8, width),
                full(24, hidden),
                jax.ShapeDtypeStruct((3, GROUP, block, width), BF),
            ],
            in_specs=[pl.BlockSpec(memory_space=pltpu.SMEM)] + [vmem] * 15,
            out_specs=[vmem] * 5,
            scratch_shapes=[
                pltpu.VMEM((GROUP, width, width), BF),
                pltpu.VMEM((2, width, width), BF),
                pltpu.VMEM((hidden, width), BF),
                pltpu.VMEM((n_mp, 8, hidden), F32),
                pltpu.VMEM((8, hidden), F32),
                pltpu.VMEM((padded, width), F32),
                pltpu.VMEM((padded, width), F32),
                pltpu.VMEM((padded, width), F32),
                pltpu.VMEM((padded, width), F32),
                pltpu.VMEM((padded, TILE), F32),
                pltpu.VMEM((8, width), F32),
                pltpu.VMEM((8, width), F32),
                pltpu.VMEM((places, width), BF),
                pltpu.VMEM((tiles, places, TILE), BF),
                pltpu.VMEM((tiles, places, TILE), BF),
                pltpu.VMEM((tiles, places, TILE), BF),
                pltpu.VMEM((tiles, places, TILE), BF),
                pltpu.VMEM((tiles * windows, SLOTS, LANES), F32),
                pltpu.VMEM((tiles, SLOTS, LANES), F32),
                pltpu.VMEM((tiles, SLOTS, LANES), F32),
                pltpu.VMEM((GROUP, padded, width), BF),
                pltpu.VMEM((GROUP, padded, width), BF),
                pltpu.VMEM((GROUP * padded, width), BF),
                pltpu.VMEM((GROUP * padded, width), BF),
                pltpu.VMEM((GROUP, padded, width), BF),
                pltpu.VMEM((2, padded, width), BF),
                pltpu.VMEM((padded, width), BF),
                pltpu.VMEM((2, padded, width), BF),
                pltpu.VMEM((2, padded, width), BF),
                pltpu.VMEM((padded, width), BF),
                pltpu.VMEM((places, width), BF),
                pltpu.VMEM((tiles, places, TILE), BF),
                pltpu.VMEM((tiles, places, TILE), BF),
                pltpu.VMEM((tiles, places, TILE), BF),
                pltpu.VMEM((tiles, SLOTS, LANES), F32),
                pltpu.VMEM((places, width), F32),
                pltpu.VMEM((GROUP, width, width), BF),
                pltpu.VMEM((2, width, width), BF),
                pltpu.VMEM((GROUP, width, width // 2), BF),
                pltpu.VMEM((width, width // 2), BF),
                pltpu.VMEM((7, z_count, block, width // 2), BF),
                pltpu.VMEM((8, z_count - 1, block, width // 2), BF),
                pltpu.VMEM((8, block, width // 2), BF),
                pltpu.VMEM((2, GROUP, block, width), BF),
                pltpu.VMEM((GROUP, block, width), BF),
                pltpu.VMEM((2, block, width // 2), BF),
                pltpu.VMEM((2, max(groups - 1, 1), block, width), BF),
                pltpu.VMEM((3, max(groups - 1, 1), block, width // 2), BF),
                pltpu.VMEM((24, width), F32),
                pltpu.VMEM((2 + z_count + groups, 24, width), F32),
                dma((7, 2 * z_count + 1)),
                dma((7, 2 * z_count + 1)),
                dma((2 * n_mp + 4,)),
                dma((2 * n_mp + 4,)),
                dma((2, 3)),
                dma((2, 3)),
                dma((2, 3)),
                dma((2, 3)),
                dma((3, 2)),
                dma((3, 2)),
                dma((7, z_count)),
                dma((7, z_count)),
                dma((8, 4)),
                dma((8, 4)),
                dma((10,)),
                dma((10,)),
                dma((2 + z_count + groups,)),
                dma((2 + z_count + groups,)),
                dma((5 * max(groups - 1, 1),)),
                dma((5 * max(groups - 1, 1),)),
            ],
            compiler_params=pltpu.CompilerParams(
                collective_id=0, has_side_effects=True, vmem_limit_bytes=63 * 2**20
            ),
        )(
            crop_kind,
            tokens,
            out_grad,
            norm1_gain,
            norm1_bias,
            jnp.swapaxes(qkv_weight, 1, 2),
            qv_bias,
            rel_table.T,
            proj_weight,
            proj_bias,
            norm2_gain,
            norm2_bias,
            fc1_weight,
            fc1_bias,
            fc2_weight,
            fc2_bias,
        )
        results = pl.pallas_call(
            unpack,
            out_shape=[
                jax.ShapeDtypeStruct((rows, width), BF),
                jax.ShapeDtypeStruct((rows, width), BF),
                full(width),
                full(width),
                full(3, block, width),
                full(2, block),
                full(heads_here, ENTRIES),
                full(block, width),
                full(width),
                full(width),
                full(width),
                full(width, hidden),
                full(hidden),
                full(hidden, width),
                full(width),
            ],
            in_specs=[vmem] * 5,
            out_specs=[vmem] * 15,
        )(*results)
        results = list(results)
        results[4] = jnp.swapaxes(results[4], 1, 2)
        results[6] = results[6].T
        return tuple(results)

    in_specs = (
        P(("dp", "mp"), None),
        P("dp"),
        P(),
        P(),
        P(None, None, "mp"),
        P(None, "mp"),
        P(None, "mp"),
        P("mp", None),
        P(),
        P(),
        P(),
        P(None, "mp"),
        P("mp"),
        P("mp", None),
        P(),
        P(("dp", "mp"), None),
    )
    out_specs = (
        P(("dp", "mp"), None),
        P(("dp", "mp"), None),
        P(),
        P(),
        P(None, None, "mp"),
        P(None, "mp"),
        P(None, "mp"),
        P("mp", None),
        P(),
        P(),
        P(),
        P(None, "mp"),
        P("mp"),
        P("mp", None),
        P(),
    )
    return jax.shard_map(shards, mesh=mesh, in_specs=in_specs, out_specs=out_specs, check_vma=False)
```

```python
import functools

import jax
import jax.numpy as jnp
from jax import lax
from jax.experimental import pallas as pl
from jax.experimental.pallas import tpu as pltpu
from jax.sharding import PartitionSpec as P

HEAD = 32
SIDE = 7
LOCAL_SIDE = 3
WIN = 49
SPAN = 2 * SIDE - 1
ENTRIES = SPAN * SPAN
CENTRE = (SIDE - 1) * SPAN + SIDE - 1
SLOTS = 64
TILE = 128
PACK = 4
GROUP = 4
LANES = 256
EPSILON = 1e-05
NEG_FILL = -1000000000.0
GELU_A = 0.7978845608028654
GELU_B = 0.044715
HIGHEST = lax.Precision.HIGHEST
MESH = pl.DeviceIdType.MESH
BF = jnp.bfloat16
F32 = jnp.float32


def dot(left, right, dims, precision=None):
    return lax.dot_general(
        left, right, (dims, ((), ())), preferred_element_type=F32, precision=precision
    )


def dot_nn(left, right, precision=None):
    return dot(left, right, ((1,), (0,)), precision)


def dot_nt(left, right, precision=None):
    return dot(left, right, ((1,), (1,)), precision)


def dot_tn(left, right, precision=None):
    return dot(left, right, ((0,), (0,)), precision)


def iota(shape, axis):
    return lax.broadcasted_iota(jnp.int32, shape, axis)


def one_hot(cond, dtype):
    return jnp.where(cond, 1.0, 0.0).astype(dtype)


def steps_of(values, width, count):
    total = jnp.zeros_like(values)
    for step in range(1, count):
        total = total + jnp.where(values >= step * width, 1, 0)
    return total


def shear(values, shift):
    moved = pltpu.roll(values, shift, axis=1)
    return pltpu.roll(moved, 0, axis=1, stride=1, stride_axis=0)


def split_two(values):
    high = values.astype(BF)
    return high, (values - high.astype(F32)).astype(BF)


def flat_row(ref):
    return ref[...].reshape(1, -1)


def norm_parts(values):
    mean = jnp.mean(values, axis=-1, keepdims=True)
    centre = values - mean
    spread = jnp.mean(centre * centre, axis=-1, keepdims=True)
    scale = lax.rsqrt(spread + EPSILON)
    return centre * scale, scale


def norm_back(grad_normed, normed, scale):
    return scale * (
        grad_normed
        - jnp.mean(grad_normed, axis=-1, keepdims=True)
        - normed * jnp.mean(grad_normed * normed, axis=-1, keepdims=True)
    )


def slot_place(columns, windows, kinds):
    window = steps_of(columns, WIN, windows)
    slot = columns - WIN * window
    kind = jnp.zeros_like(columns)
    for w in range(windows):
        kind = jnp.where(window == w, kinds[w], kind)
    whole = slot + steps_of(slot, SIDE, SIDE)
    corner = slot + (8 - LOCAL_SIDE) * steps_of(slot, LOCAL_SIDE, LOCAL_SIDE)
    rest = slot + (8 * LOCAL_SIDE - LOCAL_SIDE * LOCAL_SIDE)
    local = jnp.where(slot < LOCAL_SIDE * LOCAL_SIDE, corner, rest)
    place = SLOTS * window + jnp.where(kind == 0, whole, local)
    live = jnp.where(kind == 0, WIN, LOCAL_SIDE * LOCAL_SIDE)
    inside = columns < WIN * windows
    return jnp.where(inside, place, -1), inside & (slot < live)


def body(
    dims,
    kind_ref,
    tok_ref,
    og_ref,
    n1g_ref,
    n1b_ref,
    qkvw_ref,
    qvb_ref,
    tab_ref,
    pw_ref,
    pb_ref,
    n2g_ref,
    n2b_ref,
    f1w_ref,
    f1b_ref,
    f2w_ref,
    f2b_ref,
    out_ref,
    tgrad_ref,
    vec_ref,
    small_ref,
    fin_ref,
    wa,
    wf,
    ft,
    sp,
    pk,
    xs,
    x1s,
    n1s,
    gs,
    stats,
    qb,
    fb,
    h1p,
    qs,
    ks,
    vs,
    at,
    pt,
    bias_whole,
    bias_local,
    hg,
    gg,
    ac,
    dp_s,
    ph,
    rc_h,
    rx_h,
    ph2,
    rc_o,
    rx_o,
    gabp,
    dqs,
    dks,
    dvs,
    dbias,
    dh1,
    ga,
    gf,
    rca,
    rxa,
    ry,
    rz,
    rr,
    fin,
    fin_a,
    fin_x,
    group_m,
    group_a,
    sg,
    sg_in,
    sem_ws,
    sem_wr,
    sem_bs,
    sem_br,
    sem_rs,
    sem_rr,
    sem_hs,
    sem_hr,
    sem_as,
    sem_ar,
    sem_ys,
    sem_yr,
    sem_zs,
    sem_zr,
    sem_fs,
    sem_fr,
    sem_ss,
    sem_sr,
    sem_gs,
    sem_gr,
):
    n_dp, n_mp, rows, windows, padded, width, block, hidden = dims
    groups = n_dp // GROUP
    places = SLOTS * windows
    z_count = n_mp // 2
    heads_here = block // HEAD
    tiles = width // TILE
    half_width = width // 2
    mp = lax.axis_index("mp")
    dp = lax.axis_index("dp")
    z = mp // 2
    y = mp % 2
    base = (dp // GROUP) * GROUP
    mine = dp % GROUP
    x = mine // 2
    c = mine % 2
    core_dl = x * 2 + (1 - c)
    x_dl = (1 - x) * 2 + c
    xc_dl = (1 - x) * 2 + (1 - c)
    to_core = (base + core_dl, mp)
    to_x = (base + x_dl, mp)
    to_y = (dp, z * 2 + (1 - y))
    near = 2 * x
    far = 2 - 2 * x

    def z_at(step):
        return (z + step) % z_count

    def to_z(step):
        return (dp, z_at(step) * 2 + y)

    def to_group(step):
        return ((dp + GROUP * step) % n_dp, mp)

    pending = []

    def remote(src, dst, s_sem, r_sem, device):
        return pltpu.make_async_remote_copy(
            src_ref=src,
            dst_ref=dst,
            send_sem=s_sem,
            recv_sem=r_sem,
            device_id=device,
            device_id_type=MESH,
        )

    def send(src, dst, s_sem, r_sem, device, when=None):
        copy = remote(src, dst, s_sem, r_sem, device)
        if when is None:
            copy.start()
        else:
            pl.when(when)(copy.start)
        pending.append((copy, when))
        return copy

    def forget(copy):
        pending[:] = [other for other in pending if other[0] is not copy]

    def sent(copy):
        copy.wait_send()
        forget(copy)

    barrier = pltpu.get_barrier_semaphore()
    peers = [to_core, to_x, to_y]
    peers += [to_z(step) for step in range(1, z_count)]
    peers += [to_group(step) for step in range(1, groups)]
    for peer in peers:
        pl.semaphore_signal(barrier, inc=1, device_id=peer, device_id_type=MESH)

    own = pl.ds(pl.multiple_of(block * mp, 16), block)
    my_cols = pl.ds(pl.multiple_of(half_width * c, TILE), half_width)
    her_cols = pl.ds(pl.multiple_of(half_width * (1 - c), TILE), half_width)
    for s in range(3):
        wa[s, own, my_cols] = qkvw_ref[s, :, my_cols]
    wa[3, own, my_cols] = pw_ref[:, my_cols]

    pk[...] = jnp.zeros_like(pk)
    pk[0:heads_here, 0:ENTRIES] = tab_ref[...]
    pk[3:5, 0:block] = qvb_ref[...]
    pk[5:6, :] = flat_row(f1b_ref)
    sp[mp] = pk[...]

    pl.semaphore_wait(barrier, len(peers))

    def rows_of(other_z, other_y):
        return pl.ds(pl.multiple_of(block * (other_z * 2 + other_y), 16), block)

    relayed = z_count == 4
    if relayed:
        order = [2, jnp.where(z == 0, 3, 1), jnp.where(z == 0, 1, 3)]
    else:
        order = list(range(1, z_count))
    inner = (z == 1) | (z == 2)

    def spread_z(buffer, part, index, first):
        ref = buffer.at[part]
        for step in range(1, z_count):
            far_end = {1: z != 3, 2: None, 3: z != 0}[step] if relayed else None
            k = first + step - 1
            send(ref, ref, sem_ws.at[index, k], sem_wr.at[index, k], to_z(step), far_end)

    def arrived_z(buffer, part_of, index, first, place):
        step = order[place]
        part = part_of((z + z_count - step) % z_count)
        ref = buffer.at[part]
        k = first + step - 1
        remote(ref, ref, sem_ws.at[index, k], sem_wr.at[index, k], to_y).wait_recv()
        if relayed and place == 0:
            last = 2 * (z - 1)
            send(
                ref,
                ref,
                sem_ws.at[index, first + 3],
                sem_wr.at[index, first + last],
                (dp, 3 * (z - 1) * 2 + y),
                inner,
            )
        return part

    class Gather:
        def __init__(self, index, buffer, part):
            self.index, self.buffer, self.part = index, buffer, part

        def forward_y(self, part, step):
            k = z_count + step
            ref = self.buffer.at[part]
            send(ref, ref, sem_ws.at[self.index, k], sem_wr.at[self.index, k], to_y)

        def start_y(self):
            self.forward_y(self.part(z, y), 0)

        def start_z(self):
            spread_z(self.buffer, self.part(z, y), self.index, 0)

        def arrive_z(self, place):
            part = arrived_z(self.buffer, lambda oz: self.part(oz, y), self.index, 0, place)
            self.forward_y(part, order[place])
            return part

        def arrive_y(self, place):
            step = 0 if place == 0 else order[place - 1]
            part = self.part((z + z_count - step) % z_count, 1 - y)
            ref = self.buffer.at[part]
            k = z_count + step
            remote(ref, ref, sem_ws.at[self.index, k], sem_wr.at[self.index, k], to_y).wait_recv()
            return part

    class GatherLong:
        def __init__(self, index, buffer, part):
            self.index, self.buffer, self.part = index, buffer, part

        def pair(self):
            ref = self.buffer.at[self.part(z, y)]
            k = 2 * z_count
            return ref, ref, sem_ws.at[self.index, k], sem_wr.at[self.index, k], to_y

        def start_y(self):
            send(*self.pair())

        def start_z(self):
            spread_z(self.buffer, self.part(z, y), self.index, 0)

        def arrive_y(self):
            remote(*self.pair()).wait_recv()
            spread_z(self.buffer, self.part(z, 1 - y), self.index, z_count)

        def arrive_z(self, place):
            for column in range(2):
                other_y = y if column == 0 else 1 - y
                arrived_z(
                    self.buffer,
                    lambda oz: self.part(oz, other_y),
                    self.index,
                    z_count * column,
                    place,
                )

    def half_block(other_z, other_y):
        return rows_of(other_z, other_y), my_cols

    def whole_block(other_z, other_y):
        return (rows_of(other_z, other_y),)

    def quarter_block(other_z, other_y):
        start = block * (other_z * 2 + other_y) + (block // 2) * x
        return pl.ds(pl.multiple_of(start, 16), block // 2), my_cols

    def left_block(other_z, other_y):
        return rows_of(other_z, other_y), pl.ds(0, half_width)

    def right_block(other_z, other_y):
        return rows_of(other_z, other_y), pl.ds(half_width, half_width)

    small = Gather(0, sp, lambda oz, oy: (oz * 2 + oy,))
    near_w = Gather(1, wa.at[near], half_block)
    key_w = Gather(2, wa.at[1], half_block)
    proj_w = Gather(3, wa.at[3], quarter_block)
    fc1_w = Gather(4, wf.at[0], whole_block)
    fc2_w = Gather(5, wf.at[1], left_block)
    fc2_long = GatherLong(6, wf.at[1], right_block)
    later_z, later_y = range(z_count - 1), range(1, z_count)

    for part in (near_w, key_w, proj_w, small):
        part.start_z()
        part.start_y()
    ft[...] = f1w_ref[...].T
    quarter = pl.ds(pl.multiple_of(block * mine, 16), block)
    wf[0, own, :] = ft[quarter, :]
    wf[1, own, :] = f2w_ref[quarter, :]

    def send_rows(ring, index, slot, device, k):
        return send(ring.at[slot], ring.at[slot], sem_rs.at[index, k], sem_rr.at[index, k], device)

    kinds = [kind_ref[mp * windows + w] for w in range(windows)]
    place_row, _ = slot_place(iota((1, padded), 1), windows, kinds)
    place_col, live_col = slot_place(iota((padded, 1), 0), windows, kinds)
    spread = one_hot(iota((places, padded), 0) == place_row, BF)
    gather = one_hot(iota((padded, places), 1) == place_col, BF)
    row_live = jnp.where(live_col, 1.0, 0.0)

    gs[...] = jnp.zeros_like(gs)
    gs[0:rows, :] = og_ref[...].astype(F32)
    sg[...] = jnp.zeros_like(sg)
    masked = gs[...] * row_live
    gg[mine] = masked.astype(BF)
    gg_c0 = send_rows(gg, 0, mine, to_core, 1)
    sg[5:6, :] = jnp.sum(masked, axis=0, keepdims=True)

    xs[...] = jnp.zeros_like(xs)
    xs[0:rows, :] = tok_ref[...].astype(F32)
    normed_one, scale_one = norm_parts(xs[...])
    n1s[...] = normed_one
    stats[:, 0:1] = scale_one
    h1 = (normed_one * flat_row(n1g_ref) + flat_row(n1b_ref)).astype(BF)
    h1p[...] = dot_nn(spread, h1).astype(BF)

    along_x, proj_x = [], []

    def forward_x(part):
        k = len(along_x)
        ref = wa.at[near].at[part]
        along_x.append(send(ref, ref, sem_bs.at[k], sem_br.at[k], to_x))

    def forward_proj(part):
        k = n_mp + 4 + len(proj_x)
        ref = wa.at[3].at[part]
        proj_x.append(send(ref, ref, sem_bs.at[k], sem_br.at[k], to_x))

    forward_x(near_w.arrive_y(0))

    def core_half(index, slot):
        ref = wa.at[slot, :, my_cols]
        return send(ref, ref, sem_bs.at[n_mp + index], sem_br.at[n_mp + index], to_core)

    forward_x(near_w.arrive_z(0))
    fc1_w.start_z()
    for place in later_z[1:]:
        forward_x(near_w.arrive_z(place))
    for place in later_z:
        key_w.arrive_z(place)
        forward_proj(proj_w.arrive_z(place))
    for part in (fc1_w, fc2_w, fc2_long):
        part.start_y()
    for place in later_z:
        small.arrive_z(place)
    for place in later_y:
        forward_x(near_w.arrive_y(place))
    fc1_w.arrive_z(0)
    fc2_w.start_z()
    for place in range(z_count):
        forward_proj(proj_w.arrive_y(place))
    gg_x = send_rows(gg, 0, mine, to_x, 0)
    fc2_long.arrive_y()
    fc2_long.start_z()
    for place in later_z[1:]:
        fc1_w.arrive_z(place)
    for place in range(z_count):
        key_w.arrive_y(place)
    core_near = core_half(0, near)
    core_key = core_half(1, 1)
    for place in range(z_count):
        small.arrive_y(place)
    lane = iota((1, width), 1)
    owner = steps_of(lane, block, n_mp)
    within = lane - block * owner
    pick_row = iota((n_mp, width), 0) == owner
    spots = iota((hidden, width), 0)

    def spread_row(row, offset):
        picked = dot_nn(sp[:, row, :], one_hot(spots == within + offset, F32), HIGHEST)
        return jnp.sum(jnp.where(pick_row, picked, 0.0), axis=0, keepdims=True)

    qb[0:1, :] = spread_row(3, 0)
    qb[1:2, :] = spread_row(4, 0)
    fb[0:1, :] = spread_row(5, block * mine)

    def table_place(cells, local):
        row, column = cells >> 3, cells & 7
        spot = SPAN * row + column
        if local:
            last = LOCAL_SIDE - 1
            dead = (row > last) | (column > last)
            spot = jnp.where(dead, SPAN * last + last, spot)
        return spot

    cell = iota((1, LANES), 1)
    cell_head, cell_spot = cell >> 6, cell & 63
    source = iota((PACK * TILE, LANES), 0)
    picks = []
    for local in (False, True):
        picks.append(one_hot(source == TILE * cell_head + table_place(cell_spot, local), BF))

    def bias_of(tile):
        shifted = []
        for k in range(PACK):
            head = tile * PACK + k
            line = sp[head // heads_here, head % heads_here : head % heads_here + 1, 0:LANES]
            line = jnp.broadcast_to(line, (8, LANES))
            shifted.append(
                jnp.concatenate(
                    [
                        shear(line, (SPAN * r - CENTRE) % LANES)[:, 0:TILE]
                        for r in range(8)
                    ],
                    axis=0,
                )
            )
        high, low = split_two(jnp.concatenate(shifted, axis=1))
        bias_whole[tile] = dot_nn(high, picks[0]) + dot_nn(low, picks[0])
        bias_local[tile] = dot_nn(high, picks[1]) + dot_nn(low, picks[1])

    for tile in range(tiles):
        bias_of(tile)
    for copy in along_x:
        copy.wait_recv()
    core_far = core_half(2, far)
    core_near.wait_recv()
    core_key.wait_recv()
    core_far.wait_recv()

    head_lane = iota((PACK * SLOTS, TILE), 1) >> 5
    head_mask = (iota((PACK * SLOTS, TILE), 0) >> 6) == head_lane
    key_place = iota((SLOTS, 1), 0)
    key_row, key_col = key_place >> 3, key_place & 7
    usable = []
    for w in range(windows):
        side = jnp.where(kinds[w] == 0, SIDE, LOCAL_SIDE)
        usable.append((key_row < side) & (key_col < side))

    def four(values):
        return jnp.where(head_mask, jnp.concatenate([values] * PACK, axis=0), 0.0).astype(BF)

    def fold(values):
        picked = jnp.where(head_mask, values, 0.0)
        total = picked[0:SLOTS]
        for k in range(1, PACK):
            total = total + picked[SLOTS * k : SLOTS * (k + 1)]
        return total

    def attend(tile, carry):
        cols = pl.ds(pl.multiple_of(tile * TILE, TILE), TILE)
        normed = h1p[...]
        q_tile = (dot_nt(normed, wa[0, cols, :]) + qb[0:1, cols]) * HEAD ** (-0.5)
        qs[tile] = q_tile.astype(BF)
        ks[tile] = dot_nt(normed, wa[1, cols, :]).astype(BF)
        vs[tile] = (dot_nt(normed, wa[2, cols, :]) + qb[1:2, cols]).astype(BF)
        for w in range(windows):
            part = pl.ds(SLOTS * w, SLOTS)
            scores = dot_nt(ks[tile, part, :], four(qs[tile, part, :].astype(F32)))
            bias = jnp.where(kinds[w] == 0, bias_whole[tile], bias_local[tile])
            scores = jnp.where(usable[w], scores + bias, NEG_FILL)
            raised = jnp.exp(scores - jnp.max(scores, axis=0, keepdims=True))
            probs = raised / jnp.sum(raised, axis=0, keepdims=True)
            pt[tile * windows + w] = probs
            at[tile, part, :] = fold(dot_tn(probs.astype(BF), vs[tile, part, :])).astype(BF)
        return carry

    third = tiles // 3
    lax.fori_loop(0, third, attend, 0)
    for place in later_z:
        fc2_w.arrive_z(place)
    gg_x.wait_recv()
    gg_c1 = send_rows(gg, 0, x_dl, to_core, 2)
    lax.fori_loop(third, 2 * third, attend, 0)
    for copy in proj_x:
        copy.wait_recv()
    core_proj = core_half(3, 3)
    lax.fori_loop(2 * third, tiles, attend, 0)
    core_proj.wait_recv()

    attn = jnp.concatenate(
        [dot_nn(gather, at[tile]).astype(BF) for tile in range(tiles)], axis=1
    )
    x1 = xs[...] + (dot_nn(attn, wa[3]) + flat_row(pb_ref)) * row_live
    x1s[...] = x1
    normed_two, scale_two = norm_parts(x1)
    hg[mine] = (normed_two * flat_row(n2g_ref) + flat_row(n2b_ref)).astype(BF)
    hg_x = send_rows(hg, 1, mine, to_x, 0)
    hg_c0 = send_rows(hg, 1, mine, to_core, 1)

    for place in later_z:
        fc2_long.arrive_z(place)
    for place in range(z_count):
        fc1_w.arrive_y(place)
    for place in range(z_count):
        fc2_w.arrive_y(place)

    def slot_rows(slot):
        return pl.ds(pl.multiple_of(padded * slot, 16), padded)

    def mlp(slot):
        pre = dot_nt(hg[slot], wf[0]) + fb[0:1, :]
        square = pre * pre
        bend = jnp.tanh(GELU_A * (pre + GELU_B * (square * pre)))
        ac[slot_rows(slot), :] = (0.5 * pre * (1.0 + bend)).astype(BF)
        slope = 0.5 * (1.0 + bend) + 0.5 * pre * (1.0 - bend * bend) * (
            GELU_A * (1.0 + 3.0 * GELU_B * square)
        )
        dpre = (dot_nt(gg[slot], wf[1]) * slope).astype(BF)
        dp_s[slot_rows(slot), :] = dpre
        ph[slot] = dot_nn(dpre, wf[0]).astype(BF)

    mlp(mine)
    gg_c0.wait_recv()
    hg_c0.wait_recv()
    hg_x.wait_recv()
    hg_c1 = send_rows(hg, 1, x_dl, to_core, 2)
    mlp(core_dl)
    ph_c1 = send(ph.at[core_dl], rc_h.at[1], sem_hs.at[0, 1], sem_hr.at[0, 1], to_core)
    gg_c1.wait_recv()
    hg_c1.wait_recv()
    mlp(xc_dl)
    ph_c0 = send(ph.at[xc_dl], rc_h.at[0], sem_hs.at[0, 0], sem_hr.at[0, 0], to_core)
    mlp(x_dl)
    ph_c0.wait_recv()
    ph2[0] = (ph[x_dl].astype(F32) + rc_h[0].astype(F32)).astype(BF)
    ph_x = send(ph2.at[0], rx_h, sem_hs.at[0, 2], sem_hr.at[0, 2], to_x)

    tiles_half = tiles // 2
    z_half = z_count // 2

    def add_to(ref, *others):
        total = ref[...].astype(F32)
        for other in others:
            total = total + other[...].astype(F32)
        ref[...] = total.astype(BF)

    class Line:
        def __init__(self, index, part, relay):
            self.index, self.part = index, part
            self.relay = relay and relayed

        def recv(self, step):
            return rz.at[self.index, step - 1]

        def sems(self, k, r):
            return sem_zs.at[self.index, k], sem_zr.at[self.index, r]

        def over(self):
            return remote(
                self.part(z_count - 1 - z),
                rr.at[self.index],
                *self.sems(3, 3),
                (dp, (1 + z // 3) * 2 + y),
            )

        def far(self):
            return remote(self.part(z_at(2)), self.recv(2), *self.sems(1, 1), to_z(2))

        def start(self):
            if not self.relay:
                for step in range(1, z_count):
                    send(
                        self.part(z_at(step)),
                        self.recv(step),
                        *self.sems(step - 1, step - 1),
                        to_z(step),
                    )
                return
            outer = jnp.logical_not(inner)
            copy = self.over()
            pl.when(outer)(copy.start)
            pending.append((copy, outer))
            for step, when in ((1, z != 3), (3, z != 0)):
                send(
                    self.part(z_at(step)),
                    self.recv(step),
                    *self.sems(step - 1, step - 1),
                    to_z(step),
                    when,
                )
            pl.when(outer)(self.far().start)

        def middle(self):
            if self.relay:

                @pl.when(inner)
                def _():
                    self.over().wait_recv()
                    add_to(self.part(z_at(2)), rr.at[self.index])
                    self.far().start()

                pending.append((self.far(), None))

        def total(self):
            whens = [z != 0, None, z != z_count - 1] if self.relay else [None] * (z_count - 1)
            ref = self.part(z)
            for step in range(1, z_count):
                copy = remote(ref, self.recv(step), *self.sems(step - 1, step - 1), to_y)

                def take(copy=copy, step=step):
                    copy.wait_recv()
                    add_to(ref, self.recv(step))

                if whens[step - 1] is None:
                    take()
                else:
                    pl.when(whens[step - 1])(take)
            return ref

    class YFirst:
        def __init__(self, index, source, cols, relay):
            self.index, self.source, self.cols = index, source, cols
            self.line = Line(index, lambda oz: ry.at[index, oz], relay)
            self.along_y = {}

        def scatter(self, half):
            for oz in range(half * z_half, (half + 1) * z_half):
                self.along_y[oz] = send(
                    self.source.at[rows_of(oz, 1 - y), self.cols],
                    ry.at[self.index, oz],
                    sem_ys.at[self.index, oz],
                    sem_yr.at[self.index, oz],
                    to_y,
                )

        def start_z(self):
            for oz in range(z_count):
                self.along_y[oz].wait_recv()
                add_to(ry.at[self.index, oz], self.source.at[rows_of(oz, y), self.cols])
            self.line.start()

        def middle(self):
            self.line.middle()

        def total(self):
            return self.line.total()

    class ZFirst:
        def __init__(self, index, source, cols):
            self.index = index
            self.lines = [
                Line(index + k, lambda oz, oy=oy: source.at[rows_of(oz, oy), cols], True)
                for k, oy in enumerate((1 - y, y))
            ]

        def start_z(self):
            for line in self.lines:
                line.start()

        def middle(self):
            for line in self.lines:
                line.middle()

        def start_y(self):
            self.copy = send(
                self.lines[0].total(),
                ry.at[self.index, 0],
                sem_ys.at[self.index, 0],
                sem_yr.at[self.index, 0],
                to_y,
            )

        def total(self):
            ref = self.lines[1].total()
            self.copy.wait_recv()
            add_to(ref, ry.at[self.index, 0])
            return ref

    left_cols, right_cols = pl.ds(0, half_width), pl.ds(half_width, half_width)
    sum_near = YFirst(0, ga.at[near], my_cols, True)
    sum_key = YFirst(1, ga.at[1], my_cols, True)
    sum_proj = YFirst(2, ga.at[3], my_cols, True)
    sum_fc1 = [YFirst(3, gf.at[0], left_cols, True), YFirst(4, gf.at[0], right_cols, True)]
    sum_fc2 = [YFirst(5, gf.at[1], left_cols, True), ZFirst(6, gf.at[1], right_cols)]

    def all_rows(ring):
        return ring[...].reshape(GROUP * padded, width)

    def fc1_grad(tile, carry):
        cols = pl.ds(pl.multiple_of(tile * TILE, TILE), TILE)
        gf[0, cols, :] = dot_tn(dp_s[:, cols], all_rows(hg)).astype(BF)
        return carry

    def fc2_grad(tile, carry):
        cols = pl.ds(pl.multiple_of(tile * TILE, TILE), TILE)
        gf[1, cols, :] = dot_tn(ac[:, cols], all_rows(gg)).astype(BF)
        return carry

    lax.fori_loop(0, tiles_half, fc2_grad, 0)
    sum_fc2[0].scatter(0)
    lax.fori_loop(tiles_half, tiles, fc2_grad, 0)
    sum_fc2[1].start_z()
    sum_fc2[0].scatter(1)
    lax.fori_loop(0, tiles_half, fc1_grad, 0)
    for part in sum_fc1:
        part.scatter(0)
    lax.fori_loop(tiles_half, tiles, fc1_grad, 0)
    for part in sum_fc1:
        part.scatter(1)
    sg[pl.ds(8 + mine, 1), :] = jnp.sum(dp_s[...].astype(F32), axis=0, keepdims=True)

    ph_c1.wait_recv()
    ph_x.wait_recv()
    dh2 = ph[mine].astype(F32) + rc_h[1].astype(F32) + rx_h[...].astype(F32)
    sg[3:4, :] = jnp.sum(dh2 * normed_two, axis=0, keepdims=True)
    sg[4:5, :] = jnp.sum(dh2, axis=0, keepdims=True)
    dx1 = gs[...] + norm_back(dh2 * flat_row(n2g_ref), normed_two, scale_two)
    gs[...] = dx1
    gab = dx1 * row_live
    sg[2:3, :] = jnp.sum(gab, axis=0, keepdims=True)
    gab = gab.astype(BF)
    gabp[...] = dot_nn(spread, gab).astype(BF)
    for tile in range(tiles):
        ga[3, TILE * tile : TILE * (tile + 1), :] = dot_tn(
            attn[:, TILE * tile : TILE * (tile + 1)], gab
        ).astype(BF)

    core_copies, x_copies = [], []

    def to_core_sum(source, landing, k):
        core_copies.append(send(source, landing, sem_as.at[k, 0], sem_ar.at[k, 0], to_core))

    to_core_sum(ga.at[3, :, her_cols], rca.at[3], 2)
    sum_fc2[1].middle()

    dbias[...] = jnp.zeros_like(dbias)
    dh1[...] = jnp.zeros_like(dh1)

    def attend_back(tile, carry):
        cols = pl.ds(pl.multiple_of(tile * TILE, TILE), TILE)
        dattn = dot_nt(gabp[...], wa[3, cols, :])
        normed = h1p[...]
        total = jnp.zeros((SLOTS, LANES), F32)
        for w in range(windows):
            part = pl.ds(SLOTS * w, SLOTS)
            d_four = four(dattn[SLOTS * w : SLOTS * (w + 1)])
            q_four = four(qs[tile, part, :].astype(F32))
            probs = pt[tile * windows + w]
            dprob = dot_nt(vs[tile, part, :], d_four)
            weighed = probs * dprob
            ds = weighed - probs * jnp.sum(weighed, axis=0, keepdims=True)
            total = total + ds
            dsb = ds.astype(BF)
            dvs[tile, part, :] = dot_nn(probs.astype(BF), d_four).astype(BF)
            dks[tile, part, :] = dot_nn(dsb, q_four).astype(BF)
            dqs[tile, part, :] = (
                fold(dot_tn(dsb, ks[tile, part, :])) * HEAD ** (-0.5)
            ).astype(BF)
        dbias[tile] = total
        for s, grads in enumerate((dqs, dks, dvs)):
            ga[s, cols, :] = dot_tn(grads[tile], normed).astype(BF)
            dh1[...] += dot_nn(grads[tile], wa[s, cols, :])
        sg[6:7, cols] = jnp.sum(dqs[tile].astype(F32), axis=0, keepdims=True)
        sg[7:8, cols] = jnp.sum(dvs[tile].astype(F32), axis=0, keepdims=True)
        return carry

    half_rows = width // 2
    halves = [pl.ds(0, half_rows), pl.ds(half_rows, half_rows)]

    def add_core(slot, part):
        add_to(ga.at[slot, part, my_cols], rca.at[slot, part, :])

    def reduce_core(half):
        part = halves[half]
        to_core_sum(ga.at[pl.ds(0, 3), part, her_cols], rca.at[pl.ds(0, 3), part, :], half)

    def reduce_x(half):
        part = halves[half]
        core_copies[1 + half].wait_recv()
        add_core(far, part)
        x_copies.append(
            send(
                ga.at[far, part, my_cols],
                rxa.at[part],
                sem_as.at[half, 1],
                sem_ar.at[half, 1],
                to_x,
            )
        )
        add_core(1, part)
        sum_key.scatter(half)
        add_core(near, part)

    lax.fori_loop(0, tiles_half, attend_back, 0)
    reduce_core(0)
    core_copies[0].wait_recv()
    add_core(3, slice(None))
    sum_proj.scatter(0)
    sum_proj.scatter(1)
    reduce_x(0)
    sum_fc2[0].start_z()
    lax.fori_loop(tiles_half, tiles, attend_back, 0)
    reduce_core(1)

    def mlp_out(slot):
        ph[slot] = dot_nn(ac[slot_rows(slot), :], wf[1]).astype(BF)

    def near_y(half):
        x_copies[half].wait_recv()
        add_to(ga.at[near, halves[half], my_cols], rxa.at[halves[half]])
        sum_near.scatter(half)

    out_copies = []
    sent(ph_c0)
    sent(ph_c1)
    mlp_out(xc_dl)
    out_copies.append(send(ph.at[xc_dl], rc_o.at[0], sem_hs.at[1, 0], sem_hr.at[1, 0], to_core))
    reduce_x(1)
    mlp_out(core_dl)
    out_copies.append(send(ph.at[core_dl], rc_o.at[1], sem_hs.at[1, 1], sem_hr.at[1, 1], to_core))
    mlp_out(x_dl)
    near_y(0)
    sum_fc2[0].middle()
    sum_fc2[1].start_y()

    dh1c = dot_nn(gather, dh1[...].astype(BF))
    n1 = n1s[...]
    sg[0:1, :] = jnp.sum(dh1c * n1, axis=0, keepdims=True)
    sg[1:2, :] = jnp.sum(dh1c, axis=0, keepdims=True)
    dn = norm_back(dh1c * flat_row(n1g_ref), n1, stats[:, 0:1])
    tgrad_ref[...] = (gs[...] + dn).astype(BF)[0:rows]

    back = one_hot(
        iota((LANES, PACK * TILE), 1)
        == TILE * (iota((LANES, 1), 0) >> 6)
        + (TILE - 1 - table_place(iota((LANES, 1), 0) & 63, False)),
        BF,
    )
    for tile in range(tiles):
        high, low = split_two(dbias[tile])
        wide = dot_nn(high, back) + dot_nn(low, back)
        for k in range(PACK):
            head = tile * PACK + k
            line = jnp.zeros((8, LANES), F32)
            for r in range(8):
                piece = wide[8 * r : 8 * (r + 1), TILE * k : TILE * (k + 1)]
                piece = jnp.concatenate([piece, jnp.zeros_like(piece)], axis=1)
                shift = LANES - 1 - CENTRE - (TILE - 1) + SPAN * r
                line = line + shear(piece, shift)
            row, spot = 12 + head // heads_here, LANES * (head % heads_here)
            sg[row : row + 1, spot : spot + LANES] = jnp.sum(line, axis=0, keepdims=True)

    last_small = 1 + z_count + groups

    def small_start(stage, ref, devices):
        cols = slice(None) if ref is sg else my_cols
        return ref, [sg_in.at[stage + k, :, cols] for k in range(len(devices))], [
            send(
                ref,
                sg_in.at[stage + k, :, cols],
                sem_ss.at[stage + k],
                sem_sr.at[stage + k],
                device,
            )
            for k, device in enumerate(devices)
        ]

    def small_end(started):
        ref, landings, copies = started
        for copy in copies:
            copy.wait_recv()
            sent(copy)
        total = ref[...]
        for landing in landings:
            total = total + landing[...]
        ref[...] = total

    def swap(ref, dst, index, device):
        return send(ref, dst, sem_fs.at[index], sem_fr.at[index], device)

    def over_groups(ref, landing, index):
        for step in range(1, groups):
            k = index * (groups - 1) + step - 1
            copy = send(ref, landing.at[step - 1], sem_gs.at[k], sem_gr.at[k], to_group(step))
            copy.wait_recv()
            sent(copy)
        if groups > 1:
            add_to(ref, *[landing.at[step - 1] for step in range(1, groups)])

    final = {}

    def finish(which, parts):
        for part, cols in zip(parts, (left_cols, right_cols), strict=True):
            fin[which, mine, :, cols] = part.total()[...]
        slot = fin.at[which, mine]
        over_groups(slot, group_m.at[which], which)
        final[which, 0] = swap(slot, slot, 3 * which, to_x)
        final[which, 1] = swap(slot, slot, 3 * which + 1, to_core)

    def finish_core(which):
        final[which, 0].wait_recv()
        slot = fin.at[which, x_dl]
        final[which, 2] = swap(slot, slot, 3 * which + 2, to_core)

    def finish_out(which):
        final[which, 1].wait_recv()
        final[which, 2].wait_recv()
        fin_ref[1 + which] = fin[which]

    def share_x(k, slot, part):
        fin_a[slot, :, my_cols] = part.total()[...]
        final[2, k] = swap(fin_a.at[slot, :, my_cols], fin_x.at[k], 6 + k, to_x)

    def shared_x(k, slot):
        final[2, k].wait_recv()
        sent(final[2, k])
        ref = fin_a.at[slot, :, my_cols]
        add_to(ref, fin_x.at[k])
        over_groups(ref, group_a.at[k], 2 + k)

    smalls = small_start(0, sg, [to_core])
    for part in sum_fc1:
        part.start_z()
    near_y(1)
    small_end(smalls)
    smalls = small_start(1, sg, [to_x])
    out_copies[0].wait_recv()
    ph2[1] = (ph[x_dl].astype(F32) + rc_o[0].astype(F32)).astype(BF)
    out_copies.append(send(ph2.at[1], rx_o, sem_hs.at[1, 2], sem_hr.at[1, 2], to_x))
    mlp_out(mine)
    small_end(smalls)
    sg_half = sg.at[:, my_cols]
    smalls = small_start(2, sg_half, [to_y])
    sum_proj.start_z()
    for part in sum_fc1:
        part.middle()
    finish(1, sum_fc2)
    small_end(smalls)
    smalls = small_start(3, sg_half, [to_z(step) for step in range(1, z_count)])
    sum_key.start_z()
    sum_proj.middle()
    finish(0, sum_fc1)
    finish_core(1)

    out_copies[1].wait_recv()
    out_copies[2].wait_recv()
    branch = ph[mine].astype(F32) + rc_o[1].astype(F32) + rx_o[...].astype(F32)
    out_ref[...] = (x1s[...] + (branch + flat_row(f2b_ref)) * row_live).astype(BF)[0:rows]

    sum_key.middle()
    small_end(smalls)
    if groups > 1:
        small_end(
            small_start(
                2 + z_count, sg_half, [to_group(step) for step in range(1, groups)]
            )
        )
    small_last = send(
        sg_half,
        sg_in.at[last_small, :, my_cols],
        sem_ss.at[last_small],
        sem_sr.at[last_small],
        to_core,
    )
    sum_near.start_z()
    share_x(0, 3, sum_proj)
    finish_core(0)
    sum_near.middle()
    share_x(1, 1, sum_key)
    small_last.wait_recv()
    sg[:, her_cols] = sg_in[last_small, :, her_cols]
    finish_out(1)
    shared_x(0, 3)

    vec_ref[...] = sg[0:8, :]
    pick = one_hot(iota((width, block), 0) == block * mp + iota((width, block), 1), F32)
    small_ref[0:8, 0:block] = dot_nn(sg[0:8, :], pick, HIGHEST)
    wide_lane = iota((width, hidden), 1)
    pick = one_hot(
        iota((width, hidden), 0)
        == block * mp + wide_lane - block * steps_of(wide_lane, block, hidden // block),
        F32,
    )
    lines = dot_nn(sg[8:16, :], pick, HIGHEST)
    keep = iota((8, hidden), 0) == steps_of(iota((8, hidden), 1), block, hidden // block)
    small_ref[8:9, :] = jnp.sum(jnp.where(keep, lines, 0.0), axis=0, keepdims=True)
    table = sg[pl.ds(12 + mp, 1), :]
    table = jnp.concatenate(
        [table[:, LANES * k : LANES * (k + 1)] for k in range(heads_here)]
        + [jnp.zeros((8 - heads_here, LANES), F32)],
        axis=0,
    )
    turn = one_hot(iota((LANES, LANES), 0) + iota((LANES, LANES), 1) == LANES - 1, F32)
    small_ref[16:24, 0:LANES] = dot_nn(table, turn, HIGHEST)

    finish_out(0)
    shared_x(1, 1)
    fin_a[near, :, my_cols] = sum_near.total()[...]
    slot = fin_a.at[near, :, my_cols]
    over_groups(slot, group_a.at[2], 4)
    near_x = swap(slot, slot, 8, to_x)
    near_x.wait_recv()
    slots = fin_a.at[:, :, my_cols]
    swap(slots, slots, 9, to_core).wait_recv()
    fin_ref[0] = fin_a[...]

    for copy, when in pending:
        if when is None:
            copy.wait_send()
        else:
            pl.when(when)(copy.wait_send)


def unpack(
    out_in,
    tgrad_in,
    vec_in,
    small_in,
    fin_in,
    out_ref,
    tgrad_ref,
    n1g_ref,
    n1b_ref,
    qkvg_ref,
    qvg_ref,
    relg_ref,
    projg_ref,
    pbg_ref,
    n2g_ref,
    n2b_ref,
    f1g_ref,
    f1bg_ref,
    f2g_ref,
    f2bg_ref,
):
    hidden, width = f2g_ref.shape
    out_ref[...] = out_in[...]
    tgrad_ref[...] = tgrad_in[...]
    for k, ref in enumerate((n1g_ref, n1b_ref, pbg_ref, n2g_ref, n2b_ref, f2bg_ref)):
        ref[...] = vec_in[k : k + 1, :].reshape(width)
    for s in range(3):
        qkvg_ref[s] = fin_in[0, s].astype(F32)
    projg_ref[...] = fin_in[0, 3].astype(F32)
    f1g_ref[...] = fin_in[1].reshape(hidden, width).astype(F32).T
    f2g_ref[...] = fin_in[2].reshape(hidden, width).astype(F32)
    qvg_ref[...] = small_in[6:8, 0 : qvg_ref.shape[1]]
    f1bg_ref[...] = small_in[8:9, :].reshape(hidden)
    relg_ref[...] = small_in[16 : 16 + relg_ref.shape[0], 0:ENTRIES]


def solution(mesh):
    n_dp, n_mp = mesh.shape["dp"], mesh.shape["mp"]

    def shards(
        tokens,
        crop_kind,
        norm1_gain,
        norm1_bias,
        qkv_weight,
        qv_bias,
        rel_table,
        proj_weight,
        proj_bias,
        norm2_gain,
        norm2_bias,
        fc1_weight,
        fc1_bias,
        fc2_weight,
        fc2_bias,
        out_grad,
    ):
        rows, width = tokens.shape
        windows = rows // WIN
        padded = -(-rows // 16) * 16
        block = proj_weight.shape[0]
        hidden = fc2_weight.shape[0]
        heads_here = rel_table.shape[1]
        places = SLOTS * windows
        tiles = width // TILE
        z_count = n_mp // 2
        groups = n_dp // GROUP
        dims = (n_dp, n_mp, rows, windows, padded, width, block, hidden)

        def full(*shape):
            return jax.ShapeDtypeStruct(shape, F32)

        vmem = pl.BlockSpec(memory_space=pltpu.VMEM)
        dma = pltpu.SemaphoreType.DMA
        results = pl.pallas_call(
            functools.partial(body, dims),
            out_shape=[
                jax.ShapeDtypeStruct((rows, width), BF),
                jax.ShapeDtypeStruct((rows, width), BF),
                full(8, width),
                full(24, hidden),
                jax.ShapeDtypeStruct((3, GROUP, block, width), BF),
            ],
            in_specs=[pl.BlockSpec(memory_space=pltpu.SMEM)] + [vmem] * 15,
            out_specs=[vmem] * 5,
            scratch_shapes=[
                pltpu.VMEM((GROUP, width, width), BF),
                pltpu.VMEM((2, width, width), BF),
                pltpu.VMEM((hidden, width), BF),
                pltpu.VMEM((n_mp, 8, hidden), F32),
                pltpu.VMEM((8, hidden), F32),
                pltpu.VMEM((padded, width), F32),
                pltpu.VMEM((padded, width), F32),
                pltpu.VMEM((padded, width), F32),
                pltpu.VMEM((padded, width), F32),
                pltpu.VMEM((padded, TILE), F32),
                pltpu.VMEM((8, width), F32),
                pltpu.VMEM((8, width), F32),
                pltpu.VMEM((places, width), BF),
                pltpu.VMEM((tiles, places, TILE), BF),
                pltpu.VMEM((tiles, places, TILE), BF),
                pltpu.VMEM((tiles, places, TILE), BF),
                pltpu.VMEM((tiles, places, TILE), BF),
                pltpu.VMEM((tiles * windows, SLOTS, LANES), F32),
                pltpu.VMEM((tiles, SLOTS, LANES), F32),
                pltpu.VMEM((tiles, SLOTS, LANES), F32),
                pltpu.VMEM((GROUP, padded, width), BF),
                pltpu.VMEM((GROUP, padded, width), BF),
                pltpu.VMEM((GROUP * padded, width), BF),
                pltpu.VMEM((GROUP * padded, width), BF),
                pltpu.VMEM((GROUP, padded, width), BF),
                pltpu.VMEM((2, padded, width), BF),
                pltpu.VMEM((padded, width), BF),
                pltpu.VMEM((2, padded, width), BF),
                pltpu.VMEM((2, padded, width), BF),
                pltpu.VMEM((padded, width), BF),
                pltpu.VMEM((places, width), BF),
                pltpu.VMEM((tiles, places, TILE), BF),
                pltpu.VMEM((tiles, places, TILE), BF),
                pltpu.VMEM((tiles, places, TILE), BF),
                pltpu.VMEM((tiles, SLOTS, LANES), F32),
                pltpu.VMEM((places, width), F32),
                pltpu.VMEM((GROUP, width, width), BF),
                pltpu.VMEM((2, width, width), BF),
                pltpu.VMEM((GROUP, width, width // 2), BF),
                pltpu.VMEM((width, width // 2), BF),
                pltpu.VMEM((7, z_count, block, width // 2), BF),
                pltpu.VMEM((8, z_count - 1, block, width // 2), BF),
                pltpu.VMEM((8, block, width // 2), BF),
                pltpu.VMEM((2, GROUP, block, width), BF),
                pltpu.VMEM((GROUP, block, width), BF),
                pltpu.VMEM((2, block, width // 2), BF),
                pltpu.VMEM((2, max(groups - 1, 1), block, width), BF),
                pltpu.VMEM((3, max(groups - 1, 1), block, width // 2), BF),
                pltpu.VMEM((24, width), F32),
                pltpu.VMEM((2 + z_count + groups, 24, width), F32),
                dma((7, 2 * z_count + 1)),
                dma((7, 2 * z_count + 1)),
                dma((2 * n_mp + 4,)),
                dma((2 * n_mp + 4,)),
                dma((2, 3)),
                dma((2, 3)),
                dma((2, 3)),
                dma((2, 3)),
                dma((3, 2)),
                dma((3, 2)),
                dma((7, z_count)),
                dma((7, z_count)),
                dma((8, 4)),
                dma((8, 4)),
                dma((10,)),
                dma((10,)),
                dma((2 + z_count + groups,)),
                dma((2 + z_count + groups,)),
                dma((5 * max(groups - 1, 1),)),
                dma((5 * max(groups - 1, 1),)),
            ],
            compiler_params=pltpu.CompilerParams(
                collective_id=0, has_side_effects=True, vmem_limit_bytes=63 * 2**20
            ),
        )(
            crop_kind,
            tokens,
            out_grad,
            norm1_gain,
            norm1_bias,
            jnp.swapaxes(qkv_weight, 1, 2),
            qv_bias,
            rel_table.T,
            proj_weight,
            proj_bias,
            norm2_gain,
            norm2_bias,
            fc1_weight,
            fc1_bias,
            fc2_weight,
            fc2_bias,
        )
        results = pl.pallas_call(
            unpack,
            out_shape=[
                jax.ShapeDtypeStruct((rows, width), BF),
                jax.ShapeDtypeStruct((rows, width), BF),
                full(width),
                full(width),
                full(3, block, width),
                full(2, block),
                full(heads_here, ENTRIES),
                full(block, width),
                full(width),
                full(width),
                full(width),
                full(width, hidden),
                full(hidden),
                full(hidden, width),
                full(width),
            ],
            in_specs=[vmem] * 5,
            out_specs=[vmem] * 15,
        )(*results)
        results = list(results)
        results[4] = jnp.swapaxes(results[4], 1, 2)
        results[6] = results[6].T
        return tuple(results)

    in_specs = (
        P(("dp", "mp"), None),
        P("dp"),
        P(),
        P(),
        P(None, None, "mp"),
        P(None, "mp"),
        P(None, "mp"),
        P("mp", None),
        P(),
        P(),
        P(),
        P(None, "mp"),
        P("mp"),
        P("mp", None),
        P(),
        P(("dp", "mp"), None),
    )
    out_specs = (
        P(("dp", "mp"), None),
        P(("dp", "mp"), None),
        P(),
        P(),
        P(None, None, "mp"),
        P(None, "mp"),
        P(None, "mp"),
        P("mp", None),
        P(),
        P(),
        P(),
        P(None, "mp"),
        P("mp"),
        P("mp", None),
        P(),
    )
    return jax.shard_map(shards, mesh=mesh, in_specs=in_specs, out_specs=out_specs, check_vma=False)
```
